32 devices in a mesh: ia: 4 (over y, x), ja: 4 (over z), ka: 2 (over core).
Axes of the slice: x: 2, y: 2, z: 4, core: 2. Of those that a mesh axis runs over, the one named last changes fastest.
Arguments:
- state: float32 [8, 7, 64, 2048], P('ia', None, 'ja', 'ka'), may hold values from -6 to 6
- inverse: bfloat16 [8, 7, 7, 64, 2048], P('ia', None, None, 'ja', 'ka'), may hold values from -1 to 1
- coupling: float32 [8, 2, 64, 2048], P('ia', None, 'ja', 'ka'), may hold values from 0.49 to 1
- wall: int32 [8, 64, 2048], P('ia', 'ja', 'ka'), may hold values 0 or 1
Outputs:
- correction: float32 [8, 7, 64, 2048], P('ia', None, 'ja', 'ka')
The draws below stay inside these ranges and needn't reach their ends.
All inputs are finite; a program needn't handle non-finite values. No bound on the sum of `wall` on one device may be relied on, other than what follows from the above.
Results may differ from the reference program's by a relative error of at most 0.0003.
Values may be sent and summed in bfloat16 or wider, within the bound.
No kernel may reach another device: no remote copies, remote signals or barrier semaphores. Data moves between devices by JAX's collectives and lax.ppermute only.
A program may use at most 128 MiB of HBM per device.

```python
import math
import jax
import jax.numpy as jnp
from jax import lax

NV = 7
NI = 8
NJ = 64
NK = 2048


def draw_inverse(key, part):
    key = jax.random.fold_in(key, 11)
    subkeys = jax.random.split(key, 7)
    group_order = jax.random.permutation(subkeys[0], 4)
    slow_groups = group_order < 2
    plane_scale = jnp.exp(jax.random.uniform(subkeys[1], (NI,), jnp.float32, math.log(0.5), math.log(2.0)))
    slow_rate = jnp.exp(jax.random.uniform(subkeys[2], (NI, 4, NJ, NK), jnp.float32, math.log(0.004), math.log(0.016)))
    slow_rate = slow_rate * plane_scale[:, None, None, None]
    fast_rate = jax.random.uniform(subkeys[3], (NI, 4, NJ, NK), jnp.float32, 0.04, 0.09)
    decay_rate = 1.0 - jnp.where(slow_groups[None, :, None, None], slow_rate, fast_rate)
    angles = jax.random.uniform(subkeys[4], (NI, 3, NJ, NK), jnp.float32, 0.25, 0.6)
    flips = jnp.where(jax.random.bernoulli(subkeys[5], 0.5, (NI, 3, NJ, NK)), 1.0, -1.0)
    cosine = jnp.cos(angles)
    sine_part = jnp.sin(angles) * flips
    matrix = jax.random.uniform(subkeys[6], (NI, 7, 7, NJ, NK), jnp.float32, -0.02, 0.02)
    for pair_index in range(3):
        scale_pair = decay_rate[:, pair_index]
        row_low = 2 * pair_index
        row_high = row_low + 1
        matrix = matrix.at[:, row_low, row_low].add(scale_pair * cosine[:, pair_index])
        matrix = matrix.at[:, row_low, row_high].add(-scale_pair * sine_part[:, pair_index])
        matrix = matrix.at[:, row_high, row_low].add(scale_pair * sine_part[:, pair_index])
        matrix = matrix.at[:, row_high, row_high].add(scale_pair * cosine[:, pair_index])
    matrix = matrix.at[:, 6, 6].add(decay_rate[:, 3])
    matrix = jnp.clip(matrix, -1.0, 1.0)
    return matrix.astype(jnp.bfloat16)


def draw_coupling(key, part):
    key = jax.random.fold_in(key, 23)
    subkeys = jax.random.split(key, 4)
    base_value = jax.random.uniform(subkeys[0], (NI, 2, NJ, NK), jnp.float32, 0.985, 1.0)
    ordering_lower = jax.random.permutation(subkeys[1], NI)
    ordering_upper = jax.random.permutation(subkeys[2], NI)
    sweep_group_planes = jnp.stack([ordering_lower[:2], ordering_upper[:2]], axis=1)
    secondary_depth = jax.random.uniform(subkeys[3], (2,), jnp.float32, 0.5, 0.8)
    sweep_group_depth = jnp.stack([jnp.full((2,), 0.5, jnp.float32), secondary_depth], axis=0)
    current_plane_index = jnp.arange(NI)
    relaxation_factor = jnp.ones((NI, 2), jnp.float32)
    for sweep_group_index in range(2):
        relaxation_factor = relaxation_factor * jnp.where(current_plane_index[:, None] == sweep_group_planes[sweep_group_index][None, :], sweep_group_depth[sweep_group_index][None, :], 1.0)
    return base_value * relaxation_factor[:, :, None, None]


def place_ends(drawn, own_key, smallest, largest):
    dims = drawn.shape
    index_at = [jax.random.randint(jax.random.fold_in(own_key, axis), (), 0, dims[axis]) for axis in range(len(dims))]
    drawn = drawn.at[tuple(index_at)].set(smallest)
    longest = dims.index(max(dims))
    index_at[longest] = (index_at[longest] + 1) % dims[longest]
    return drawn.at[tuple(index_at)].set(largest)


def steps_of(key, shape, pieces, low, top_value):
    def one(dim, blocks):
        draws = jax.random.uniform(jax.random.fold_in(jax.random.fold_in(key, 6), dim), (blocks,), jnp.float32, low / len(pieces), top_value / len(pieces))
        return jnp.repeat(jnp.exp(draws), shape[dim] // blocks).reshape((-1,) + (1,) * (len(shape) - dim - 1))

    factor_of = one(*pieces[0])
    for cut in pieces[1:]:
        factor_of = factor_of * one(*cut)
    return factor_of


def gaussian(own_key, dims, deviation, most, pieces=(), dtype=jnp.bfloat16):
    level = steps_of(own_key, dims, pieces, -0.22, 0.18) if pieces else 1.0
    entries = jax.random.normal(own_key, dims, jnp.float32) * deviation * level
    return jnp.minimum(jnp.maximum(entries, -most), most).astype(dtype)


def setup_inputs(seed: int = 0) -> dict:
    key_of = jax.random.split(jax.random.key(seed), 5)
    return {
        "state": gaussian(key_of[0], (NI, NV, NJ, NK), 1.0, 6.0, ((0, 4), (2, 4), (3, 2)), jnp.float32),
        "inverse": draw_inverse(jax.random.fold_in(key_of[4], 71), 0),
        "coupling": draw_coupling(jax.random.fold_in(key_of[4], 71), 0),
        "wall": place_ends((jax.random.randint(key_of[3], (NI, NJ, NK), 0, 8) < 1).astype(jnp.int32), jax.random.fold_in(key_of[3], 1), 0, 1),
    }


advection = 0.012
viscosity = 0.006
damping = 0.003


def sliced(padded, shift_i, shift_j, shift_k):
    rows_i = padded.shape[0] - 4
    rows_j = padded.shape[2] - 4
    rows_k = padded.shape[3] - 4
    return padded[2 + shift_i:2 + shift_i + rows_i, :, 2 + shift_j:2 + shift_j + rows_j, 2 + shift_k:2 + shift_k + rows_k]


def fourth_along(padded, centre, shift_i, shift_j, shift_k):
    return (sliced(padded, 2 * shift_i, 2 * shift_j, 2 * shift_k) - 4.0 * sliced(padded, shift_i, shift_j, shift_k) + 6.0 * centre
            - 4.0 * sliced(padded, -shift_i, -shift_j, -shift_k) + sliced(padded, -2 * shift_i, -2 * shift_j, -2 * shift_k))


def stencil(padded, wall):
    centre = sliced(padded, 0, 0, 0)
    convect = -advection * 0.5 * (3.0 * centre - 4.0 * sliced(padded, -1, 0, 0) + sliced(padded, -2, 0, 0))
    laplace = (sliced(padded, 1, 0, 0) + sliced(padded, -1, 0, 0) + sliced(padded, 0, 1, 0) + sliced(padded, 0, -1, 0)
               + sliced(padded, 0, 0, 1) + sliced(padded, 0, 0, -1) - 6.0 * centre)
    fourth = fourth_along(padded, centre, 1, 0, 0) + fourth_along(padded, centre, 0, 1, 0) + fourth_along(padded, centre, 0, 0, 1)
    open_cells = (1 - wall).astype(jnp.float32)[:, None]
    return open_cells * (convect + viscosity * laplace - damping * fourth)


def apply_inverse(inverse_plane, vector):
    return jnp.sum(inverse_plane.astype(jnp.float32) * vector[None], axis=1)


def forward_local(inverse, residual, factors, entry_face):
    def advance(running, inputs):
        inverse_plane, residual_plane, relaxation_factor = inputs
        result = apply_inverse(inverse_plane, residual_plane + relaxation_factor[None] * running)
        return result, result
    last_plane, planes = lax.scan(advance, entry_face, (inverse, residual, factors))
    return planes, last_plane


def backward_local(inverse, base_planes, factors, entry_face):
    def advance(running, inputs):
        inverse_plane, base_plane, relaxation_factor = inputs
        result = base_plane + apply_inverse(inverse_plane, relaxation_factor[None] * running)
        return result, result
    first_plane, planes = lax.scan(advance, entry_face, (inverse, base_planes, factors), reverse=True)
    return planes, first_plane


def reference(state, inverse, coupling, wall):
    padded = jnp.pad(state, ((2, 2), (0, 0), (2, 2), (2, 2)))
    residual = stencil(padded, wall)
    zero_face = jnp.zeros((state.shape[1], state.shape[2], state.shape[3]), jnp.float32)
    planes, last_plane = forward_local(inverse, residual, coupling[:, 0], zero_face)
    correction, first_plane = backward_local(inverse, planes, coupling[:, 1], zero_face)
    return correction
```

```python
import functools

import jax
import jax.numpy as jnp
from jax import lax
from jax.experimental import pallas as pl
from jax.experimental.pallas import tpu as pltpu
from jax.sharding import PartitionSpec as P

advection = 0.012
viscosity = 0.006
damping = 0.003

CENTRE = -1.5 * advection - 6.0 * viscosity - 18.0 * damping
BEHIND_1 = 2.0 * advection + viscosity + 4.0 * damping
BEHIND_2 = -0.5 * advection - damping
NEAR = viscosity + 4.0 * damping
FAR = -damping

LANES = 128
TOP = 32767.0
VMEM = pltpu.VMEM
CHUNKS = 2


def scale_of(code):
    return jnp.exp2(code.astype(jnp.float32) * (1.0 / 256.0))


def put_coded(blocks, most, out_ref, rows):
    code = jnp.ceil(256.0 * jnp.log2(jnp.maximum(most, 1e-30))).astype(jnp.int32)
    factor = TOP / scale_of(code)
    for index, block in enumerate(blocks):
        coded = jnp.floor(block() * factor + 0.5)
        coded = jnp.minimum(jnp.maximum(coded, -TOP), TOP).astype(jnp.int32)
        out_ref[index * rows : (index + 1) * rows, :] = coded.astype(jnp.int16)
    count = len(blocks)
    out_ref[count * rows : (count + 1) * rows, :] = code.astype(jnp.int16)


def get_scale(coded_ref, count, rows):
    code = coded_ref[count * rows : (count + 1) * rows, :].astype(jnp.int32)
    return scale_of(code) * (1.0 / TOP)


def get_coded(coded_ref, index, rows, scale):
    return coded_ref[index * rows : (index + 1) * rows, :].astype(jnp.int32).astype(jnp.float32) * scale


def encode_kernel(state_ref, *out_refs):
    planes, nv, rows, columns = state_ref.shape
    width = columns // len(out_refs)
    for chunk, out_ref in enumerate(out_refs):
        places = [
            (p, v, chunk * width + b * LANES)
            for p in range(planes)
            for v in range(nv)
            for b in range(width // LANES)
        ]
        most = None
        for p, v, at in places:
            size = jnp.abs(state_ref[p, v, :, at : at + LANES])
            most = size if most is None else jnp.maximum(most, size)
        blocks = [
            (lambda p=p, v=v, at=at: state_ref[p, v, :, at : at + LANES]) for p, v, at in places
        ]
        put_coded(blocks, most, out_ref, rows)


def residual_kernel(
    chunk, chunks, count_k, state_ref, low_j, high_j, low_k, high_k, ahead, wall_ref, x_out, rows_pad
):
    planes, nv, rows, columns = state_ref.shape
    width = columns // chunks
    start = chunk * width
    stop = start + width
    per = width // LANES
    scale = get_scale(ahead, planes * nv * per, rows)
    place_k = lax.axis_index("ka")
    open_cells = [1.0 - wall_ref[p, :, start:stop].astype(jnp.float32) for p in range(planes)]

    def next_plane(p, v):
        parts = [get_coded(ahead, (p * nv + v) * per + b, rows, scale) for b in range(per)]
        return jnp.concatenate(parts, axis=1)

    for v in range(nv):
        here = [state_ref[p, v, :, start:stop] for p in range(planes)]
        after = [next_plane(p, v) for p in range(planes)]
        for p in range(planes):
            line = here + after
            total = CENTRE * here[p] + NEAR * line[p + 1] + FAR * line[p + 2]
            if p >= 1:
                total += BEHIND_1 * here[p - 1]
            if p >= 2:
                total += BEHIND_2 * here[p - 2]
            rows_pad[6:8, :] = low_j[p, v, :, start:stop]
            rows_pad[8 : 8 + rows, :] = here[p]
            rows_pad[8 + rows : 10 + rows, :] = high_j[p, v, :, start:stop]
            total += NEAR * (rows_pad[7 : 7 + rows, :] + rows_pad[9 : 9 + rows, :])
            total += FAR * (rows_pad[6 : 6 + rows, :] + rows_pad[10 : 10 + rows, :])
            if start == 0:
                left = jnp.where(place_k > 0, low_k[p, v], 0.0)
            else:
                left = state_ref[p, v, :, start - LANES : start]
            if stop == columns:
                right = jnp.where(place_k < count_k - 1, high_k[p, v], 0.0)
            else:
                right = state_ref[p, v, :, stop : stop + LANES]
            wide = jnp.concatenate([left, here[p], right], axis=1)
            span = wide.shape[1]
            one = pltpu.roll(wide, 1, 1) + pltpu.roll(wide, span - 1, 1)
            two = pltpu.roll(wide, 2, 1) + pltpu.roll(wide, span - 2, 1)
            total += (NEAR * one + FAR * two)[:, LANES : LANES + width]
            x_out[p, v] = open_cells[p] * total


def apply_block(inverse_ref, p, at, vector):
    result = []
    for a in range(len(vector)):
        total = None
        for b in range(len(vector)):
            term = inverse_ref[p, a, b, :, at : at + LANES].astype(jnp.float32) * vector[b]
            total = term if total is None else total + term
        result.append(total)
    return result


def forward_part(chunk, first, inverse_ref, coupling_ref, wall_ref, behind, face, x_in, x_out, send):
    planes, nv, rows, width = x_out.shape
    per = width // LANES
    if not first:
        face_scale = get_scale(face, nv * per, rows)
        behind_scale = get_scale(behind, planes * nv * per, rows)
    most = None
    for block in range(per):
        own = slice(block * LANES, (block + 1) * LANES)
        at = chunk * width + block * LANES
        running = None
        if not first:
            running = [get_coded(face, v * per + block, rows, face_scale) for v in range(nv)]

            def old(p, v):
                return get_coded(behind, (p * nv + v) * per + block, rows, behind_scale)

        for p in range(planes):
            factor = coupling_ref[p, 0, :, at : at + LANES]
            if not first and p < 2:
                open_cells = 1.0 - wall_ref[p, :, at : at + LANES].astype(jnp.float32)
            right = []
            for v in range(nv):
                entry = x_in[p, v, :, own]
                if running is not None:
                    entry = entry + factor * running[v]
                if not first and p == 0:
                    entry += open_cells * (BEHIND_1 * old(planes - 1, v) + BEHIND_2 * old(planes - 2, v))
                if not first and p == 1:
                    entry += open_cells * (BEHIND_2 * old(planes - 1, v))
                right.append(entry)
            running = apply_block(inverse_ref, p, at, right)
            for v in range(nv):
                x_out[p, v, :, own] = running[v]
        for v in range(nv):
            size = jnp.abs(running[v])
            most = size if most is None else jnp.maximum(most, size)
    if send is not None:
        put_face(planes - 1, most, x_out, send)


def put_face(plane, most, x_out, send):
    nv, rows, width = x_out.shape[1:]
    blocks = [
        (lambda v=v, at=b * LANES: x_out[plane, v, :, at : at + LANES])
        for v in range(nv)
        for b in range(width // LANES)
    ]
    put_coded(blocks, most, send, rows)


def backward_part(chunk, last, inverse_ref, coupling_ref, face, x_in, x_out, send):
    planes, nv, rows, width = x_out.shape
    per = width // LANES
    if not last:
        scale = get_scale(face, nv * per, rows)
    most = None
    for block in range(per):
        own = slice(block * LANES, (block + 1) * LANES)
        at = chunk * width + block * LANES
        running = None
        if not last:
            running = [get_coded(face, v * per + block, rows, scale) for v in range(nv)]
        for p in reversed(range(planes)):
            base = [x_in[p, v, :, own] for v in range(nv)]
            if running is None:
                running = base
            else:
                factor = coupling_ref[p, 1, :, at : at + LANES]
                change = apply_block(inverse_ref, p, at, [factor * running[v] for v in range(nv)])
                running = [base[v] + change[v] for v in range(nv)]
            for v in range(nv):
                x_out[p, v, :, own] = running[v]
        for v in range(nv):
            size = jnp.abs(running[v])
            most = size if most is None else jnp.maximum(most, size)
    if send is not None:
        put_face(0, most, x_out, send)


def forward_kernel(chunk, hop, count, inverse_ref, coupling_ref, wall_ref, behind, face, x_in, x_out, send):
    active = lax.axis_index("ia") == hop
    last = hop == count - 1

    @pl.when(active)
    def _():
        forward_part(
            chunk, hop == 0, inverse_ref, coupling_ref, wall_ref, behind, face, x_in, x_out,
            None if last else send,
        )
        if last:
            backward_part(chunk, True, inverse_ref, coupling_ref, None, x_out, x_out, send)

    @pl.when(jnp.logical_not(active))
    def _():
        x_out[...] = x_in[...]


def backward_kernel(chunk, hop, inverse_ref, coupling_ref, face, x_in, x_out, send):
    active = lax.axis_index("ia") == hop

    @pl.when(active)
    def _():
        backward_part(chunk, False, inverse_ref, coupling_ref, face, x_in, x_out, send)

    @pl.when(jnp.logical_not(active))
    def _():
        x_out[...] = x_in[...]


def final_kernel(chunk, inverse_ref, coupling_ref, face, *refs):
    parts, out = refs[:-1], refs[-1]
    width = parts[0].shape[3]
    mine = out.at[:, :, :, chunk * width : (chunk + 1) * width]
    active = lax.axis_index("ia") == 0

    @pl.when(active)
    def _():
        backward_part(chunk, False, inverse_ref, coupling_ref, face, parts[chunk], mine, None)

    @pl.when(jnp.logical_not(active))
    def _():
        mine[...] = parts[chunk][...]

    for other, part in enumerate(parts):
        if other != chunk:
            out[:, :, :, other * width : (other + 1) * width] = part[...]


def whole():
    return pl.BlockSpec(memory_space=VMEM)


def call(kernel, operands, outs, name, alias=None, scratch=()):
    return pl.pallas_call(
        kernel,
        in_specs=[whole()] * len(operands),
        out_specs=[whole()] * len(outs),
        out_shape=outs,
        scratch_shapes=list(scratch),
        input_output_aliases=alias or {},
        compiler_params=pltpu.CompilerParams(vmem_limit_bytes=24 * 2**20),
        name=name,
    )(*operands)


def shards(state, inverse, coupling, wall):
    planes, nv, rows, columns = state.shape
    chunks = CHUNKS
    width = columns // chunks
    per = width // LANES
    count = lax.axis_size("ia")
    count_j = lax.axis_size("ja")
    count_k = lax.axis_size("ka")
    up = lambda n: [(i, i + 1) for i in range(n - 1)]
    down = lambda n: [(i + 1, i) for i in range(n - 1)]

    halo_code = jax.ShapeDtypeStruct(((planes * nv * per + 1) * rows, LANES), jnp.int16)
    face_code = jax.ShapeDtypeStruct(((nv * per + 1) * rows, LANES), jnp.int16)
    full = jax.ShapeDtypeStruct(state.shape, jnp.float32)
    part = jax.ShapeDtypeStruct((planes, nv, rows, width), jnp.float32)

    coded = call(encode_kernel, [state], [halo_code] * chunks, "encode")
    ahead = [lax.ppermute(coded[c], "ia", down(count)) for c in range(chunks)]

    head_k = state[:, :, :, :LANES]
    tail_k = state[:, :, :, columns - LANES :]
    if count_k == 2:
        mine = jnp.where(lax.axis_index("ka") == 0, tail_k, head_k)
        low_k = lax.ppermute(mine, "ka", [(0, 1), (1, 0)])
        high_k = low_k
    else:
        low_k = lax.ppermute(tail_k, "ka", up(count_k))
        high_k = lax.ppermute(head_k, "ka", down(count_k))
    low_j = lax.ppermute(state[:, :, rows - 2 :, :], "ja", up(count_j))
    high_j = lax.ppermute(state[:, :, :2, :], "ja", down(count_j))
    behind = [lax.ppermute(coded[c], "ia", up(count)) for c in range(chunks)]

    x = []
    for c in range(chunks):
        kernel = functools.partial(residual_kernel, c, chunks, count_k)
        operands = [state, low_j, high_j, low_k, high_k, ahead[c], wall]
        x += call(kernel, operands, [part], "residual", None, [VMEM((rows + 16, width), jnp.float32)])

    face = [None] * chunks
    for hop in range(count):
        for c in range(chunks):
            if hop == 0:
                def kernel(inverse_ref, coupling_ref, wall_ref, *refs, c=c):
                    forward_kernel(c, 0, count, inverse_ref, coupling_ref, wall_ref, None, None, *refs)
                operands = [inverse, coupling, wall, x[c]]
            else:
                kernel = functools.partial(forward_kernel, c, hop, count)
                operands = [inverse, coupling, wall, behind[c], face[c], x[c]]
            x[c], send = call(kernel, operands, [part, face_code], "forward", {len(operands) - 1: 0})
            pair = (hop, hop + 1) if hop < count - 1 else (hop, hop - 1)
            face[c] = lax.ppermute(send, "ia", [pair])
    for hop in reversed(range(count - 1)):
        for c in range(chunks):
            if hop == 0 and c == chunks - 1:
                operands = [inverse, coupling, face[c], *x]
                return call(functools.partial(final_kernel, c), operands, [full], "last")[0]
            if hop == 0:
                def kernel(*refs, c=c):
                    backward_kernel(c, 0, *refs, None)
                (x[c],) = call(kernel, [inverse, coupling, face[c], x[c]], [part], "backward", {3: 0})
                continue
            kernel = functools.partial(backward_kernel, c, hop)
            x[c], send = call(kernel, [inverse, coupling, face[c], x[c]], [part, face_code], "backward", {3: 0})
            face[c] = lax.ppermute(send, "ia", [(hop, hop - 1)])


def solution(mesh):
    return jax.shard_map(
        shards,
        mesh=mesh,
        in_specs=(
            P("ia", None, "ja", "ka"),
            P("ia", None, None, "ja", "ka"),
            P("ia", None, "ja", "ka"),
            P("ia", "ja", "ka"),
        ),
        out_specs=P("ia", None, "ja", "ka"),
        check_vma=False,
    )
```

```python
import functools

import jax
import jax.numpy as jnp
from jax import lax
from jax.experimental import pallas as pl
from jax.experimental.pallas import tpu as pltpu
from jax.sharding import PartitionSpec as P

advection = 0.012
viscosity = 0.006
damping = 0.003

CENTRE = -1.5 * advection - 6.0 * viscosity - 18.0 * damping
BEHIND_1 = 2.0 * advection + viscosity + 4.0 * damping
BEHIND_2 = -0.5 * advection - damping
NEAR = viscosity + 4.0 * damping
FAR = -damping

LANES = 128
TOP = 32767.0
VMEM = pltpu.VMEM
CHUNKS = 2


def scale_of(code):
    return jnp.exp2(code.astype(jnp.float32) * (1.0 / 256.0))


def put_coded(blocks, most, out_ref, rows):
    code = jnp.ceil(256.0 * jnp.log2(jnp.maximum(most, 1e-30))).astype(jnp.int32)
    factor = TOP / scale_of(code)
    for index, block in enumerate(blocks):
        coded = jnp.floor(block() * factor + 0.5)
        coded = jnp.minimum(jnp.maximum(coded, -TOP), TOP).astype(jnp.int32)
        out_ref[index * rows : (index + 1) * rows, :] = coded.astype(jnp.int16)
    count = len(blocks)
    out_ref[count * rows : (count + 1) * rows, :] = code.astype(jnp.int16)


def get_scale(coded_ref, count, rows):
    code = coded_ref[count * rows : (count + 1) * rows, :].astype(jnp.int32)
    return scale_of(code) * (1.0 / TOP)


def get_coded(coded_ref, index, rows, scale):
    return coded_ref[index * rows : (index + 1) * rows, :].astype(jnp.int32).astype(jnp.float32) * scale


def encode_kernel(chunks, both_k, state_ref, wall_ref, *outs):
    planes, nv, rows, columns = state_ref.shape
    coded, (j_first, j_second), edges_k, open_ref = outs[:chunks], outs[chunks : chunks + 2], outs[chunks + 2 : -1], outs[-1]
    width = columns // chunks
    for chunk, out_ref in enumerate(coded):
        places = [
            (p, v, chunk * width + b * LANES)
            for p in range(planes)
            for v in range(nv)
            for b in range(width // LANES)
        ]
        most = None
        for p, v, at in places:
            size = jnp.abs(state_ref[p, v, :, at : at + LANES])
            most = size if most is None else jnp.maximum(most, size)
        blocks = [
            (lambda p=p, v=v, at=at: state_ref[p, v, :, at : at + LANES]) for p, v, at in places
        ]
        put_coded(blocks, most, out_ref, rows)
    open_ref[...] = 1.0 - wall_ref[...].astype(jnp.float32)

    def rows_for(next_ref, previous_ref):
        for p in range(planes):
            for v in range(nv):
                end = rows - 1
                next_ref[p, v, 0:1, :] = NEAR * state_ref[p, v, end:rows, :] + FAR * state_ref[p, v, end - 1 : end, :]
                next_ref[p, v, 1:2, :] = FAR * state_ref[p, v, end:rows, :]
                previous_ref[p, v, 0:1, :] = FAR * state_ref[p, v, 0:1, :]
                previous_ref[p, v, 1:2, :] = NEAR * state_ref[p, v, 0:1, :] + FAR * state_ref[p, v, 1:2, :]

    even_j = lax.axis_index("ja") % 2 == 0
    pl.when(even_j)(lambda: rows_for(j_first, j_second))
    pl.when(jnp.logical_not(even_j))(lambda: rows_for(j_second, j_first))

    lane = lax.broadcasted_iota(jnp.int32, (rows, LANES), 1)

    def columns_for_next(out_ref):
        for p in range(planes):
            for v in range(nv):
                block = state_ref[p, v, :, columns - LANES :]
                one, two = pltpu.roll(block, 1, 1), pltpu.roll(block, 2, 1)
                out_ref[p, v] = jnp.where(lane < 1, NEAR * one, 0.0) + jnp.where(lane < 2, FAR * two, 0.0)

    def columns_for_previous(out_ref):
        for p in range(planes):
            for v in range(nv):
                block = state_ref[p, v, :, :LANES]
                one, two = pltpu.roll(block, LANES - 1, 1), pltpu.roll(block, LANES - 2, 1)
                out_ref[p, v] = jnp.where(lane > LANES - 2, NEAR * one, 0.0) + jnp.where(lane > LANES - 3, FAR * two, 0.0)

    even_k = lax.axis_index("ka") % 2 == 0

    @pl.when(even_k)
    def _():
        columns_for_next(edges_k[0])
        if both_k:
            columns_for_previous(edges_k[1])

    @pl.when(jnp.logical_not(even_k))
    def _():
        columns_for_previous(edges_k[0])
        if both_k:
            columns_for_next(edges_k[1])


def local_kernel(state_ref, *refs):
    x_outs, rows_pad = refs[:-1], refs[-1]
    planes, nv, rows, columns = state_ref.shape
    width = columns // len(x_outs)
    nothing = jnp.zeros((rows, LANES), jnp.float32)
    rows_pad[0:8, :] = jnp.zeros((8, width), jnp.float32)
    rows_pad[8 + rows :, :] = jnp.zeros((8, width), jnp.float32)
    for chunk, x_out in enumerate(x_outs):
        start, stop = chunk * width, (chunk + 1) * width
        for v in range(nv):
            here = [state_ref[p, v, :, start:stop] for p in range(planes)]
            for p in range(planes):
                total = CENTRE * here[p]
                for shift, factor in ((-2, BEHIND_2), (-1, BEHIND_1), (1, NEAR), (2, FAR)):
                    if 0 <= p + shift < planes:
                        total += factor * here[p + shift]
                rows_pad[8 : 8 + rows, :] = here[p]
                total += NEAR * (rows_pad[7 : 7 + rows, :] + rows_pad[9 : 9 + rows, :])
                total += FAR * (rows_pad[6 : 6 + rows, :] + rows_pad[10 : 10 + rows, :])
                left = nothing if start == 0 else state_ref[p, v, :, start - LANES : start]
                right = nothing if stop == columns else state_ref[p, v, :, stop : stop + LANES]
                wide = jnp.concatenate([left, here[p], right], axis=1)
                span = wide.shape[1]
                one = pltpu.roll(wide, 1, 1) + pltpu.roll(wide, span - 1, 1)
                two = pltpu.roll(wide, 2, 1) + pltpu.roll(wide, span - 2, 1)
                total += (NEAR * one + FAR * two)[:, LANES : LANES + width]
                x_out[p, v] = total


def add_plane_terms(coded, x_ref, p, v, block, terms, scale, per):
    nv, rows = x_ref.shape[1:3]
    own = slice(block * LANES, (block + 1) * LANES)
    total = x_ref[p, v, :, own]
    for q, factor in terms:
        total += factor * get_coded(coded, (q * nv + v) * per + block, rows, scale)
    return total


def terms_ahead(planes, p):
    found = [(p + shift - planes, factor) for shift, factor in ((1, NEAR), (2, FAR))]
    return [(q, factor) for q, factor in found if q >= 0]


def terms_behind(planes, p):
    found = [(planes + p - shift, factor) for shift, factor in ((1, BEHIND_1), (2, BEHIND_2))]
    return [(q, factor) for q, factor in found if q < planes]


def halo_kernel(chunk, chunks, counts, j_first, j_second, edges_k, neighbour, open_ref, x_in, x_out):
    planes, nv, rows, width = x_out.shape
    per = width // LANES
    start = chunk * width
    place_i, place_j, place_k = (lax.axis_index(name) for name in ("ia", "ja", "ka"))
    count_i, count_j, count_k = counts
    scale = get_scale(neighbour, planes * nv * per, rows)
    even_i = place_i % 2 == 0

    def with_planes(terms_of):
        for p in range(planes):
            for v in range(nv):
                for block in range(per):
                    own = slice(block * LANES, (block + 1) * LANES)
                    x_out[p, v, :, own] = add_plane_terms(neighbour, x_in, p, v, block, terms_of(planes, p), scale, per)

    takes_ahead = jnp.logical_and(even_i, place_i + 1 < count_i)
    takes_behind = jnp.logical_not(even_i)
    pl.when(takes_ahead)(lambda: with_planes(terms_ahead))
    pl.when(takes_behind)(lambda: with_planes(terms_behind))
    if count_i % 2:
        pl.when(place_i == count_i - 1)(lambda: with_planes(lambda planes, p: []))

    even_j = place_j % 2 == 0
    from_next = place_j + 1 < count_j
    from_previous = place_j > 0

    def add_rows(ref, low):
        at = 0 if low else rows - 2
        for p in range(planes):
            for v in range(nv):
                x_out[p, v, at : at + 2, :] += ref[p, v, :, start : start + width]

    pl.when(jnp.logical_and(even_j, from_next))(lambda: add_rows(j_first, False))
    pl.when(jnp.logical_and(even_j, from_previous))(lambda: add_rows(j_second, True))
    odd_j = jnp.logical_not(even_j)
    pl.when(odd_j)(lambda: add_rows(j_first, True))
    pl.when(jnp.logical_and(odd_j, from_next))(lambda: add_rows(j_second, False))

    even_k = place_k % 2 == 0
    odd_k = jnp.logical_not(even_k)

    def add_columns(ref, low):
        at = 0 if low else width - LANES
        for p in range(planes):
            for v in range(nv):
                x_out[p, v, :, at : at + LANES] += ref[p, v]

    if chunk == 0:
        pl.when(odd_k)(lambda: add_columns(edges_k[0], True))
        if len(edges_k) > 1:
            pl.when(jnp.logical_and(even_k, place_k > 0))(lambda: add_columns(edges_k[1], True))
    if chunk == chunks - 1:
        pl.when(jnp.logical_and(even_k, place_k + 1 < count_k))(lambda: add_columns(edges_k[0], False))
        if len(edges_k) > 1:
            pl.when(jnp.logical_and(odd_k, place_k + 1 < count_k))(lambda: add_columns(edges_k[1], False))

    for p in range(planes):
        open_cells = open_ref[p, :, start : start + width]
        for v in range(nv):
            x_out[p, v] = open_cells * x_out[p, v]


def apply_block(inverse_ref, p, at, vector):
    result = []
    for a in range(len(vector)):
        total = None
        for b in range(len(vector)):
            term = inverse_ref[p, a, b, :, at : at + LANES].astype(jnp.float32) * vector[b]
            total = term if total is None else total + term
        result.append(total)
    return result


def forward_part(chunk, hop, count, inverse_ref, coupling_ref, open_ref, neighbour, face, x_in, x_out, send):
    planes, nv, rows, width = x_out.shape
    per = width // LANES
    first = hop == 0
    terms_of = None
    if not first:
        face_scale = get_scale(face, nv * per, rows)
        if hop % 2 == 0:
            terms_of = terms_behind
        elif hop < count - 1:
            terms_of = terms_ahead
    if terms_of is not None:
        scale = get_scale(neighbour, planes * nv * per, rows)
    most = None
    for block in range(per):
        own = slice(block * LANES, (block + 1) * LANES)
        at = chunk * width + block * LANES
        running = None
        if not first:
            running = [get_coded(face, v * per + block, rows, face_scale) for v in range(nv)]
        for p in range(planes):
            factor = coupling_ref[p, 0, :, at : at + LANES]
            if terms_of is not None:
                open_cells = open_ref[p, :, at : at + LANES]
            right = []
            for v in range(nv):
                entry = x_in[p, v, :, own]
                if terms_of is not None:
                    extra = None
                    for q, weight in terms_of(planes, p):
                        term = weight * get_coded(neighbour, (q * nv + v) * per + block, rows, scale)
                        extra = term if extra is None else extra + term
                    if extra is not None:
                        entry += open_cells * extra
                if running is not None:
                    entry += factor * running[v]
                right.append(entry)
            running = apply_block(inverse_ref, p, at, right)
            for v in range(nv):
                x_out[p, v, :, own] = running[v]
        for v in range(nv):
            size = jnp.abs(running[v])
            most = size if most is None else jnp.maximum(most, size)
    if send is not None:
        put_face(planes - 1, most, x_out, send)


def put_face(plane, most, x_out, send):
    nv, rows, width = x_out.shape[1:]
    blocks = [
        (lambda v=v, at=b * LANES: x_out[plane, v, :, at : at + LANES])
        for v in range(nv)
        for b in range(width // LANES)
    ]
    put_coded(blocks, most, send, rows)


def backward_part(chunk, last, inverse_ref, coupling_ref, face, x_in, x_out, send):
    planes, nv, rows, width = x_out.shape
    per = width // LANES
    if not last:
        scale = get_scale(face, nv * per, rows)
    most = None
    for block in range(per):
        own = slice(block * LANES, (block + 1) * LANES)
        at = chunk * width + block * LANES
        running = None
        if not last:
            running = [get_coded(face, v * per + block, rows, scale) for v in range(nv)]
        for p in reversed(range(planes)):
            base = [x_in[p, v, :, own] for v in range(nv)]
            if running is None:
                running = base
            else:
                factor = coupling_ref[p, 1, :, at : at + LANES]
                change = apply_block(inverse_ref, p, at, [factor * running[v] for v in range(nv)])
                running = [base[v] + change[v] for v in range(nv)]
            for v in range(nv):
                x_out[p, v, :, own] = running[v]
        for v in range(nv):
            size = jnp.abs(running[v])
            most = size if most is None else jnp.maximum(most, size)
    if send is not None:
        put_face(0, most, x_out, send)


def forward_kernel(chunk, hop, count, inverse_ref, coupling_ref, open_ref, neighbour, face, x_in, x_out, send):
    active = lax.axis_index("ia") == hop
    last = hop == count - 1

    @pl.when(active)
    def _():
        forward_part(
            chunk, hop, count, inverse_ref, coupling_ref, open_ref, neighbour, face, x_in, x_out, None if last else send
        )
        if last:
            backward_part(chunk, True, inverse_ref, coupling_ref, None, x_out, x_out, send)

    @pl.when(jnp.logical_not(active))
    def _():
        x_out[...] = x_in[...]


def backward_kernel(chunk, hop, inverse_ref, coupling_ref, face, x_in, x_out, send):
    active = lax.axis_index("ia") == hop

    @pl.when(active)
    def _():
        backward_part(chunk, False, inverse_ref, coupling_ref, face, x_in, x_out, send)

    @pl.when(jnp.logical_not(active))
    def _():
        x_out[...] = x_in[...]


def final_kernel(chunk, inverse_ref, coupling_ref, face, *refs):
    parts, out = refs[:-1], refs[-1]
    width = parts[0].shape[3]
    mine = out.at[:, :, :, chunk * width : (chunk + 1) * width]
    active = lax.axis_index("ia") == 0

    @pl.when(active)
    def _():
        backward_part(chunk, False, inverse_ref, coupling_ref, face, parts[chunk], mine, None)

    @pl.when(jnp.logical_not(active))
    def _():
        mine[...] = parts[chunk][...]

    for other, part in enumerate(parts):
        if other != chunk:
            out[:, :, :, other * width : (other + 1) * width] = part[...]


def whole():
    return pl.BlockSpec(memory_space=VMEM)


def call(kernel, operands, outs, name, alias=None, scratch=()):
    return pl.pallas_call(
        kernel,
        in_specs=[whole()] * len(operands),
        out_specs=[whole()] * len(outs),
        out_shape=outs,
        scratch_shapes=list(scratch),
        input_output_aliases=alias or {},
        compiler_params=pltpu.CompilerParams(vmem_limit_bytes=24 * 2**20),
        name=name,
    )(*operands)


def swaps(count, first):
    partner = list(range(count))
    for i in range(first, count - 1, 2):
        partner[i], partner[i + 1] = i + 1, i
    return list(enumerate(partner))


def swap_of(count, low):
    partner = list(range(count))
    partner[low], partner[low + 1] = low + 1, low
    return list(enumerate(partner))


def shards(state, inverse, coupling, wall):
    planes, nv, rows, columns = state.shape
    chunks = CHUNKS
    width = columns // chunks
    per = width // LANES
    counts = count, count_j, count_k = [lax.axis_size(name) for name in ("ia", "ja", "ka")]
    sets_k = 1 if count_k == 2 else 2

    halo_code = jax.ShapeDtypeStruct(((planes * nv * per + 1) * rows, LANES), jnp.int16)
    face_code = jax.ShapeDtypeStruct(((nv * per + 1) * rows, LANES), jnp.int16)
    full = jax.ShapeDtypeStruct(state.shape, jnp.float32)
    part = jax.ShapeDtypeStruct((planes, nv, rows, width), jnp.float32)
    edge_j = jax.ShapeDtypeStruct((planes, nv, 2, columns), jnp.float32)
    edge_k = jax.ShapeDtypeStruct((planes, nv, rows, LANES), jnp.float32)
    cells = jax.ShapeDtypeStruct((planes, rows, columns), jnp.float32)

    made = call(
        functools.partial(encode_kernel, chunks, sets_k == 2),
        [state, wall],
        [halo_code] * chunks + [edge_j] * 2 + [edge_k] * sets_k + [cells],
        "encode",
    )
    coded, edges_j, edges_k, open_cells = made[:chunks], made[chunks : chunks + 2], made[chunks + 2 : -1], made[-1]
    near = [lax.ppermute(coded[c], "ia", swaps(count, 0)) for c in range(chunks)]
    edges_k = [lax.ppermute(edge, "ka", swaps(count_k, s)) for s, edge in enumerate(edges_k)]
    edges_j = [lax.ppermute(edge, "ja", swaps(count_j, s)) for s, edge in enumerate(edges_j)]
    local = call(local_kernel, [state], [part] * chunks, "local", None, [VMEM((rows + 16, width), jnp.float32)])

    x, far = [], []
    for c in range(chunks):
        later, _ = lax.optimization_barrier((coded[c], near[c]))
        far.append(lax.ppermute(later, "ia", swaps(count, 1)))

        def kernel(*refs, c=c):
            rest = refs[2 + sets_k :]
            halo_kernel(c, chunks, counts, *refs[:2], refs[2 : 2 + sets_k], *rest)

        operands = [*edges_j, *edges_k, near[c], open_cells, local[c]]
        x += call(kernel, operands, [part], "halo", {len(operands) - 1: 0})

    face = [None] * chunks
    for hop in range(count):
        for c in range(chunks):
            if hop == 0:
                def kernel(inverse_ref, coupling_ref, *refs, c=c):
                    forward_kernel(c, 0, count, inverse_ref, coupling_ref, None, None, None, *refs)
                operands = [inverse, coupling, x[c]]
            else:
                kernel = functools.partial(forward_kernel, c, hop, count)
                operands = [inverse, coupling, open_cells, far[c], face[c], x[c]]
            x[c], send = call(kernel, operands, [part, face_code], "forward", {len(operands) - 1: 0})
            face[c] = lax.ppermute(send, "ia", swap_of(count, min(hop, count - 2)))
    for hop in reversed(range(count - 1)):
        for c in range(chunks):
            if hop == 0 and c == chunks - 1:
                operands = [inverse, coupling, face[c], *x]
                return call(functools.partial(final_kernel, c), operands, [full], "last")[0]
            if hop == 0:
                def kernel(*refs, c=c):
                    backward_kernel(c, 0, *refs, None)
                (x[c],) = call(kernel, [inverse, coupling, face[c], x[c]], [part], "backward", {3: 0})
                continue
            kernel = functools.partial(backward_kernel, c, hop)
            x[c], send = call(kernel, [inverse, coupling, face[c], x[c]], [part, face_code], "backward", {3: 0})
            face[c] = lax.ppermute(send, "ia", swap_of(count, hop - 1))


def solution(mesh):
    return jax.shard_map(
        shards,
        mesh=mesh,
        in_specs=(
            P("ia", None, "ja", "ka"),
            P("ia", None, None, "ja", "ka"),
            P("ia", None, "ja", "ka"),
            P("ia", "ja", "ka"),
        ),
        out_specs=P("ia", None, "ja", "ka"),
        check_vma=False,
    )
```

```python
import functools

import jax
import jax.numpy as jnp
from jax import lax
from jax.experimental import pallas as pl
from jax.experimental.pallas import tpu as pltpu
from jax.sharding import PartitionSpec as P

advection = 0.012
viscosity = 0.006
damping = 0.003

CENTRE = -1.5 * advection - 6.0 * viscosity - 18.0 * damping
BEHIND_1 = 2.0 * advection + viscosity + 4.0 * damping
BEHIND_2 = -0.5 * advection - damping
NEAR = viscosity + 4.0 * damping
FAR = -damping

LANES = 128
TOP = 32767.0
VMEM = pltpu.VMEM
CHUNKS = 4
HALO_CHUNKS = 2


def scale_of(code):
    return jnp.exp2(code.astype(jnp.float32) * (1.0 / 256.0))


def put_coded(blocks, most, out_ref, rows):
    code = jnp.ceil(256.0 * jnp.log2(jnp.maximum(most, 1e-30))).astype(jnp.int32)
    factor = TOP / scale_of(code)
    for index, block in enumerate(blocks):
        coded = jnp.floor(block() * factor + 0.5)
        coded = jnp.minimum(jnp.maximum(coded, -TOP), TOP).astype(jnp.int32)
        out_ref[index * rows : (index + 1) * rows, :] = coded.astype(jnp.int16)
    count = len(blocks)
    out_ref[count * rows : (count + 1) * rows, :] = code.astype(jnp.int16)


def get_scale(coded_ref, count, rows):
    code = coded_ref[count * rows : (count + 1) * rows, :].astype(jnp.int32)
    return scale_of(code) * (1.0 / TOP)


def get_coded(coded_ref, index, rows, scale):
    return coded_ref[index * rows : (index + 1) * rows, :].astype(jnp.int32).astype(jnp.float32) * scale


def encode_kernel(start, width, state_ref, out_ref):
    planes, nv, rows, _ = state_ref.shape
    places = [
        (p, v, start + b * LANES) for p in range(planes) for v in range(nv) for b in range(width // LANES)
    ]
    most = None
    for p, v, at in places:
        size = jnp.abs(state_ref[p, v, :, at : at + LANES])
        most = size if most is None else jnp.maximum(most, size)
    blocks = [(lambda p=p, v=v, at=at: state_ref[p, v, :, at : at + LANES]) for p, v, at in places]
    put_coded(blocks, most, out_ref, rows)


def edges_kernel(both_k, state_ref, after_ref, j_first, j_second, *edges_k):
    planes, nv, rows, columns = state_ref.shape

    def rows_for(next_ref, previous_ref):
        for p in range(planes):
            for v in range(nv):
                end = rows - 1
                next_ref[p, v, 0:1, :] = NEAR * state_ref[p, v, end:rows, :] + FAR * state_ref[p, v, end - 1 : end, :]
                next_ref[p, v, 1:2, :] = FAR * state_ref[p, v, end:rows, :]
                previous_ref[p, v, 0:1, :] = FAR * state_ref[p, v, 0:1, :]
                previous_ref[p, v, 1:2, :] = NEAR * state_ref[p, v, 0:1, :] + FAR * state_ref[p, v, 1:2, :]

    even_j = lax.axis_index("ja") % 2 == 0
    pl.when(even_j)(lambda: rows_for(j_first, j_second))
    pl.when(jnp.logical_not(even_j))(lambda: rows_for(j_second, j_first))

    lane = lax.broadcasted_iota(jnp.int32, (rows, LANES), 1)

    def columns_for_next(out_ref):
        for p in range(planes):
            for v in range(nv):
                block = state_ref[p, v, :, columns - LANES :]
                one, two = pltpu.roll(block, 1, 1), pltpu.roll(block, 2, 1)
                out_ref[p, v] = jnp.where(lane < 1, NEAR * one, 0.0) + jnp.where(lane < 2, FAR * two, 0.0)

    def columns_for_previous(out_ref):
        for p in range(planes):
            for v in range(nv):
                block = state_ref[p, v, :, :LANES]
                one, two = pltpu.roll(block, LANES - 1, 1), pltpu.roll(block, LANES - 2, 1)
                out_ref[p, v] = jnp.where(lane > LANES - 2, NEAR * one, 0.0) + jnp.where(lane > LANES - 3, FAR * two, 0.0)

    even_k = lax.axis_index("ka") % 2 == 0

    @pl.when(even_k)
    def _():
        columns_for_next(edges_k[0])
        if both_k:
            columns_for_previous(edges_k[1])

    @pl.when(jnp.logical_not(even_k))
    def _():
        columns_for_previous(edges_k[0])
        if both_k:
            columns_for_next(edges_k[1])


def local_kernel(state_ref, wall_ref, *refs):
    x_outs, open_ref, rows_pad = refs[:-2], refs[-2], refs[-1]
    open_ref[...] = 1.0 - wall_ref[...].astype(jnp.float32)
    planes, nv, rows, columns = state_ref.shape
    width = columns // len(x_outs)
    nothing = jnp.zeros((rows, LANES), jnp.float32)
    rows_pad[0:8, :] = jnp.zeros((8, width), jnp.float32)
    rows_pad[8 + rows :, :] = jnp.zeros((8, width), jnp.float32)
    for chunk, x_out in enumerate(x_outs):
        start, stop = chunk * width, (chunk + 1) * width
        for v in range(nv):
            here = [state_ref[p, v, :, start:stop] for p in range(planes)]
            for p in range(planes):
                total = CENTRE * here[p]
                for shift, factor in ((-2, BEHIND_2), (-1, BEHIND_1), (1, NEAR), (2, FAR)):
                    if 0 <= p + shift < planes:
                        total += factor * here[p + shift]
                rows_pad[8 : 8 + rows, :] = here[p]
                total += NEAR * (rows_pad[7 : 7 + rows, :] + rows_pad[9 : 9 + rows, :])
                total += FAR * (rows_pad[6 : 6 + rows, :] + rows_pad[10 : 10 + rows, :])
                left = nothing if start == 0 else state_ref[p, v, :, start - LANES : start]
                right = nothing if stop == columns else state_ref[p, v, :, stop : stop + LANES]
                wide = jnp.concatenate([left, here[p], right], axis=1)
                span = wide.shape[1]
                one = pltpu.roll(wide, 1, 1) + pltpu.roll(wide, span - 1, 1)
                two = pltpu.roll(wide, 2, 1) + pltpu.roll(wide, span - 2, 1)
                total += (NEAR * one + FAR * two)[:, LANES : LANES + width]
                x_out[p, v] = total


def terms_ahead(planes, p):
    found = [(p + shift - planes, factor) for shift, factor in ((1, NEAR), (2, FAR))]
    return [(q, factor) for q, factor in found if q >= 0]


def terms_behind(planes, p):
    found = [(planes + p - shift, factor) for shift, factor in ((1, BEHIND_1), (2, BEHIND_2))]
    return [(q, factor) for q, factor in found if q < planes]


def halo_kernel(half, halves, counts, j_first, j_second, edges_k, neighbour, open_ref, x_ins, x_outs):
    planes, nv, rows, width = x_outs[0].shape
    per = width // LANES
    parts = len(x_outs)
    start = half * parts * width
    place_i, place_j, place_k = (lax.axis_index(name) for name in ("ia", "ja", "ka"))
    count_i, count_j, count_k = counts
    scale = get_scale(neighbour, planes * nv * per * parts, rows)
    even_i = place_i % 2 == 0

    def with_planes(terms_of):
        for p in range(planes):
            for v in range(nv):
                for block in range(per * parts):
                    own = slice(block % per * LANES, (block % per + 1) * LANES)
                    total = x_ins[block // per][p, v, :, own]
                    for q, factor in terms_of(planes, p):
                        total += factor * get_coded(neighbour, (q * nv + v) * per * parts + block, rows, scale)
                    x_outs[block // per][p, v, :, own] = total

    takes_ahead = jnp.logical_and(even_i, place_i + 1 < count_i)
    takes_behind = jnp.logical_not(even_i)
    pl.when(takes_ahead)(lambda: with_planes(terms_ahead))
    pl.when(takes_behind)(lambda: with_planes(terms_behind))
    if count_i % 2:
        pl.when(place_i == count_i - 1)(lambda: with_planes(lambda planes, p: []))

    even_j = place_j % 2 == 0
    odd_j = jnp.logical_not(even_j)
    from_next = place_j + 1 < count_j
    from_previous = place_j > 0

    def add_rows(ref, low):
        at = 0 if low else rows - 2
        for p in range(planes):
            for v in range(nv):
                for part, x_out in enumerate(x_outs):
                    first = start + part * width
                    x_out[p, v, at : at + 2, :] += ref[p, v, :, first : first + width]

    pl.when(jnp.logical_and(even_j, from_next))(lambda: add_rows(j_first, False))
    pl.when(jnp.logical_and(even_j, from_previous))(lambda: add_rows(j_second, True))
    pl.when(odd_j)(lambda: add_rows(j_first, True))
    pl.when(jnp.logical_and(odd_j, from_next))(lambda: add_rows(j_second, False))

    even_k = place_k % 2 == 0
    odd_k = jnp.logical_not(even_k)

    def add_columns(ref, low):
        at = 0 if low else width - LANES
        x_out = x_outs[0 if low else -1]
        for p in range(planes):
            for v in range(nv):
                x_out[p, v, :, at : at + LANES] += ref[p, v]

    if half == 0:
        pl.when(odd_k)(lambda: add_columns(edges_k[0], True))
        if len(edges_k) > 1:
            pl.when(jnp.logical_and(even_k, place_k > 0))(lambda: add_columns(edges_k[1], True))
    if half == halves - 1:
        pl.when(jnp.logical_and(even_k, place_k + 1 < count_k))(lambda: add_columns(edges_k[0], False))
        if len(edges_k) > 1:
            pl.when(jnp.logical_and(odd_k, place_k + 1 < count_k))(lambda: add_columns(edges_k[1], False))

    for p in range(planes):
        for part, x_out in enumerate(x_outs):
            first = start + part * width
            open_cells = open_ref[p, :, first : first + width]
            for v in range(nv):
                x_out[p, v] = open_cells * x_out[p, v]


def apply_block(inverse_ref, p, at, vector):
    result = []
    for a in range(len(vector)):
        total = None
        for b in range(len(vector)):
            term = inverse_ref[p, a, b, :, at : at + LANES].astype(jnp.float32) * vector[b]
            total = term if total is None else total + term
        result.append(total)
    return result


def forward_part(chunk, parts, hop, count, inverse_ref, coupling_ref, open_ref, neighbour, face, x_in, x_out, send):
    planes, nv, rows, width = x_out.shape
    per = width // LANES
    first = hop == 0
    terms_of = None
    if not first:
        face_scale = get_scale(face, nv * per, rows)
        if hop % 2 == 0:
            terms_of = terms_behind
        elif hop < count - 1:
            terms_of = terms_ahead
    if terms_of is not None:
        scale = get_scale(neighbour, planes * nv * per * parts, rows)
    skip = chunk % parts * per
    most = None
    for block in range(per):
        own = slice(block * LANES, (block + 1) * LANES)
        at = chunk * width + block * LANES
        running = None
        if not first:
            running = [get_coded(face, v * per + block, rows, face_scale) for v in range(nv)]
        for p in range(planes):
            factor = coupling_ref[p, 0, :, at : at + LANES]
            if terms_of is not None:
                open_cells = open_ref[p, :, at : at + LANES]
            right = []
            for v in range(nv):
                entry = x_in[p, v, :, own]
                if terms_of is not None:
                    extra = None
                    for q, weight in terms_of(planes, p):
                        term = weight * get_coded(neighbour, (q * nv + v) * per * parts + skip + block, rows, scale)
                        extra = term if extra is None else extra + term
                    if extra is not None:
                        entry += open_cells * extra
                if running is not None:
                    entry += factor * running[v]
                right.append(entry)
            running = apply_block(inverse_ref, p, at, right)
            for v in range(nv):
                x_out[p, v, :, own] = running[v]
        for v in range(nv):
            size = jnp.abs(running[v])
            most = size if most is None else jnp.maximum(most, size)
    if send is not None:
        put_face(planes - 1, most, x_out, send)


def put_face(plane, most, x_out, send):
    nv, rows, width = x_out.shape[1:]
    blocks = [
        (lambda v=v, at=b * LANES: x_out[plane, v, :, at : at + LANES])
        for v in range(nv)
        for b in range(width // LANES)
    ]
    put_coded(blocks, most, send, rows)


def backward_part(chunk, last, inverse_ref, coupling_ref, face, x_in, x_out, send):
    planes, nv, rows, width = x_out.shape
    per = width // LANES
    if not last:
        scale = get_scale(face, nv * per, rows)
    most = None
    for block in range(per):
        own = slice(block * LANES, (block + 1) * LANES)
        at = chunk * width + block * LANES
        running = None
        if not last:
            running = [get_coded(face, v * per + block, rows, scale) for v in range(nv)]
        for p in reversed(range(planes)):
            base = [x_in[p, v, :, own] for v in range(nv)]
            if running is None:
                running = base
            else:
                factor = coupling_ref[p, 1, :, at : at + LANES]
                change = apply_block(inverse_ref, p, at, [factor * running[v] for v in range(nv)])
                running = [base[v] + change[v] for v in range(nv)]
            for v in range(nv):
                x_out[p, v, :, own] = running[v]
        for v in range(nv):
            size = jnp.abs(running[v])
            most = size if most is None else jnp.maximum(most, size)
    if send is not None:
        put_face(0, most, x_out, send)


def forward_kernel(chunk, parts, hop, count, inverse_ref, coupling_ref, open_ref, neighbour, face, x_in, x_out, send):
    active = lax.axis_index("ia") == hop
    last = hop == count - 1

    @pl.when(active)
    def _():
        forward_part(
            chunk, parts, hop, count, inverse_ref, coupling_ref, open_ref, neighbour, face, x_in, x_out,
            None if last else send,
        )
        if last:
            backward_part(chunk, True, inverse_ref, coupling_ref, None, x_out, x_out, send)

    @pl.when(jnp.logical_not(active))
    def _():
        x_out[...] = x_in[...]


def backward_kernel(chunk, hop, inverse_ref, coupling_ref, face, x_in, x_out, send):
    active = lax.axis_index("ia") == hop

    @pl.when(active)
    def _():
        backward_part(chunk, False, inverse_ref, coupling_ref, face, x_in, x_out, send)

    @pl.when(jnp.logical_not(active))
    def _():
        x_out[...] = x_in[...]


def final_kernel(chunk, inverse_ref, coupling_ref, face, *refs):
    parts, out = refs[:-1], refs[-1]
    width = parts[0].shape[3]
    mine = out.at[:, :, :, chunk * width : (chunk + 1) * width]
    active = lax.axis_index("ia") == 0

    @pl.when(active)
    def _():
        backward_part(chunk, False, inverse_ref, coupling_ref, face, parts[chunk], mine, None)

    @pl.when(jnp.logical_not(active))
    def _():
        mine[...] = parts[chunk][...]

    for other, part in enumerate(parts):
        if other != chunk:
            out[:, :, :, other * width : (other + 1) * width] = part[...]


def whole():
    return pl.BlockSpec(memory_space=VMEM)


def call(kernel, operands, outs, name, alias=None, scratch=(), cost=None):
    return pl.pallas_call(
        kernel,
        in_specs=[whole()] * len(operands),
        out_specs=[whole()] * len(outs),
        out_shape=outs,
        scratch_shapes=list(scratch),
        input_output_aliases=alias or {},
        compiler_params=pltpu.CompilerParams(vmem_limit_bytes=12 * 2**20),
        cost_estimate=cost,
        name=name,
    )(*operands)


def swaps(count, first):
    partner = list(range(count))
    for i in range(first, count - 1, 2):
        partner[i], partner[i + 1] = i + 1, i
    return list(enumerate(partner))


def shards(state, inverse, coupling, wall):
    planes, nv, rows, columns = state.shape
    chunks, halves = CHUNKS, HALO_CHUNKS
    parts = chunks // halves
    width = columns // chunks
    per = width // LANES
    counts = count, count_j, count_k = [lax.axis_size(name) for name in ("ia", "ja", "ka")]
    sets_k = 1 if count_k == 2 else 2

    halo_code = jax.ShapeDtypeStruct(((planes * nv * per * parts + 1) * rows, LANES), jnp.int16)
    face_code = jax.ShapeDtypeStruct(((nv * per + 1) * rows, LANES), jnp.int16)
    full = jax.ShapeDtypeStruct(state.shape, jnp.float32)
    part = jax.ShapeDtypeStruct((planes, nv, rows, width), jnp.float32)
    edge_j = jax.ShapeDtypeStruct((planes, nv, 2, columns), jnp.float32)
    edge_k = jax.ShapeDtypeStruct((planes, nv, rows, LANES), jnp.float32)
    cells = jax.ShapeDtypeStruct((planes, rows, columns), jnp.float32)

    coded = []
    for h in range(halves):
        kernel = functools.partial(encode_kernel, h * parts * width, parts * width)
        coded += call(kernel, [state], [halo_code], "encode")
    near = [lax.ppermute(coded[h], "ia", swaps(count, 0)) for h in range(halves)]
    made = call(
        functools.partial(edges_kernel, sets_k == 2), [state, coded[-1]], [edge_j] * 2 + [edge_k] * sets_k, "edges"
    )
    edges_j, edges_k = made[:2], made[2:]
    edges_k = [lax.ppermute(edge, "ka", swaps(count_k, s)) for s, edge in enumerate(edges_k)]
    edges_j = [lax.ppermute(edge, "ja", swaps(count_j, s)) for s, edge in enumerate(edges_j)]
    size = state.size
    *local, open_cells = call(
        local_kernel,
        [state, wall],
        [part] * chunks + [cells],
        "local",
        None,
        [VMEM((rows + 16, width), jnp.float32)],
        pl.CostEstimate(flops=40 * size, bytes_accessed=10 * size, transcendentals=0),
    )

    def hop_pair(value, source, target):
        return lax.ppermute(value, "ia", [(source, target)])

    gated = lax.optimization_barrier((*coded, open_cells, *edges_j, *edges_k))[:halves]
    far = [lax.ppermute(value, "ia", swaps(count, 1)) for value in gated]
    x, face = [], [None] * chunks
    for h in range(halves):
        def kernel(*refs, h=h):
            rest = refs[2 + sets_k : 4 + sets_k]
            xs = refs[4 + sets_k :]
            halo_kernel(h, halves, counts, *refs[:2], refs[2 : 2 + sets_k], *rest, xs[:parts], xs[parts:])

        operands = [*edges_j, *edges_k, near[h], open_cells, *local[h * parts : (h + 1) * parts]]
        first = len(operands) - parts
        x += call(kernel, operands, [part] * parts, "halo", {first + i: i for i in range(parts)})
        for c in range(h * parts, (h + 1) * parts):
            def kernel(inverse_ref, coupling_ref, *refs, c=c):
                forward_kernel(c, parts, 0, count, inverse_ref, coupling_ref, None, None, None, *refs)

            x[c], send = call(kernel, [inverse, coupling, x[c]], [part, face_code], "forward", {2: 0})
            face[c] = hop_pair(send, 0, 1)

    for hop in range(1, count):
        for c in range(chunks):
            kernel = functools.partial(forward_kernel, c, parts, hop, count)
            operands = [inverse, coupling, open_cells, far[c // parts], face[c], x[c]]
            x[c], send = call(kernel, operands, [part, face_code], "forward", {5: 0})
            face[c] = hop_pair(send, hop, hop + 1) if hop < count - 1 else hop_pair(send, hop, hop - 1)
    for hop in reversed(range(1, count - 1)):
        for c in range(chunks):
            kernel = functools.partial(backward_kernel, c, hop)
            x[c], send = call(kernel, [inverse, coupling, face[c], x[c]], [part, face_code], "backward", {3: 0})
            face[c] = hop_pair(send, hop, hop - 1)
    for c in range(chunks - 1):
        def kernel(*refs, c=c):
            backward_kernel(c, 0, *refs, None)

        (x[c],) = call(kernel, [inverse, coupling, face[c], x[c]], [part], "backward", {3: 0})
    return call(functools.partial(final_kernel, chunks - 1), [inverse, coupling, face[-1], *x], [full], "last")[0]


def solution(mesh):
    return jax.shard_map(
        shards,
        mesh=mesh,
        in_specs=(
            P("ia", None, "ja", "ka"),
            P("ia", None, None, "ja", "ka"),
            P("ia", None, "ja", "ka"),
            P("ia", "ja", "ka"),
        ),
        out_specs=P("ia", None, "ja", "ka"),
        check_vma=False,
    )
```

```python
import functools

import jax
import jax.numpy as jnp
from jax import lax
from jax.experimental import pallas as pl
from jax.experimental.pallas import tpu as pltpu
from jax.sharding import PartitionSpec as P

advection = 0.012
viscosity = 0.006
damping = 0.003

CENTRE = -1.5 * advection - 6.0 * viscosity - 18.0 * damping
BEHIND_1 = 2.0 * advection + viscosity + 4.0 * damping
BEHIND_2 = -0.5 * advection - damping
NEAR = viscosity + 4.0 * damping
FAR = -damping

LANES = 128
TOP = 32767.0
VMEM = pltpu.VMEM
CHUNKS = 2
HALO_CHUNKS = 2


def scale_of(code):
    return jnp.exp2(code.astype(jnp.float32) * (1.0 / 256.0))


def put_coded(blocks, most, out_ref, rows):
    code = jnp.ceil(256.0 * jnp.log2(jnp.maximum(most, 1e-30))).astype(jnp.int32)
    factor = TOP / scale_of(code)
    for index, block in enumerate(blocks):
        coded = jnp.floor(block() * factor + 0.5)
        coded = jnp.minimum(jnp.maximum(coded, -TOP), TOP).astype(jnp.int32)
        out_ref[index * rows : (index + 1) * rows, :] = coded.astype(jnp.int16)
    count = len(blocks)
    out_ref[count * rows : (count + 1) * rows, :] = code.astype(jnp.int16)


def get_scale(coded_ref, count, rows):
    code = coded_ref[count * rows : (count + 1) * rows, :].astype(jnp.int32)
    return scale_of(code) * (1.0 / TOP)


def get_coded(coded_ref, index, rows, scale):
    return coded_ref[index * rows : (index + 1) * rows, :].astype(jnp.int32).astype(jnp.float32) * scale


def encode_kernel(start, width, state_ref, out_ref):
    planes, nv, rows, _ = state_ref.shape
    places = [
        (p, v, start + b * LANES) for p in range(planes) for v in range(nv) for b in range(width // LANES)
    ]
    most = None
    for p, v, at in places:
        size = jnp.abs(state_ref[p, v, :, at : at + LANES])
        most = size if most is None else jnp.maximum(most, size)
    blocks = [(lambda p=p, v=v, at=at: state_ref[p, v, :, at : at + LANES]) for p, v, at in places]
    put_coded(blocks, most, out_ref, rows)


def edges_kernel(both_k, state_ref, after_ref, j_first, j_second, *edges_k):
    planes, nv, rows, columns = state_ref.shape

    def rows_for(next_ref, previous_ref):
        for p in range(planes):
            for v in range(nv):
                end = rows - 1
                next_ref[p, v, 0:1, :] = NEAR * state_ref[p, v, end:rows, :] + FAR * state_ref[p, v, end - 1 : end, :]
                next_ref[p, v, 1:2, :] = FAR * state_ref[p, v, end:rows, :]
                previous_ref[p, v, 0:1, :] = FAR * state_ref[p, v, 0:1, :]
                previous_ref[p, v, 1:2, :] = NEAR * state_ref[p, v, 0:1, :] + FAR * state_ref[p, v, 1:2, :]

    even_j = lax.axis_index("ja") % 2 == 0
    pl.when(even_j)(lambda: rows_for(j_first, j_second))
    pl.when(jnp.logical_not(even_j))(lambda: rows_for(j_second, j_first))

    lane = lax.broadcasted_iota(jnp.int32, (rows, LANES), 1)

    def columns_for_next(out_ref):
        for p in range(planes):
            for v in range(nv):
                block = state_ref[p, v, :, columns - LANES :]
                one, two = pltpu.roll(block, 1, 1), pltpu.roll(block, 2, 1)
                out_ref[p, v] = jnp.where(lane < 1, NEAR * one, 0.0) + jnp.where(lane < 2, FAR * two, 0.0)

    def columns_for_previous(out_ref):
        for p in range(planes):
            for v in range(nv):
                block = state_ref[p, v, :, :LANES]
                one, two = pltpu.roll(block, LANES - 1, 1), pltpu.roll(block, LANES - 2, 1)
                out_ref[p, v] = jnp.where(lane > LANES - 2, NEAR * one, 0.0) + jnp.where(lane > LANES - 3, FAR * two, 0.0)

    even_k = lax.axis_index("ka") % 2 == 0

    @pl.when(even_k)
    def _():
        columns_for_next(edges_k[0])
        if both_k:
            columns_for_previous(edges_k[1])

    @pl.when(jnp.logical_not(even_k))
    def _():
        columns_for_previous(edges_k[0])
        if both_k:
            columns_for_next(edges_k[1])


def local_kernel(state_ref, wall_ref, *refs):
    x_outs, (open_ref, rows_pad, wall_here, done) = refs[:-4], refs[-4:]
    copy = pltpu.make_async_copy(wall_ref, wall_here, done)
    copy.start()
    planes, nv, rows, columns = state_ref.shape
    width = columns // len(x_outs)
    nothing = jnp.zeros((rows, LANES), jnp.float32)
    rows_pad[0:8, :] = jnp.zeros((8, width), jnp.float32)
    rows_pad[8 + rows :, :] = jnp.zeros((8, width), jnp.float32)
    for chunk, x_out in enumerate(x_outs):
        start, stop = chunk * width, (chunk + 1) * width
        for v in range(nv):
            here = [state_ref[p, v, :, start:stop] for p in range(planes)]
            for p in range(planes):
                total = CENTRE * here[p]
                for shift, factor in ((-2, BEHIND_2), (-1, BEHIND_1), (1, NEAR), (2, FAR)):
                    if 0 <= p + shift < planes:
                        total += factor * here[p + shift]
                rows_pad[8 : 8 + rows, :] = here[p]
                total += NEAR * (rows_pad[7 : 7 + rows, :] + rows_pad[9 : 9 + rows, :])
                total += FAR * (rows_pad[6 : 6 + rows, :] + rows_pad[10 : 10 + rows, :])
                left = nothing if start == 0 else state_ref[p, v, :, start - LANES : start]
                right = nothing if stop == columns else state_ref[p, v, :, stop : stop + LANES]
                wide = jnp.concatenate([left, here[p], right], axis=1)
                span = wide.shape[1]
                one = pltpu.roll(wide, 1, 1) + pltpu.roll(wide, span - 1, 1)
                two = pltpu.roll(wide, 2, 1) + pltpu.roll(wide, span - 2, 1)
                total += (NEAR * one + FAR * two)[:, LANES : LANES + width]
                x_out[p, v] = total
    copy.wait()
    open_ref[...] = 1.0 - wall_here[...].astype(jnp.float32)


def terms_ahead(planes, p):
    found = [(p + shift - planes, factor) for shift, factor in ((1, NEAR), (2, FAR))]
    return [(q, factor) for q, factor in found if q >= 0]


def terms_behind(planes, p):
    found = [(planes + p - shift, factor) for shift, factor in ((1, BEHIND_1), (2, BEHIND_2))]
    return [(q, factor) for q, factor in found if q < planes]


def halo_kernel(half, halves, counts, j_first, j_second, edges_k, neighbour, open_ref, x_ins, x_outs):
    planes, nv, rows, width = x_outs[0].shape
    per = width // LANES
    parts = len(x_outs)
    start = half * parts * width
    place_i, place_j, place_k = (lax.axis_index(name) for name in ("ia", "ja", "ka"))
    count_i, count_j, count_k = counts
    scale = get_scale(neighbour, planes * nv * per * parts, rows)
    even_i = place_i % 2 == 0

    def with_planes(terms_of):
        for p in range(planes):
            for v in range(nv):
                for block in range(per * parts):
                    own = slice(block % per * LANES, (block % per + 1) * LANES)
                    total = x_ins[block // per][p, v, :, own]
                    for q, factor in terms_of(planes, p):
                        total += factor * get_coded(neighbour, (q * nv + v) * per * parts + block, rows, scale)
                    x_outs[block // per][p, v, :, own] = total

    takes_ahead = jnp.logical_and(even_i, place_i + 1 < count_i)
    takes_behind = jnp.logical_not(even_i) if half == 0 else place_i == 1
    pl.when(takes_ahead)(lambda: with_planes(terms_ahead))
    pl.when(takes_behind)(lambda: with_planes(terms_behind))
    neither = jnp.logical_not(jnp.logical_or(takes_ahead, takes_behind))
    pl.when(neither)(lambda: with_planes(lambda planes, p: []))

    even_j = place_j % 2 == 0
    odd_j = jnp.logical_not(even_j)
    from_next = place_j + 1 < count_j
    from_previous = place_j > 0

    def add_rows(ref, low):
        at = 0 if low else rows - 2
        for p in range(planes):
            for v in range(nv):
                for part, x_out in enumerate(x_outs):
                    first = start + part * width
                    x_out[p, v, at : at + 2, :] += ref[p, v, :, first : first + width]

    pl.when(jnp.logical_and(even_j, from_next))(lambda: add_rows(j_first, False))
    pl.when(jnp.logical_and(even_j, from_previous))(lambda: add_rows(j_second, True))
    pl.when(odd_j)(lambda: add_rows(j_first, True))
    pl.when(jnp.logical_and(odd_j, from_next))(lambda: add_rows(j_second, False))

    even_k = place_k % 2 == 0
    odd_k = jnp.logical_not(even_k)

    def add_columns(ref, low):
        at = 0 if low else width - LANES
        x_out = x_outs[0 if low else -1]
        for p in range(planes):
            for v in range(nv):
                x_out[p, v, :, at : at + LANES] += ref[p, v]

    if half == 0:
        pl.when(odd_k)(lambda: add_columns(edges_k[0], True))
        if len(edges_k) > 1:
            pl.when(jnp.logical_and(even_k, place_k > 0))(lambda: add_columns(edges_k[1], True))
    if half == halves - 1:
        pl.when(jnp.logical_and(even_k, place_k + 1 < count_k))(lambda: add_columns(edges_k[0], False))
        if len(edges_k) > 1:
            pl.when(jnp.logical_and(odd_k, place_k + 1 < count_k))(lambda: add_columns(edges_k[1], False))

    for p in range(planes):
        for part, x_out in enumerate(x_outs):
            first = start + part * width
            open_cells = open_ref[p, :, first : first + width]
            for v in range(nv):
                x_out[p, v] = open_cells * x_out[p, v]


def apply_block(inverse_ref, p, at, vector):
    result = []
    for a in range(len(vector)):
        total = None
        for b in range(len(vector)):
            term = inverse_ref[p, a, b, :, at : at + LANES].astype(jnp.float32) * vector[b]
            total = term if total is None else total + term
        result.append(total)
    return result


def forward_part(chunk, parts, first, inverse_ref, coupling_ref, open_ref, messages, face, x_in, x_out, send):
    planes, nv, rows, width = x_out.shape
    per = width // LANES
    if not first:
        face_scale = get_scale(face, nv * per, rows)
    scales = [get_scale(coded, planes * nv * per * parts, rows) for coded, _ in messages]
    skip = chunk % parts * per
    most = None
    for block in range(per):
        own = slice(block * LANES, (block + 1) * LANES)
        at = chunk * width + block * LANES
        running = None
        if not first:
            running = [get_coded(face, v * per + block, rows, face_scale) for v in range(nv)]
        for p in range(planes):
            factor = coupling_ref[p, 0, :, at : at + LANES]
            if messages:
                open_cells = open_ref[p, :, at : at + LANES]
            right = []
            for v in range(nv):
                entry = x_in[p, v, :, own]
                extra = None
                for (coded, terms_of), scale in zip(messages, scales):
                    for q, weight in terms_of(planes, p):
                        index = (q * nv + v) * per * parts + skip + block
                        term = weight * get_coded(coded, index, rows, scale)
                        extra = term if extra is None else extra + term
                if extra is not None:
                    entry += open_cells * extra
                if running is not None:
                    entry += factor * running[v]
                right.append(entry)
            running = apply_block(inverse_ref, p, at, right)
            for v in range(nv):
                x_out[p, v, :, own] = running[v]
        for v in range(nv):
            size = jnp.abs(running[v])
            most = size if most is None else jnp.maximum(most, size)
    if send is not None:
        put_face(planes - 1, most, x_out, send)


def put_face(plane, most, x_out, send):
    nv, rows, width = x_out.shape[1:]
    blocks = [
        (lambda v=v, at=b * LANES: x_out[plane, v, :, at : at + LANES])
        for v in range(nv)
        for b in range(width // LANES)
    ]
    put_coded(blocks, most, send, rows)


def backward_part(chunk, last, inverse_ref, coupling_ref, face, x_in, x_out, send):
    planes, nv, rows, width = x_out.shape
    per = width // LANES
    if not last:
        scale = get_scale(face, nv * per, rows)
    most = None
    for block in range(per):
        own = slice(block * LANES, (block + 1) * LANES)
        at = chunk * width + block * LANES
        running = None
        if not last:
            running = [get_coded(face, v * per + block, rows, scale) for v in range(nv)]
        for p in reversed(range(planes)):
            base = [x_in[p, v, :, own] for v in range(nv)]
            if running is None:
                running = base
            else:
                factor = coupling_ref[p, 1, :, at : at + LANES]
                change = apply_block(inverse_ref, p, at, [factor * running[v] for v in range(nv)])
                running = [base[v] + change[v] for v in range(nv)]
            for v in range(nv):
                x_out[p, v, :, own] = running[v]
        for v in range(nv):
            size = jnp.abs(running[v])
            most = size if most is None else jnp.maximum(most, size)
    if send is not None:
        put_face(0, most, x_out, send)


def forward_kernel(chunk, parts, hop, count, kinds, inverse_ref, coupling_ref, *refs):
    active = lax.axis_index("ia") == hop
    first, last = hop == 0, hop == count - 1
    x_in, x_out, send = refs[-3:]
    open_ref = face = None
    messages = []
    if not first:
        open_ref, face = refs[0], refs[1]
        messages = list(zip(refs[2:-3], kinds))

    @pl.when(active)
    def _():
        forward_part(
            chunk, parts, first, inverse_ref, coupling_ref, open_ref, messages, face, x_in, x_out,
            None if last else send,
        )
        if last:
            backward_part(chunk, True, inverse_ref, coupling_ref, None, x_out, x_out, send)

    @pl.when(jnp.logical_not(active))
    def _():
        x_out[...] = x_in[...]


def backward_kernel(chunk, hop, inverse_ref, coupling_ref, face, x_in, x_out, send):
    active = lax.axis_index("ia") == hop

    @pl.when(active)
    def _():
        backward_part(chunk, False, inverse_ref, coupling_ref, face, x_in, x_out, send)

    @pl.when(jnp.logical_not(active))
    def _():
        x_out[...] = x_in[...]


def final_kernel(chunk, inverse_ref, coupling_ref, face, *refs):
    parts, out = refs[:-1], refs[-1]
    width = parts[0].shape[3]
    mine = out.at[:, :, :, chunk * width : (chunk + 1) * width]
    active = lax.axis_index("ia") == 0

    @pl.when(active)
    def _():
        backward_part(chunk, False, inverse_ref, coupling_ref, face, parts[chunk], mine, None)

    @pl.when(jnp.logical_not(active))
    def _():
        mine[...] = parts[chunk][...]

    for other, part in enumerate(parts):
        if other != chunk:
            out[:, :, :, other * width : (other + 1) * width] = part[...]


def whole():
    return pl.BlockSpec(memory_space=VMEM)


def call(kernel, operands, outs, name, alias=None, scratch=(), cost=None, far=()):
    return pl.pallas_call(
        kernel,
        in_specs=[pl.BlockSpec(memory_space=pl.ANY) if i in far else whole() for i in range(len(operands))],
        out_specs=[whole()] * len(outs),
        out_shape=outs,
        scratch_shapes=list(scratch),
        input_output_aliases=alias or {},
        compiler_params=pltpu.CompilerParams(vmem_limit_bytes=12 * 2**20),
        cost_estimate=cost,
        name=name,
    )(*operands)


def swaps(count, first):
    partner = list(range(count))
    for i in range(first, count - 1, 2):
        partner[i], partner[i + 1] = i + 1, i
    return list(enumerate(partner))


def shards(state, inverse, coupling, wall):
    planes, nv, rows, columns = state.shape
    chunks, halves = CHUNKS, HALO_CHUNKS
    parts = chunks // halves
    width = columns // chunks
    per = width // LANES
    counts = count, count_j, count_k = [lax.axis_size(name) for name in ("ia", "ja", "ka")]
    sets_k = 1 if count_k == 2 else 2

    halo_code = jax.ShapeDtypeStruct(((planes * nv * per * parts + 1) * rows, LANES), jnp.int16)
    face_code = jax.ShapeDtypeStruct(((nv * per + 1) * rows, LANES), jnp.int16)
    full = jax.ShapeDtypeStruct(state.shape, jnp.float32)
    part = jax.ShapeDtypeStruct((planes, nv, rows, width), jnp.float32)
    edge_j = jax.ShapeDtypeStruct((planes, nv, 2, columns), jnp.float32)
    edge_k = jax.ShapeDtypeStruct((planes, nv, rows, LANES), jnp.float32)
    cells = jax.ShapeDtypeStruct((planes, rows, columns), jnp.float32)

    coded = []
    for h in range(halves):
        kernel = functools.partial(encode_kernel, h * parts * width, parts * width)
        coded += call(kernel, [state], [halo_code], "encode")
    to_even = [(i + 1, i) for i in range(0, count - 1, 2)]
    near = [lax.ppermute(coded[h], "ia", swaps(count, 0) if h == 0 else to_even + [(0, 1)]) for h in range(halves)]
    made = call(
        functools.partial(edges_kernel, sets_k == 2), [state, coded[-1]], [edge_j] * 2 + [edge_k] * sets_k, "edges"
    )
    edges_j, edges_k = made[:2], made[2:]
    edges_k = [lax.ppermute(edge, "ka", swaps(count_k, s)) for s, edge in enumerate(edges_k)]
    edges_j = [lax.ppermute(edge, "ja", swaps(count_j, s)) for s, edge in enumerate(edges_j)]
    size = state.size
    *local, open_cells = call(
        local_kernel,
        [state, wall],
        [part] * chunks + [cells],
        "local",
        None,
        [VMEM((rows + 16, width), jnp.float32), VMEM(wall.shape, wall.dtype), pltpu.SemaphoreType.DMA],
        pl.CostEstimate(flops=40 * size, bytes_accessed=10 * size, transcendentals=0),
        (1,),
    )

    def hop_pair(value, source, target):
        low = min(source, target)
        return lax.ppermute(value, "ia", swaps(count, 0) if low % 2 == 0 and count % 2 == 0 else [(source, target)])

    to_odd = [(i + 1, i) for i in range(1, count - 1, 2)]
    gates = [edges_k] + [[*edges_k, open_cells]] * (halves - 1)
    gated = [lax.optimization_barrier((value, *gate))[0] for value, gate in zip(coded, gates)]
    far_ahead = [lax.ppermute(value, "ia", to_odd) for value in gated]

    x, sent, face = [], [], [None] * chunks
    for h in range(halves):
        def kernel(*refs, h=h):
            rest = refs[2 + sets_k : 4 + sets_k]
            xs = refs[4 + sets_k :]
            halo_kernel(h, halves, counts, *refs[:2], refs[2 : 2 + sets_k], *rest, xs[:parts], xs[parts:])

        operands = [*edges_j, *edges_k, near[h], open_cells, *local[h * parts : (h + 1) * parts]]
        first = len(operands) - parts
        x += call(kernel, operands, [part] * parts, "halo", {first + i: i for i in range(parts)})
        for c in range(h * parts, (h + 1) * parts):
            kernel = functools.partial(forward_kernel, c, parts, 0, count, ())
            x[c], send = call(kernel, [inverse, coupling, x[c]], [part, face_code], "forward", {2: 0})
            face[c] = hop_pair(send, 0, 1)
            sent.append(send)

    gated = lax.optimization_barrier((*coded, sent[0]))[:halves]
    to_behind = [[(i, i + 1) for i in range(1, count - 1) if h or i % 2] for h in range(halves)]
    far_behind = [lax.ppermute(gated[h], "ia", to_behind[h]) for h in range(halves)]

    for hop in range(1, count):
        for c in range(chunks):
            h = c // parts
            messages, kinds = [], []
            if hop % 2 and hop < count - 1:
                messages, kinds = messages + [far_ahead[h]], kinds + [terms_ahead]
            if hop >= 2 and (hop % 2 == 0 or h):
                messages, kinds = messages + [far_behind[h]], kinds + [terms_behind]
            kernel = functools.partial(forward_kernel, c, parts, hop, count, kinds)
            operands = [inverse, coupling, open_cells, face[c], *messages, x[c]]
            x[c], send = call(kernel, operands, [part, face_code], "forward", {len(operands) - 1: 0})
            face[c] = hop_pair(send, hop, hop + 1) if hop < count - 1 else hop_pair(send, hop, hop - 1)
    for hop in reversed(range(1, count - 1)):
        for c in range(chunks):
            kernel = functools.partial(backward_kernel, c, hop)
            x[c], send = call(kernel, [inverse, coupling, face[c], x[c]], [part, face_code], "backward", {3: 0})
            face[c] = hop_pair(send, hop, hop - 1)
    for c in range(chunks - 1):
        def kernel(*refs, c=c):
            backward_kernel(c, 0, *refs, None)

        (x[c],) = call(kernel, [inverse, coupling, face[c], x[c]], [part], "backward", {3: 0})
    return call(functools.partial(final_kernel, chunks - 1), [inverse, coupling, face[-1], *x], [full], "last")[0]


def solution(mesh):
    return jax.shard_map(
        shards,
        mesh=mesh,
        in_specs=(
            P("ia", None, "ja", "ka"),
            P("ia", None, None, "ja", "ka"),
            P("ia", None, "ja", "ka"),
            P("ia", "ja", "ka"),
        ),
        out_specs=P("ia", None, "ja", "ka"),
        check_vma=False,
    )
```

```python
import functools

import jax
import jax.numpy as jnp
from jax import lax
from jax.experimental import pallas as pl
from jax.experimental.pallas import tpu as pltpu
from jax.sharding import PartitionSpec as P

advection = 0.012
viscosity = 0.006
damping = 0.003

CENTRE = -1.5 * advection - 6.0 * viscosity - 18.0 * damping
BEHIND_1 = 2.0 * advection + viscosity + 4.0 * damping
BEHIND_2 = -0.5 * advection - damping
NEAR = viscosity + 4.0 * damping
FAR = -damping

LANES = 128
TOP = 32767.0
VMEM = pltpu.VMEM
CHUNKS = 2
HALO_CHUNKS = 2


def scale_of(code):
    return jnp.exp2(code.astype(jnp.float32) * (1.0 / 256.0))


def put_coded(blocks, most, out_ref, rows):
    code = jnp.ceil(256.0 * jnp.log2(jnp.maximum(most, 1e-30))).astype(jnp.int32)
    factor = TOP / scale_of(code)
    for index, block in enumerate(blocks):
        coded = jnp.floor(block() * factor + 0.5)
        coded = jnp.minimum(jnp.maximum(coded, -TOP), TOP).astype(jnp.int32)
        out_ref[index * rows : (index + 1) * rows, :] = coded.astype(jnp.int16)
    count = len(blocks)
    out_ref[count * rows : (count + 1) * rows, :] = code.astype(jnp.int16)


def get_scale(coded_ref, count, rows):
    code = coded_ref[count * rows : (count + 1) * rows, :].astype(jnp.int32)
    return scale_of(code) * (1.0 / TOP)


def get_coded(coded_ref, index, rows, scale):
    return coded_ref[index * rows : (index + 1) * rows, :].astype(jnp.int32).astype(jnp.float32) * scale


def encode_kernel(start, width, state_ref, out_ref):
    planes, nv, rows, _ = state_ref.shape
    places = [
        (p, v, start + b * LANES) for p in range(planes) for v in range(nv) for b in range(width // LANES)
    ]
    most = None
    for p, v, at in places:
        size = jnp.abs(state_ref[p, v, :, at : at + LANES])
        most = size if most is None else jnp.maximum(most, size)
    blocks = [(lambda p=p, v=v, at=at: state_ref[p, v, :, at : at + LANES]) for p, v, at in places]
    put_coded(blocks, most, out_ref, rows)


def edges_kernel(both_k, state_ref, after_ref, j_first, j_second, *edges_k):
    planes, nv, rows, columns = state_ref.shape

    def rows_for(next_ref, previous_ref):
        for p in range(planes):
            for v in range(nv):
                end = rows - 1
                next_ref[p, v, 0:1, :] = NEAR * state_ref[p, v, end:rows, :] + FAR * state_ref[p, v, end - 1 : end, :]
                next_ref[p, v, 1:2, :] = FAR * state_ref[p, v, end:rows, :]
                previous_ref[p, v, 0:1, :] = FAR * state_ref[p, v, 0:1, :]
                previous_ref[p, v, 1:2, :] = NEAR * state_ref[p, v, 0:1, :] + FAR * state_ref[p, v, 1:2, :]

    even_j = lax.axis_index("ja") % 2 == 0
    pl.when(even_j)(lambda: rows_for(j_first, j_second))
    pl.when(jnp.logical_not(even_j))(lambda: rows_for(j_second, j_first))

    lane = lax.broadcasted_iota(jnp.int32, (rows, LANES), 1)

    def columns_for_next(out_ref):
        for p in range(planes):
            for v in range(nv):
                block = state_ref[p, v, :, columns - LANES :]
                one, two = pltpu.roll(block, 1, 1), pltpu.roll(block, 2, 1)
                out_ref[p, v] = jnp.where(lane < 1, NEAR * one, 0.0) + jnp.where(lane < 2, FAR * two, 0.0)

    def columns_for_previous(out_ref):
        for p in range(planes):
            for v in range(nv):
                block = state_ref[p, v, :, :LANES]
                one, two = pltpu.roll(block, LANES - 1, 1), pltpu.roll(block, LANES - 2, 1)
                out_ref[p, v] = jnp.where(lane > LANES - 2, NEAR * one, 0.0) + jnp.where(lane > LANES - 3, FAR * two, 0.0)

    even_k = lax.axis_index("ka") % 2 == 0

    @pl.when(even_k)
    def _():
        columns_for_next(edges_k[0])
        if both_k:
            columns_for_previous(edges_k[1])

    @pl.when(jnp.logical_not(even_k))
    def _():
        columns_for_previous(edges_k[0])
        if both_k:
            columns_for_next(edges_k[1])


def local_kernel(state_ref, wall_ref, *refs):
    x_outs, open_ref, rows_pad = refs[:-2], refs[-2], refs[-1]
    open_ref[...] = 1.0 - wall_ref[...].astype(jnp.float32)
    planes, nv, rows, columns = state_ref.shape
    width = columns // len(x_outs)
    nothing = jnp.zeros((rows, LANES), jnp.float32)
    rows_pad[0:8, :] = jnp.zeros((8, width), jnp.float32)
    rows_pad[8 + rows :, :] = jnp.zeros((8, width), jnp.float32)
    for chunk, x_out in enumerate(x_outs):
        start, stop = chunk * width, (chunk + 1) * width
        for v in range(nv):
            here = [state_ref[p, v, :, start:stop] for p in range(planes)]
            for p in range(planes):
                total = CENTRE * here[p]
                for shift, factor in ((-2, BEHIND_2), (-1, BEHIND_1), (1, NEAR), (2, FAR)):
                    if 0 <= p + shift < planes:
                        total += factor * here[p + shift]
                rows_pad[8 : 8 + rows, :] = here[p]
                total += NEAR * (rows_pad[7 : 7 + rows, :] + rows_pad[9 : 9 + rows, :])
                total += FAR * (rows_pad[6 : 6 + rows, :] + rows_pad[10 : 10 + rows, :])
                left = nothing if start == 0 else state_ref[p, v, :, start - LANES : start]
                right = nothing if stop == columns else state_ref[p, v, :, stop : stop + LANES]
                wide = jnp.concatenate([left, here[p], right], axis=1)
                span = wide.shape[1]
                one = pltpu.roll(wide, 1, 1) + pltpu.roll(wide, span - 1, 1)
                two = pltpu.roll(wide, 2, 1) + pltpu.roll(wide, span - 2, 1)
                total += (NEAR * one + FAR * two)[:, LANES : LANES + width]
                x_out[p, v] = total


def terms_ahead(planes, p):
    found = [(p + shift - planes, factor) for shift, factor in ((1, NEAR), (2, FAR))]
    return [(q, factor) for q, factor in found if q >= 0]


def terms_behind(planes, p):
    found = [(planes + p - shift, factor) for shift, factor in ((1, BEHIND_1), (2, BEHIND_2))]
    return [(q, factor) for q, factor in found if q < planes]


def halo_kernel(half, halves, counts, j_first, j_second, edges_k, neighbour, open_ref, x_ins, x_outs):
    planes, nv, rows, width = x_outs[0].shape
    per = width // LANES
    parts = len(x_outs)
    start = half * parts * width
    place_i, place_j, place_k = (lax.axis_index(name) for name in ("ia", "ja", "ka"))
    count_i, count_j, count_k = counts
    scale = get_scale(neighbour, planes * nv * per * parts, rows)
    even_i = place_i % 2 == 0

    def with_planes(terms_of):
        for p in range(planes):
            for v in range(nv):
                for block in range(per * parts):
                    own = slice(block % per * LANES, (block % per + 1) * LANES)
                    total = x_ins[block // per][p, v, :, own]
                    for q, factor in terms_of(planes, p):
                        total += factor * get_coded(neighbour, (q * nv + v) * per * parts + block, rows, scale)
                    x_outs[block // per][p, v, :, own] = total

    takes_ahead = jnp.logical_and(even_i, place_i + 1 < count_i)
    takes_behind = jnp.logical_not(even_i)
    pl.when(takes_ahead)(lambda: with_planes(terms_ahead))
    pl.when(takes_behind)(lambda: with_planes(terms_behind))
    if count_i % 2:
        pl.when(place_i == count_i - 1)(lambda: with_planes(lambda planes, p: []))

    even_j = place_j % 2 == 0
    odd_j = jnp.logical_not(even_j)
    from_next = place_j + 1 < count_j
    from_previous = place_j > 0

    def add_rows(ref, low):
        at = 0 if low else rows - 2
        for p in range(planes):
            for v in range(nv):
                for part, x_out in enumerate(x_outs):
                    first = start + part * width
                    x_out[p, v, at : at + 2, :] += ref[p, v, :, first : first + width]

    pl.when(jnp.logical_and(even_j, from_next))(lambda: add_rows(j_first, False))
    pl.when(jnp.logical_and(even_j, from_previous))(lambda: add_rows(j_second, True))
    pl.when(odd_j)(lambda: add_rows(j_first, True))
    pl.when(jnp.logical_and(odd_j, from_next))(lambda: add_rows(j_second, False))

    even_k = place_k % 2 == 0
    odd_k = jnp.logical_not(even_k)

    def add_columns(ref, low):
        at = 0 if low else width - LANES
        x_out = x_outs[0 if low else -1]
        for p in range(planes):
            for v in range(nv):
                x_out[p, v, :, at : at + LANES] += ref[p, v]

    if half == 0:
        pl.when(odd_k)(lambda: add_columns(edges_k[0], True))
        if len(edges_k) > 1:
            pl.when(jnp.logical_and(even_k, place_k > 0))(lambda: add_columns(edges_k[1], True))
    if half == halves - 1:
        pl.when(jnp.logical_and(even_k, place_k + 1 < count_k))(lambda: add_columns(edges_k[0], False))
        if len(edges_k) > 1:
            pl.when(jnp.logical_and(odd_k, place_k + 1 < count_k))(lambda: add_columns(edges_k[1], False))

    for p in range(planes):
        for part, x_out in enumerate(x_outs):
            first = start + part * width
            open_cells = open_ref[p, :, first : first + width]
            for v in range(nv):
                x_out[p, v] = open_cells * x_out[p, v]


def apply_block(inverse_ref, p, at, vector):
    result = []
    for a in range(len(vector)):
        total = None
        for b in range(len(vector)):
            term = inverse_ref[p, a, b, :, at : at + LANES].astype(jnp.float32) * vector[b]
            total = term if total is None else total + term
        result.append(total)
    return result


def forward_part(chunk, parts, hop, count, inverse_ref, coupling_ref, open_ref, neighbour, face, x_in, x_out, send):
    planes, nv, rows, width = x_out.shape
    per = width // LANES
    first = hop == 0
    terms_of = None
    if not first:
        face_scale = get_scale(face, nv * per, rows)
        if hop % 2 == 0:
            terms_of = terms_behind
        elif hop < count - 1:
            terms_of = terms_ahead
    if terms_of is not None:
        scale = get_scale(neighbour, planes * nv * per * parts, rows)
    skip = chunk % parts * per
    most = None
    for block in range(per):
        own = slice(block * LANES, (block + 1) * LANES)
        at = chunk * width + block * LANES
        running = None
        if not first:
            running = [get_coded(face, v * per + block, rows, face_scale) for v in range(nv)]
        for p in range(planes):
            factor = coupling_ref[p, 0, :, at : at + LANES]
            if terms_of is not None:
                open_cells = open_ref[p, :, at : at + LANES]
            right = []
            for v in range(nv):
                entry = x_in[p, v, :, own]
                if terms_of is not None:
                    extra = None
                    for q, weight in terms_of(planes, p):
                        term = weight * get_coded(neighbour, (q * nv + v) * per * parts + skip + block, rows, scale)
                        extra = term if extra is None else extra + term
                    if extra is not None:
                        entry += open_cells * extra
                if running is not None:
                    entry += factor * running[v]
                right.append(entry)
            running = apply_block(inverse_ref, p, at, right)
            for v in range(nv):
                x_out[p, v, :, own] = running[v]
        for v in range(nv):
            size = jnp.abs(running[v])
            most = size if most is None else jnp.maximum(most, size)
    if send is not None:
        put_face(planes - 1, most, x_out, send)


def put_face(plane, most, x_out, send):
    nv, rows, width = x_out.shape[1:]
    blocks = [
        (lambda v=v, at=b * LANES: x_out[plane, v, :, at : at + LANES])
        for v in range(nv)
        for b in range(width // LANES)
    ]
    put_coded(blocks, most, send, rows)


def backward_part(chunk, last, inverse_ref, coupling_ref, face, x_in, x_out, send):
    planes, nv, rows, width = x_out.shape
    per = width // LANES
    if not last:
        scale = get_scale(face, nv * per, rows)
    most = None
    for block in range(per):
        own = slice(block * LANES, (block + 1) * LANES)
        at = chunk * width + block * LANES
        running = None
        if not last:
            running = [get_coded(face, v * per + block, rows, scale) for v in range(nv)]
        for p in reversed(range(planes)):
            base = [x_in[p, v, :, own] for v in range(nv)]
            if running is None:
                running = base
            else:
                factor = coupling_ref[p, 1, :, at : at + LANES]
                change = apply_block(inverse_ref, p, at, [factor * running[v] for v in range(nv)])
                running = [base[v] + change[v] for v in range(nv)]
            for v in range(nv):
                x_out[p, v, :, own] = running[v]
        for v in range(nv):
            size = jnp.abs(running[v])
            most = size if most is None else jnp.maximum(most, size)
    if send is not None:
        put_face(0, most, x_out, send)


def forward_kernel(chunk, parts, hop, count, inverse_ref, coupling_ref, open_ref, neighbour, face, x_in, x_out, send):
    active = lax.axis_index("ia") == hop
    last = hop == count - 1

    @pl.when(active)
    def _():
        forward_part(
            chunk, parts, hop, count, inverse_ref, coupling_ref, open_ref, neighbour, face, x_in, x_out,
            None if last else send,
        )
        if last:
            backward_part(chunk, True, inverse_ref, coupling_ref, None, x_out, x_out, send)

    @pl.when(jnp.logical_not(active))
    def _():
        x_out[...] = x_in[...]


def backward_kernel(chunk, hop, inverse_ref, coupling_ref, face, x_in, x_out, send):
    active = lax.axis_index("ia") == hop

    @pl.when(active)
    def _():
        backward_part(chunk, False, inverse_ref, coupling_ref, face, x_in, x_out, send)

    @pl.when(jnp.logical_not(active))
    def _():
        x_out[...] = x_in[...]


def final_kernel(chunk, inverse_ref, coupling_ref, face, *refs):
    parts, out = refs[:-1], refs[-1]
    width = parts[0].shape[3]
    mine = out.at[:, :, :, chunk * width : (chunk + 1) * width]
    active = lax.axis_index("ia") == 0

    @pl.when(active)
    def _():
        backward_part(chunk, False, inverse_ref, coupling_ref, face, parts[chunk], mine, None)

    @pl.when(jnp.logical_not(active))
    def _():
        mine[...] = parts[chunk][...]

    for other, part in enumerate(parts):
        if other != chunk:
            out[:, :, :, other * width : (other + 1) * width] = part[...]


def whole():
    return pl.BlockSpec(memory_space=VMEM)


def call(kernel, operands, outs, name, alias=None, scratch=(), cost=None):
    return pl.pallas_call(
        kernel,
        in_specs=[whole()] * len(operands),
        out_specs=[whole()] * len(outs),
        out_shape=outs,
        scratch_shapes=list(scratch),
        input_output_aliases=alias or {},
        compiler_params=pltpu.CompilerParams(vmem_limit_bytes=12 * 2**20),
        cost_estimate=cost,
        name=name,
    )(*operands)


def swaps(count, first):
    if count % 2 == 0:
        return [(i, (i + 1 if i % 2 == first else i - 1) % count) for i in range(count)]
    partner = list(range(count))
    for i in range(first, count - 1, 2):
        partner[i], partner[i + 1] = i + 1, i
    return list(enumerate(partner))


def shards(state, inverse, coupling, wall):
    planes, nv, rows, columns = state.shape
    chunks, halves = CHUNKS, HALO_CHUNKS
    parts = chunks // halves
    width = columns // chunks
    per = width // LANES
    counts = count, count_j, count_k = [lax.axis_size(name) for name in ("ia", "ja", "ka")]
    sets_k = 1 if count_k == 2 else 2

    halo_code = jax.ShapeDtypeStruct(((planes * nv * per * parts + 1) * rows, LANES), jnp.int16)
    face_code = jax.ShapeDtypeStruct(((nv * per + 1) * rows, LANES), jnp.int16)
    full = jax.ShapeDtypeStruct(state.shape, jnp.float32)
    part = jax.ShapeDtypeStruct((planes, nv, rows, width), jnp.float32)
    edge_j = jax.ShapeDtypeStruct((planes, nv, 2, columns), jnp.float32)
    edge_k = jax.ShapeDtypeStruct((planes, nv, rows, LANES), jnp.float32)
    cells = jax.ShapeDtypeStruct((planes, rows, columns), jnp.float32)

    coded = []
    for h in range(halves):
        kernel = functools.partial(encode_kernel, h * parts * width, parts * width)
        coded += call(kernel, [state], [halo_code], "encode")
    near = [lax.ppermute(coded[h], "ia", swaps(count, 0)) for h in range(halves)]
    made = call(
        functools.partial(edges_kernel, sets_k == 2), [state, coded[-1]], [edge_j] * 2 + [edge_k] * sets_k, "edges"
    )
    edges_j, edges_k = made[:2], made[2:]
    edges_k = [lax.ppermute(edge, "ka", swaps(count_k, s)) for s, edge in enumerate(edges_k)]
    edges_j = [lax.ppermute(edge, "ja", swaps(count_j, s)) for s, edge in enumerate(edges_j)]
    size = state.size
    *local, open_cells = call(
        local_kernel,
        [state, wall],
        [part] * chunks + [cells],
        "local",
        None,
        [VMEM((rows + 16, width), jnp.float32)],
        pl.CostEstimate(flops=40 * size, bytes_accessed=10 * size, transcendentals=0),
    )

    def hop_pair(value, source, target):
        return lax.ppermute(value, "ia", swaps(count, min(source, target) % 2))

    def pass_on(h, *gate):
        passed = near[h] if count == 4 else coded[h]
        if gate:
            passed = lax.optimization_barrier((passed, *gate))[0]
        return lax.ppermute(passed, "ia", [(i, i ^ 2) for i in range(4)] if count == 4 else swaps(count, 1))

    x, far, face = [], [pass_on(0)], [None] * chunks
    for h in range(halves):
        def kernel(*refs, h=h):
            rest = refs[2 + sets_k : 4 + sets_k]
            xs = refs[4 + sets_k :]
            halo_kernel(h, halves, counts, *refs[:2], refs[2 : 2 + sets_k], *rest, xs[:parts], xs[parts:])

        operands = [*edges_j, *edges_k, near[h], open_cells, *local[h * parts : (h + 1) * parts]]
        first = len(operands) - parts
        x += call(kernel, operands, [part] * parts, "halo", {first + i: i for i in range(parts)})
        for c in range(h * parts, (h + 1) * parts):
            def kernel(inverse_ref, coupling_ref, *refs, c=c):
                forward_kernel(c, parts, 0, count, inverse_ref, coupling_ref, None, None, None, *refs)

            x[c], send = call(kernel, [inverse, coupling, x[c]], [part, face_code], "forward", {2: 0})
            face[c] = hop_pair(send, 0, 1)
        if h:
            far.append(pass_on(h, send))

    for hop in range(1, count):
        for c in range(chunks):
            kernel = functools.partial(forward_kernel, c, parts, hop, count)
            operands = [inverse, coupling, open_cells, far[c // parts], face[c], x[c]]
            x[c], send = call(kernel, operands, [part, face_code], "forward", {5: 0})
            face[c] = hop_pair(send, hop, hop + 1) if hop < count - 1 else hop_pair(send, hop, hop - 1)
    for hop in reversed(range(1, count - 1)):
        for c in range(chunks):
            kernel = functools.partial(backward_kernel, c, hop)
            x[c], send = call(kernel, [inverse, coupling, face[c], x[c]], [part, face_code], "backward", {3: 0})
            face[c] = hop_pair(send, hop, hop - 1)
    for c in range(chunks - 1):
        def kernel(*refs, c=c):
            backward_kernel(c, 0, *refs, None)

        (x[c],) = call(kernel, [inverse, coupling, face[c], x[c]], [part], "backward", {3: 0})
    return call(functools.partial(final_kernel, chunks - 1), [inverse, coupling, face[-1], *x], [full], "last")[0]


def solution(mesh):
    return jax.shard_map(
        shards,
        mesh=mesh,
        in_specs=(
            P("ia", None, "ja", "ka"),
            P("ia", None, None, "ja", "ka"),
            P("ia", None, "ja", "ka"),
            P("ia", "ja", "ka"),
        ),
        out_specs=P("ia", None, "ja", "ka"),
        check_vma=False,
    )
```

```python
import functools

import jax
import jax.numpy as jnp
from jax import lax
from jax.experimental import pallas as pl
from jax.experimental.pallas import tpu as pltpu
from jax.sharding import PartitionSpec as P

advection = 0.012
viscosity = 0.006
damping = 0.003

CENTRE = -1.5 * advection - 6.0 * viscosity - 18.0 * damping
BEHIND_1 = 2.0 * advection + viscosity + 4.0 * damping
BEHIND_2 = -0.5 * advection - damping
NEAR = viscosity + 4.0 * damping
FAR = -damping

LANES = 128
TOP = 32767.0
VMEM = pltpu.VMEM
CHUNKS = 2
HALO_CHUNKS = 2


def scale_of(code):
    return jnp.exp2(code.astype(jnp.float32) * (1.0 / 256.0))


def put_coded(blocks, most, out_ref, rows):
    code = jnp.ceil(256.0 * jnp.log2(jnp.maximum(most, 1e-30))).astype(jnp.int32)
    factor = TOP / scale_of(code)
    for index, block in enumerate(blocks):
        coded = jnp.floor(block() * factor + 0.5)
        coded = jnp.minimum(jnp.maximum(coded, -TOP), TOP).astype(jnp.int32)
        out_ref[index * rows : (index + 1) * rows, :] = coded.astype(jnp.int16)
    count = len(blocks)
    out_ref[count * rows : (count + 1) * rows, :] = code.astype(jnp.int16)


def get_scale(coded_ref, count, rows):
    code = coded_ref[count * rows : (count + 1) * rows, :].astype(jnp.int32)
    return scale_of(code) * (1.0 / TOP)


def get_coded(coded_ref, index, rows, scale):
    return coded_ref[index * rows : (index + 1) * rows, :].astype(jnp.int32).astype(jnp.float32) * scale


def encode_kernel(start, width, state_ref, out_ref):
    planes, nv, rows, _ = state_ref.shape
    places = [
        (p, v, start + b * LANES) for p in range(planes) for v in range(nv) for b in range(width // LANES)
    ]
    most = None
    for p, v, at in places:
        size = jnp.abs(state_ref[p, v, :, at : at + LANES])
        most = size if most is None else jnp.maximum(most, size)
    blocks = [(lambda p=p, v=v, at=at: state_ref[p, v, :, at : at + LANES]) for p, v, at in places]
    put_coded(blocks, most, out_ref, rows)


def edges_kernel(both_k, state_ref, after_ref, j_first, j_second, *edges_k):
    planes, nv, rows, columns = state_ref.shape

    def rows_for(next_ref, previous_ref):
        for p in range(planes):
            for v in range(nv):
                end = rows - 1
                next_ref[p, v, 0:1, :] = NEAR * state_ref[p, v, end:rows, :] + FAR * state_ref[p, v, end - 1 : end, :]
                next_ref[p, v, 1:2, :] = FAR * state_ref[p, v, end:rows, :]
                previous_ref[p, v, 0:1, :] = FAR * state_ref[p, v, 0:1, :]
                previous_ref[p, v, 1:2, :] = NEAR * state_ref[p, v, 0:1, :] + FAR * state_ref[p, v, 1:2, :]

    even_j = lax.axis_index("ja") % 2 == 0
    pl.when(even_j)(lambda: rows_for(j_first, j_second))
    pl.when(jnp.logical_not(even_j))(lambda: rows_for(j_second, j_first))

    lane = lax.broadcasted_iota(jnp.int32, (rows, LANES), 1)

    def columns_for_next(out_ref):
        for p in range(planes):
            for v in range(nv):
                block = state_ref[p, v, :, columns - LANES :]
                one, two = pltpu.roll(block, 1, 1), pltpu.roll(block, 2, 1)
                out_ref[p, v] = jnp.where(lane < 1, NEAR * one, 0.0) + jnp.where(lane < 2, FAR * two, 0.0)

    def columns_for_previous(out_ref):
        for p in range(planes):
            for v in range(nv):
                block = state_ref[p, v, :, :LANES]
                one, two = pltpu.roll(block, LANES - 1, 1), pltpu.roll(block, LANES - 2, 1)
                out_ref[p, v] = jnp.where(lane > LANES - 2, NEAR * one, 0.0) + jnp.where(lane > LANES - 3, FAR * two, 0.0)

    even_k = lax.axis_index("ka") % 2 == 0

    @pl.when(even_k)
    def _():
        columns_for_next(edges_k[0])
        if both_k:
            columns_for_previous(edges_k[1])

    @pl.when(jnp.logical_not(even_k))
    def _():
        columns_for_previous(edges_k[0])
        if both_k:
            columns_for_next(edges_k[1])


def local_kernel(state_ref, wall_ref, *refs):
    x_outs, open_ref, rows_pad = refs[:-2], refs[-2], refs[-1]
    open_ref[...] = 1.0 - wall_ref[...].astype(jnp.float32)
    planes, nv, rows, columns = state_ref.shape
    width = columns // len(x_outs)
    nothing = jnp.zeros((rows, LANES), jnp.float32)
    rows_pad[0:8, :] = jnp.zeros((8, width), jnp.float32)
    rows_pad[8 + rows :, :] = jnp.zeros((8, width), jnp.float32)
    for chunk, x_out in enumerate(x_outs):
        start, stop = chunk * width, (chunk + 1) * width
        for v in range(nv):
            here = [state_ref[p, v, :, start:stop] for p in range(planes)]
            for p in range(planes):
                total = CENTRE * here[p]
                for shift, factor in ((-2, BEHIND_2), (-1, BEHIND_1), (1, NEAR), (2, FAR)):
                    if 0 <= p + shift < planes:
                        total += factor * here[p + shift]
                rows_pad[8 : 8 + rows, :] = here[p]
                total += NEAR * (rows_pad[7 : 7 + rows, :] + rows_pad[9 : 9 + rows, :])
                total += FAR * (rows_pad[6 : 6 + rows, :] + rows_pad[10 : 10 + rows, :])
                left = nothing if start == 0 else state_ref[p, v, :, start - LANES : start]
                right = nothing if stop == columns else state_ref[p, v, :, stop : stop + LANES]
                wide = jnp.concatenate([left, here[p], right], axis=1)
                span = wide.shape[1]
                one = pltpu.roll(wide, 1, 1) + pltpu.roll(wide, span - 1, 1)
                two = pltpu.roll(wide, 2, 1) + pltpu.roll(wide, span - 2, 1)
                total += (NEAR * one + FAR * two)[:, LANES : LANES + width]
                x_out[p, v] = total


def terms_ahead(planes, p):
    found = [(p + shift - planes, factor) for shift, factor in ((1, NEAR), (2, FAR))]
    return [(q, factor) for q, factor in found if q >= 0]


def terms_behind(planes, p):
    found = [(planes + p - shift, factor) for shift, factor in ((1, BEHIND_1), (2, BEHIND_2))]
    return [(q, factor) for q, factor in found if q < planes]


def halo_kernel(half, halves, counts, j_first, j_second, edges_k, neighbour, open_ref, x_ins, x_outs):
    planes, nv, rows, width = x_outs[0].shape
    per = width // LANES
    parts = len(x_outs)
    start = half * parts * width
    place_i, place_j, place_k = (lax.axis_index(name) for name in ("ia", "ja", "ka"))
    count_i, count_j, count_k = counts
    scale = get_scale(neighbour, planes * nv * per * parts, rows)
    even_i = place_i % 2 == 0

    def with_planes(terms_of):
        for p in range(planes):
            for v in range(nv):
                for block in range(per * parts):
                    own = slice(block % per * LANES, (block % per + 1) * LANES)
                    total = x_ins[block // per][p, v, :, own]
                    for q, factor in terms_of(planes, p):
                        total += factor * get_coded(neighbour, (q * nv + v) * per * parts + block, rows, scale)
                    x_outs[block // per][p, v, :, own] = total

    takes_ahead = jnp.logical_and(even_i, place_i + 1 < count_i)
    takes_behind = jnp.logical_not(even_i)
    pl.when(takes_ahead)(lambda: with_planes(terms_ahead))
    pl.when(takes_behind)(lambda: with_planes(terms_behind))
    if count_i % 2:
        pl.when(place_i == count_i - 1)(lambda: with_planes(lambda planes, p: []))

    even_j = place_j % 2 == 0
    odd_j = jnp.logical_not(even_j)
    from_next = place_j + 1 < count_j
    from_previous = place_j > 0

    def add_rows(ref, low):
        at = 0 if low else rows - 2
        for p in range(planes):
            for v in range(nv):
                for part, x_out in enumerate(x_outs):
                    first = start + part * width
                    x_out[p, v, at : at + 2, :] += ref[p, v, :, first : first + width]

    pl.when(jnp.logical_and(even_j, from_next))(lambda: add_rows(j_first, False))
    pl.when(jnp.logical_and(even_j, from_previous))(lambda: add_rows(j_second, True))
    pl.when(odd_j)(lambda: add_rows(j_first, True))
    pl.when(jnp.logical_and(odd_j, from_next))(lambda: add_rows(j_second, False))

    even_k = place_k % 2 == 0
    odd_k = jnp.logical_not(even_k)

    def add_columns(ref, low):
        at = 0 if low else width - LANES
        x_out = x_outs[0 if low else -1]
        for p in range(planes):
            for v in range(nv):
                x_out[p, v, :, at : at + LANES] += ref[p, v]

    if half == 0:
        pl.when(odd_k)(lambda: add_columns(edges_k[0], True))
        if len(edges_k) > 1:
            pl.when(jnp.logical_and(even_k, place_k > 0))(lambda: add_columns(edges_k[1], True))
    if half == halves - 1:
        pl.when(jnp.logical_and(even_k, place_k + 1 < count_k))(lambda: add_columns(edges_k[0], False))
        if len(edges_k) > 1:
            pl.when(jnp.logical_and(odd_k, place_k + 1 < count_k))(lambda: add_columns(edges_k[1], False))

    for p in range(planes):
        for part, x_out in enumerate(x_outs):
            first = start + part * width
            open_cells = open_ref[p, :, first : first + width]
            for v in range(nv):
                x_out[p, v] = open_cells * x_out[p, v]


def apply_block(inverse_ref, p, at, vector):
    result = []
    for a in range(len(vector)):
        total = None
        for b in range(len(vector)):
            term = inverse_ref[p, a, b, :, at : at + LANES].astype(jnp.float32) * vector[b]
            total = term if total is None else total + term
        result.append(total)
    return result


def forward_part(chunk, parts, hop, count, inverse_ref, coupling_ref, open_ref, neighbour, face, x_in, x_out, send):
    planes, nv, rows, width = x_out.shape
    per = width // LANES
    first = hop == 0
    terms_of = None
    if not first:
        face_scale = get_scale(face, nv * per, rows)
        if hop % 2 == 0:
            terms_of = terms_behind
        elif hop < count - 1:
            terms_of = terms_ahead
    if terms_of is not None:
        scale = get_scale(neighbour, planes * nv * per * parts, rows)
    skip = chunk % parts * per
    most = None
    for block in range(per):
        own = slice(block * LANES, (block + 1) * LANES)
        at = chunk * width + block * LANES
        running = None
        if not first:
            running = [get_coded(face, v * per + block, rows, face_scale) for v in range(nv)]
        for p in range(planes):
            factor = coupling_ref[p, 0, :, at : at + LANES]
            if terms_of is not None:
                open_cells = open_ref[p, :, at : at + LANES]
            right = []
            for v in range(nv):
                entry = x_in[p, v, :, own]
                if terms_of is not None:
                    extra = None
                    for q, weight in terms_of(planes, p):
                        term = weight * get_coded(neighbour, (q * nv + v) * per * parts + skip + block, rows, scale)
                        extra = term if extra is None else extra + term
                    if extra is not None:
                        entry += open_cells * extra
                if running is not None:
                    entry += factor * running[v]
                right.append(entry)
            running = apply_block(inverse_ref, p, at, right)
            for v in range(nv):
                x_out[p, v, :, own] = running[v]
        for v in range(nv):
            size = jnp.abs(running[v])
            most = size if most is None else jnp.maximum(most, size)
    if send is not None:
        put_face(planes - 1, most, x_out, send)


def put_face(plane, most, x_out, send):
    nv, rows, width = x_out.shape[1:]
    blocks = [
        (lambda v=v, at=b * LANES: x_out[plane, v, :, at : at + LANES])
        for v in range(nv)
        for b in range(width // LANES)
    ]
    put_coded(blocks, most, send, rows)


def backward_part(chunk, last, inverse_ref, coupling_ref, face, x_in, x_out, send):
    planes, nv, rows, width = x_out.shape
    per = width // LANES
    if not last:
        scale = get_scale(face, nv * per, rows)
    most = None
    for block in range(per):
        own = slice(block * LANES, (block + 1) * LANES)
        at = chunk * width + block * LANES
        running = None
        if not last:
            running = [get_coded(face, v * per + block, rows, scale) for v in range(nv)]
        for p in reversed(range(planes)):
            base = [x_in[p, v, :, own] for v in range(nv)]
            if running is None:
                running = base
            else:
                factor = coupling_ref[p, 1, :, at : at + LANES]
                change = apply_block(inverse_ref, p, at, [factor * running[v] for v in range(nv)])
                running = [base[v] + change[v] for v in range(nv)]
            for v in range(nv):
                x_out[p, v, :, own] = running[v]
        for v in range(nv):
            size = jnp.abs(running[v])
            most = size if most is None else jnp.maximum(most, size)
    if send is not None:
        put_face(0, most, x_out, send)


def forward_kernel(chunk, parts, hop, count, inverse_ref, coupling_ref, open_ref, neighbour, face, x_in, x_out, send):
    active = lax.axis_index("ia") == hop
    last = hop == count - 1

    @pl.when(active)
    def _():
        forward_part(
            chunk, parts, hop, count, inverse_ref, coupling_ref, open_ref, neighbour, face, x_in, x_out,
            None if last else send,
        )
        if last:
            backward_part(chunk, True, inverse_ref, coupling_ref, None, x_out, x_out, send)

    @pl.when(jnp.logical_not(active))
    def _():
        x_out[...] = x_in[...]


def backward_kernel(chunk, hop, inverse_ref, coupling_ref, face, x_in, x_out, send):
    active = lax.axis_index("ia") == hop

    @pl.when(active)
    def _():
        backward_part(chunk, False, inverse_ref, coupling_ref, face, x_in, x_out, send)

    @pl.when(jnp.logical_not(active))
    def _():
        x_out[...] = x_in[...]


def first_kernel(chunk, parts, count, inverse_ref, coupling_ref, *refs):
    forward_kernel(chunk, parts, 0, count, inverse_ref, coupling_ref, None, None, None, *refs)


def unsent_kernel(chunk, *refs):
    backward_kernel(chunk, 0, *refs, None)


def final_kernel(chunk, inverse_ref, coupling_ref, face, *refs):
    parts, out = refs[:-1], refs[-1]
    width = parts[0].shape[3]
    mine = out.at[:, :, :, chunk * width : (chunk + 1) * width]
    active = lax.axis_index("ia") == 0

    @pl.when(active)
    def _():
        backward_part(chunk, False, inverse_ref, coupling_ref, face, parts[chunk], mine, None)

    @pl.when(jnp.logical_not(active))
    def _():
        mine[...] = parts[chunk][...]

    for other, part in enumerate(parts):
        if other != chunk:
            out[:, :, :, other * width : (other + 1) * width] = part[...]


def whole():
    return pl.BlockSpec(memory_space=VMEM)


def call(kernel, operands, outs, name, alias=None, scratch=(), cost=None):
    return pl.pallas_call(
        kernel,
        in_specs=[whole()] * len(operands),
        out_specs=[whole()] * len(outs),
        out_shape=outs,
        scratch_shapes=list(scratch),
        input_output_aliases=alias or {},
        compiler_params=pltpu.CompilerParams(vmem_limit_bytes=12 * 2**20),
        cost_estimate=cost,
        name=name,
    )(*operands)


def swaps(count, first):
    if count % 2 == 0:
        return [(i, (i + 1 if i % 2 == first else i - 1) % count) for i in range(count)]
    partner = list(range(count))
    for i in range(first, count - 1, 2):
        partner[i], partner[i + 1] = i + 1, i
    return list(enumerate(partner))


def shards(state, inverse, coupling, wall):
    planes, nv, rows, columns = state.shape
    chunks, halves = CHUNKS, HALO_CHUNKS
    parts = chunks // halves
    width = columns // chunks
    per = width // LANES
    counts = count, count_j, count_k = [lax.axis_size(name) for name in ("ia", "ja", "ka")]
    sets_k = 1 if count_k == 2 else 2

    halo_code = jax.ShapeDtypeStruct(((planes * nv * per * parts + 1) * rows, LANES), jnp.int16)
    face_code = jax.ShapeDtypeStruct(((nv * per + 1) * rows, LANES), jnp.int16)
    full = jax.ShapeDtypeStruct(state.shape, jnp.float32)
    part = jax.ShapeDtypeStruct((planes, nv, rows, width), jnp.float32)
    edge_j = jax.ShapeDtypeStruct((planes, nv, 2, columns), jnp.float32)
    edge_k = jax.ShapeDtypeStruct((planes, nv, rows, LANES), jnp.float32)
    cells = jax.ShapeDtypeStruct((planes, rows, columns), jnp.float32)

    coded = []
    for h in range(halves):
        kernel = functools.partial(encode_kernel, h * parts * width, parts * width)
        coded += call(kernel, [state], [halo_code], "encode")
    near = [lax.ppermute(coded[h], "ia", swaps(count, 0)) for h in range(halves)]
    made = call(
        functools.partial(edges_kernel, sets_k == 2), [state, coded[-1]], [edge_j] * 2 + [edge_k] * sets_k, "edges"
    )
    edges_j, edges_k = made[:2], made[2:]
    edges_k = [lax.ppermute(edge, "ka", swaps(count_k, s)) for s, edge in enumerate(edges_k)]
    edges_j = [lax.ppermute(edge, "ja", swaps(count_j, s)) for s, edge in enumerate(edges_j)]
    size = state.size
    *local, open_cells = call(
        local_kernel,
        [state, wall],
        [part] * chunks + [cells],
        "local",
        None,
        [VMEM((rows + 16, width), jnp.float32)],
        pl.CostEstimate(flops=40 * size, bytes_accessed=10 * size, transcendentals=0),
    )

    def hop_pair(value, source, target):
        return lax.ppermute(value, "ia", swaps(count, min(source, target) % 2))

    def pass_on(h, *gate):
        passed = near[h] if count == 4 else coded[h]
        if gate:
            passed = lax.optimization_barrier((passed, *gate))[0]
        return lax.ppermute(passed, "ia", [(i, i ^ 2) for i in range(4)] if count == 4 else swaps(count, 1))

    last_step = 2 * count - 2
    x, sent, face, far = list(local), {}, [None] * chunks, [pass_on(0, open_cells)]

    def halo(h):
        def kernel(*refs):
            rest = refs[2 + sets_k : 4 + sets_k]
            xs = refs[4 + sets_k :]
            halo_kernel(h, halves, counts, *refs[:2], refs[2 : 2 + sets_k], *rest, xs[:parts], xs[parts:])

        own = slice(h * parts, (h + 1) * parts)
        operands = [*edges_j, *edges_k, near[h], open_cells, *x[own]]
        first = len(operands) - parts
        x[own] = call(kernel, operands, [part] * parts, "halo", {first + i: i for i in range(parts)})

    def step(c, k):
        hop = min(k, last_step - k)
        forward = k < count
        gate = sent.get((c - 1, k + 1))
        entry = x[c] if gate is None else lax.optimization_barrier((x[c], gate))[0]
        if k == 0:
            kernel = functools.partial(first_kernel, c, parts, count)
            operands = [inverse, coupling, entry]
        elif forward:
            kernel = functools.partial(forward_kernel, c, parts, hop, count)
            operands = [inverse, coupling, open_cells, far[c // parts], face[c], entry]
        elif k < last_step:
            kernel = functools.partial(backward_kernel, c, hop)
            operands = [inverse, coupling, face[c], entry]
        else:
            kernel = functools.partial(unsent_kernel, c)
            operands = [inverse, coupling, face[c], entry]
        alias = {len(operands) - 1: 0}
        name = "forward" if forward else "backward"
        if k == last_step:
            (x[c],) = call(kernel, operands, [part], name, alias)
            return
        x[c], sent[c, k] = call(kernel, operands, [part, face_code], name, alias)
        face[c] = hop_pair(sent[c, k], hop, hop + 1 if k < count - 1 else hop - 1)

    halo(0)
    step(0, 0)
    for h in range(1, halves):
        far.append(pass_on(h, sent[0, 0]))
        halo(h)
    for turn in range(1, last_step + chunks):
        for c in range(chunks):
            if 0 <= turn - c <= last_step and (c, turn - c) != (chunks - 1, last_step):
                step(c, turn - c)
    return call(functools.partial(final_kernel, chunks - 1), [inverse, coupling, face[-1], *x], [full], "last")[0]


def solution(mesh):
    return jax.shard_map(
        shards,
        mesh=mesh,
        in_specs=(
            P("ia", None, "ja", "ka"),
            P("ia", None, None, "ja", "ka"),
            P("ia", None, "ja", "ka"),
            P("ia", "ja", "ka"),
        ),
        out_specs=P("ia", None, "ja", "ka"),
        check_vma=False,
    )
```

```python
import functools

import jax
import jax.numpy as jnp
from jax import lax
from jax.experimental import pallas as pl
from jax.experimental.pallas import tpu as pltpu
from jax.sharding import PartitionSpec as P

advection = 0.012
viscosity = 0.006
damping = 0.003

CENTRE = -1.5 * advection - 6.0 * viscosity - 18.0 * damping
BEHIND_1 = 2.0 * advection + viscosity + 4.0 * damping
BEHIND_2 = -0.5 * advection - damping
NEAR = viscosity + 4.0 * damping
FAR = -damping

LANES = 128
TOP = 32767.0
VMEM = pltpu.VMEM
CHUNKS = 2
HALO_CHUNKS = 2


def scale_of(code):
    return jnp.exp2(code.astype(jnp.float32) * (1.0 / 256.0))


def put_coded(blocks, most, out_ref, rows):
    code = jnp.ceil(256.0 * jnp.log2(jnp.maximum(most, 1e-30))).astype(jnp.int32)
    factor = TOP / scale_of(code)
    for index, block in enumerate(blocks):
        coded = jnp.floor(block() * factor + 0.5)
        coded = jnp.minimum(jnp.maximum(coded, -TOP), TOP).astype(jnp.int32)
        out_ref[index * rows : (index + 1) * rows, :] = coded.astype(jnp.int16)
    count = len(blocks)
    out_ref[count * rows : (count + 1) * rows, :] = code.astype(jnp.int16)


def get_scale(coded_ref, count, rows):
    code = coded_ref[count * rows : (count + 1) * rows, :].astype(jnp.int32)
    return scale_of(code) * (1.0 / TOP)


def get_coded(coded_ref, index, rows, scale):
    return coded_ref[index * rows : (index + 1) * rows, :].astype(jnp.int32).astype(jnp.float32) * scale


def encode_kernel(start, width, state_ref, out_ref):
    planes, nv, rows, _ = state_ref.shape
    places = [
        (p, v, start + b * LANES) for p in range(planes) for v in range(nv) for b in range(width // LANES)
    ]
    most = None
    for p, v, at in places:
        size = jnp.abs(state_ref[p, v, :, at : at + LANES])
        most = size if most is None else jnp.maximum(most, size)
    blocks = [(lambda p=p, v=v, at=at: state_ref[p, v, :, at : at + LANES]) for p, v, at in places]
    put_coded(blocks, most, out_ref, rows)


def edges_kernel(both_k, state_ref, after_ref, j_first, j_second, *edges_k):
    planes, nv, rows, columns = state_ref.shape

    def rows_for(next_ref, previous_ref):
        for p in range(planes):
            for v in range(nv):
                end = rows - 1
                next_ref[p, v, 0:1, :] = NEAR * state_ref[p, v, end:rows, :] + FAR * state_ref[p, v, end - 1 : end, :]
                next_ref[p, v, 1:2, :] = FAR * state_ref[p, v, end:rows, :]
                previous_ref[p, v, 0:1, :] = FAR * state_ref[p, v, 0:1, :]
                previous_ref[p, v, 1:2, :] = NEAR * state_ref[p, v, 0:1, :] + FAR * state_ref[p, v, 1:2, :]

    even_j = lax.axis_index("ja") % 2 == 0
    pl.when(even_j)(lambda: rows_for(j_first, j_second))
    pl.when(jnp.logical_not(even_j))(lambda: rows_for(j_second, j_first))

    lane = lax.broadcasted_iota(jnp.int32, (rows, LANES), 1)

    def columns_for_next(out_ref):
        for p in range(planes):
            for v in range(nv):
                block = state_ref[p, v, :, columns - LANES :]
                one, two = pltpu.roll(block, 1, 1), pltpu.roll(block, 2, 1)
                out_ref[p, v] = jnp.where(lane < 1, NEAR * one, 0.0) + jnp.where(lane < 2, FAR * two, 0.0)

    def columns_for_previous(out_ref):
        for p in range(planes):
            for v in range(nv):
                block = state_ref[p, v, :, :LANES]
                one, two = pltpu.roll(block, LANES - 1, 1), pltpu.roll(block, LANES - 2, 1)
                out_ref[p, v] = jnp.where(lane > LANES - 2, NEAR * one, 0.0) + jnp.where(lane > LANES - 3, FAR * two, 0.0)

    even_k = lax.axis_index("ka") % 2 == 0

    @pl.when(even_k)
    def _():
        columns_for_next(edges_k[0])
        if both_k:
            columns_for_previous(edges_k[1])

    @pl.when(jnp.logical_not(even_k))
    def _():
        columns_for_previous(edges_k[0])
        if both_k:
            columns_for_next(edges_k[1])


def local_kernel(state_ref, wall_ref, *refs):
    x_outs, open_ref, rows_pad = refs[:-2], refs[-2], refs[-1]
    open_ref[...] = 1.0 - wall_ref[...].astype(jnp.float32)
    planes, nv, rows, columns = state_ref.shape
    width = columns // len(x_outs)
    nothing = jnp.zeros((rows, LANES), jnp.float32)
    rows_pad[0:8, :] = jnp.zeros((8, width), jnp.float32)
    rows_pad[8 + rows :, :] = jnp.zeros((8, width), jnp.float32)
    for chunk, x_out in enumerate(x_outs):
        start, stop = chunk * width, (chunk + 1) * width
        for v in range(nv):
            here = [state_ref[p, v, :, start:stop] for p in range(planes)]
            for p in range(planes):
                total = CENTRE * here[p]
                for shift, factor in ((-2, BEHIND_2), (-1, BEHIND_1), (1, NEAR), (2, FAR)):
                    if 0 <= p + shift < planes:
                        total += factor * here[p + shift]
                rows_pad[8 : 8 + rows, :] = here[p]
                total += NEAR * (rows_pad[7 : 7 + rows, :] + rows_pad[9 : 9 + rows, :])
                total += FAR * (rows_pad[6 : 6 + rows, :] + rows_pad[10 : 10 + rows, :])
                left = nothing if start == 0 else state_ref[p, v, :, start - LANES : start]
                right = nothing if stop == columns else state_ref[p, v, :, stop : stop + LANES]
                wide = jnp.concatenate([left, here[p], right], axis=1)
                span = wide.shape[1]
                one = pltpu.roll(wide, 1, 1) + pltpu.roll(wide, span - 1, 1)
                two = pltpu.roll(wide, 2, 1) + pltpu.roll(wide, span - 2, 1)
                total += (NEAR * one + FAR * two)[:, LANES : LANES + width]
                x_out[p, v] = total


def terms_ahead(planes, p):
    found = [(p + shift - planes, factor) for shift, factor in ((1, NEAR), (2, FAR))]
    return [(q, factor) for q, factor in found if q >= 0]


def terms_behind(planes, p):
    found = [(planes + p - shift, factor) for shift, factor in ((1, BEHIND_1), (2, BEHIND_2))]
    return [(q, factor) for q, factor in found if q < planes]


def halo_kernel(half, halves, counts, j_first, j_second, edges_k, neighbour, open_ref, x_ins, x_outs):
    planes, nv, rows, width = x_outs[0].shape
    per = width // LANES
    parts = len(x_outs)
    start = half * parts * width
    place_i, place_j, place_k = (lax.axis_index(name) for name in ("ia", "ja", "ka"))
    count_i, count_j, count_k = counts
    scale = get_scale(neighbour, planes * nv * per * parts, rows)
    even_i = place_i % 2 == 0

    def with_planes(terms_of):
        for p in range(planes):
            for v in range(nv):
                for block in range(per * parts):
                    own = slice(block % per * LANES, (block % per + 1) * LANES)
                    total = x_ins[block // per][p, v, :, own]
                    for q, factor in terms_of(planes, p):
                        total += factor * get_coded(neighbour, (q * nv + v) * per * parts + block, rows, scale)
                    x_outs[block // per][p, v, :, own] = total

    takes_ahead = jnp.logical_and(even_i, place_i + 1 < count_i)
    takes_behind = jnp.logical_not(even_i)
    pl.when(takes_ahead)(lambda: with_planes(terms_ahead))
    pl.when(takes_behind)(lambda: with_planes(terms_behind))
    if count_i % 2:
        pl.when(place_i == count_i - 1)(lambda: with_planes(lambda planes, p: []))

    even_j = place_j % 2 == 0
    odd_j = jnp.logical_not(even_j)
    from_next = place_j + 1 < count_j
    from_previous = place_j > 0

    def add_rows(ref, low):
        at = 0 if low else rows - 2
        for p in range(planes):
            for v in range(nv):
                for part, x_out in enumerate(x_outs):
                    first = start + part * width
                    x_out[p, v, at : at + 2, :] += ref[p, v, :, first : first + width]

    pl.when(jnp.logical_and(even_j, from_next))(lambda: add_rows(j_first, False))
    pl.when(jnp.logical_and(even_j, from_previous))(lambda: add_rows(j_second, True))
    pl.when(odd_j)(lambda: add_rows(j_first, True))
    pl.when(jnp.logical_and(odd_j, from_next))(lambda: add_rows(j_second, False))

    even_k = place_k % 2 == 0
    odd_k = jnp.logical_not(even_k)

    def add_columns(ref, low):
        at = 0 if low else width - LANES
        x_out = x_outs[0 if low else -1]
        for p in range(planes):
            for v in range(nv):
                x_out[p, v, :, at : at + LANES] += ref[p, v]

    if half == 0:
        pl.when(odd_k)(lambda: add_columns(edges_k[0], True))
        if len(edges_k) > 1:
            pl.when(jnp.logical_and(even_k, place_k > 0))(lambda: add_columns(edges_k[1], True))
    if half == halves - 1:
        pl.when(jnp.logical_and(even_k, place_k + 1 < count_k))(lambda: add_columns(edges_k[0], False))
        if len(edges_k) > 1:
            pl.when(jnp.logical_and(odd_k, place_k + 1 < count_k))(lambda: add_columns(edges_k[1], False))

    for p in range(planes):
        for part, x_out in enumerate(x_outs):
            first = start + part * width
            open_cells = open_ref[p, :, first : first + width]
            for v in range(nv):
                x_out[p, v] = open_cells * x_out[p, v]


def apply_block(inverse_ref, p, at, vector):
    result = []
    for a in range(len(vector)):
        total = None
        for b in range(len(vector)):
            term = inverse_ref[p, a, b, :, at : at + LANES].astype(jnp.float32) * vector[b]
            total = term if total is None else total + term
        result.append(total)
    return result


def forward_part(chunk, parts, hop, count, inverse_ref, coupling_ref, open_ref, neighbour, face, x_in, x_out, send):
    planes, nv, rows, width = x_out.shape
    per = width // LANES
    first = hop == 0
    terms_of = None
    if not first:
        face_scale = get_scale(face, nv * per, rows)
        if hop % 2 == 0:
            terms_of = terms_behind
        elif hop < count - 1:
            terms_of = terms_ahead
    if terms_of is not None:
        scale = get_scale(neighbour, planes * nv * per * parts, rows)
    skip = chunk % parts * per
    most = None
    for block in range(per):
        own = slice(block * LANES, (block + 1) * LANES)
        at = chunk * width + block * LANES
        running = None
        if not first:
            running = [get_coded(face, v * per + block, rows, face_scale) for v in range(nv)]
        for p in range(planes):
            factor = coupling_ref[p, 0, :, at : at + LANES]
            if terms_of is not None:
                open_cells = open_ref[p, :, at : at + LANES]
            right = []
            for v in range(nv):
                entry = x_in[p, v, :, own]
                if terms_of is not None:
                    extra = None
                    for q, weight in terms_of(planes, p):
                        term = weight * get_coded(neighbour, (q * nv + v) * per * parts + skip + block, rows, scale)
                        extra = term if extra is None else extra + term
                    if extra is not None:
                        entry += open_cells * extra
                if running is not None:
                    entry += factor * running[v]
                right.append(entry)
            running = apply_block(inverse_ref, p, at, right)
            for v in range(nv):
                x_out[p, v, :, own] = running[v]
        for v in range(nv):
            size = jnp.abs(running[v])
            most = size if most is None else jnp.maximum(most, size)
    if send is not None:
        put_face(planes - 1, most, x_out, send)


def put_face(plane, most, x_out, send):
    nv, rows, width = x_out.shape[1:]
    blocks = [
        (lambda v=v, at=b * LANES: x_out[plane, v, :, at : at + LANES])
        for v in range(nv)
        for b in range(width // LANES)
    ]
    put_coded(blocks, most, send, rows)


def backward_part(chunk, last, inverse_ref, coupling_ref, face, x_in, x_out, send):
    planes, nv, rows, width = x_out.shape
    per = width // LANES
    if not last:
        scale = get_scale(face, nv * per, rows)
    most = None
    for block in range(per):
        own = slice(block * LANES, (block + 1) * LANES)
        at = chunk * width + block * LANES
        running = None
        if not last:
            running = [get_coded(face, v * per + block, rows, scale) for v in range(nv)]
        for p in reversed(range(planes)):
            base = [x_in[p, v, :, own] for v in range(nv)]
            if running is None:
                running = base
            else:
                factor = coupling_ref[p, 1, :, at : at + LANES]
                change = apply_block(inverse_ref, p, at, [factor * running[v] for v in range(nv)])
                running = [base[v] + change[v] for v in range(nv)]
            for v in range(nv):
                x_out[p, v, :, own] = running[v]
        for v in range(nv):
            size = jnp.abs(running[v])
            most = size if most is None else jnp.maximum(most, size)
    if send is not None:
        put_face(0, most, x_out, send)


def forward_kernel(chunk, parts, hop, count, inverse_ref, coupling_ref, open_ref, neighbour, face, x_in, x_out, send):
    active = lax.axis_index("ia") == hop
    last = hop == count - 1

    @pl.when(active)
    def _():
        forward_part(
            chunk, parts, hop, count, inverse_ref, coupling_ref, open_ref, neighbour, face, x_in, x_out,
            None if last else send,
        )
        if last:
            backward_part(chunk, True, inverse_ref, coupling_ref, None, x_out, x_out, send)

    @pl.when(jnp.logical_not(active))
    def _():
        x_out[...] = x_in[...]


def backward_kernel(chunk, hop, inverse_ref, coupling_ref, face, x_in, x_out, send):
    active = lax.axis_index("ia") == hop

    @pl.when(active)
    def _():
        backward_part(chunk, False, inverse_ref, coupling_ref, face, x_in, x_out, send)

    @pl.when(jnp.logical_not(active))
    def _():
        x_out[...] = x_in[...]


def first_kernel(chunk, parts, count, inverse_ref, coupling_ref, *refs):
    forward_kernel(chunk, parts, 0, count, inverse_ref, coupling_ref, None, None, None, *refs)


def unsent_kernel(chunk, *refs):
    backward_kernel(chunk, 0, *refs, None)


def final_kernel(chunk, inverse_ref, coupling_ref, face, *refs):
    parts, out = refs[:-1], refs[-1]
    width = parts[0].shape[3]
    mine = out.at[:, :, :, chunk * width : (chunk + 1) * width]
    active = lax.axis_index("ia") == 0

    @pl.when(active)
    def _():
        backward_part(chunk, False, inverse_ref, coupling_ref, face, parts[chunk], mine, None)

    @pl.when(jnp.logical_not(active))
    def _():
        mine[...] = parts[chunk][...]

    for other, part in enumerate(parts):
        if other != chunk:
            out[:, :, :, other * width : (other + 1) * width] = part[...]


def whole():
    return pl.BlockSpec(memory_space=VMEM)


def call(kernel, operands, outs, name, alias=None, scratch=(), cost=None):
    return pl.pallas_call(
        kernel,
        in_specs=[whole()] * len(operands),
        out_specs=[whole()] * len(outs),
        out_shape=outs,
        scratch_shapes=list(scratch),
        input_output_aliases=alias or {},
        compiler_params=pltpu.CompilerParams(vmem_limit_bytes=12 * 2**20),
        cost_estimate=cost,
        name=name,
    )(*operands)


def swaps(count, first):
    if count % 2 == 0:
        return [(i, (i + 1 if i % 2 == first else i - 1) % count) for i in range(count)]
    partner = list(range(count))
    for i in range(first, count - 1, 2):
        partner[i], partner[i + 1] = i + 1, i
    return list(enumerate(partner))


def shards(state, inverse, coupling, wall):
    planes, nv, rows, columns = state.shape
    chunks, halves = CHUNKS, HALO_CHUNKS
    parts = chunks // halves
    width = columns // chunks
    per = width // LANES
    counts = count, count_j, count_k = [lax.axis_size(name) for name in ("ia", "ja", "ka")]
    sets_k = 1 if count_k == 2 else 2

    halo_code = jax.ShapeDtypeStruct(((planes * nv * per * parts + 1) * rows, LANES), jnp.int16)
    face_code = jax.ShapeDtypeStruct(((nv * per + 1) * rows, LANES), jnp.int16)
    full = jax.ShapeDtypeStruct(state.shape, jnp.float32)
    part = jax.ShapeDtypeStruct((planes, nv, rows, width), jnp.float32)
    edge_j = jax.ShapeDtypeStruct((planes, nv, 2, columns), jnp.float32)
    edge_k = jax.ShapeDtypeStruct((planes, nv, rows, LANES), jnp.float32)
    cells = jax.ShapeDtypeStruct((planes, rows, columns), jnp.float32)

    coded = []
    for h in range(halves):
        kernel = functools.partial(encode_kernel, h * parts * width, parts * width)
        coded += call(kernel, [state], [halo_code], "encode")
    near = [lax.ppermute(coded[h], "ia", swaps(count, 0)) for h in range(halves)]
    made = call(
        functools.partial(edges_kernel, sets_k == 2), [state, coded[-1]], [edge_j] * 2 + [edge_k] * sets_k, "edges"
    )
    edges_j, edges_k = made[:2], made[2:]
    edges_k = [lax.ppermute(edge, "ka", swaps(count_k, s)) for s, edge in enumerate(edges_k)]
    edges_j = [lax.ppermute(edge, "ja", swaps(count_j, s)) for s, edge in enumerate(edges_j)]
    size = state.size
    *local, open_cells = call(
        local_kernel,
        [state, wall],
        [part] * chunks + [cells],
        "local",
        None,
        [VMEM((rows + 16, width), jnp.float32)],
        pl.CostEstimate(flops=40 * size, bytes_accessed=10 * size, transcendentals=0),
    )

    def hop_pair(value, source, target):
        return lax.ppermute(value, "ia", [(source, target)])

    def pass_on(h, *gate):
        passed = near[h] if count == 4 else coded[h]
        if gate:
            passed = lax.optimization_barrier((passed, *gate))[0]
        return lax.ppermute(passed, "ia", [(i, i ^ 2) for i in range(4)] if count == 4 else swaps(count, 1))

    last_step = 2 * count - 2
    x, sent, face, far = list(local), {}, [None] * chunks, [pass_on(0, open_cells)]

    def halo(h):
        def kernel(*refs):
            rest = refs[2 + sets_k : 4 + sets_k]
            xs = refs[4 + sets_k :]
            halo_kernel(h, halves, counts, *refs[:2], refs[2 : 2 + sets_k], *rest, xs[:parts], xs[parts:])

        own = slice(h * parts, (h + 1) * parts)
        operands = [*edges_j, *edges_k, near[h], open_cells, *x[own]]
        first = len(operands) - parts
        x[own] = call(kernel, operands, [part] * parts, "halo", {first + i: i for i in range(parts)})

    def step(c, k):
        hop = min(k, last_step - k)
        forward = k < count
        gate = sent.get((c - 1, 0)) if k == 0 else None
        entry = x[c] if gate is None else lax.optimization_barrier((x[c], gate))[0]
        if k == 0:
            kernel = functools.partial(first_kernel, c, parts, count)
            operands = [inverse, coupling, entry]
        elif forward:
            kernel = functools.partial(forward_kernel, c, parts, hop, count)
            operands = [inverse, coupling, open_cells, far[c // parts], face[c], entry]
        elif k < last_step:
            kernel = functools.partial(backward_kernel, c, hop)
            operands = [inverse, coupling, face[c], entry]
        else:
            kernel = functools.partial(unsent_kernel, c)
            operands = [inverse, coupling, face[c], entry]
        alias = {len(operands) - 1: 0}
        name = "forward" if forward else "backward"
        if k == last_step:
            (x[c],) = call(kernel, operands, [part], name, alias)
            return
        x[c], sent[c, k] = call(kernel, operands, [part, face_code], name, alias)
        face[c] = hop_pair(sent[c, k], hop, hop + 1 if k < count - 1 else hop - 1)

    halo(0)
    for h in range(1, halves):
        far.append(pass_on(h, x[0]))
        halo(h)
    for k in range(last_step + 1):
        for c in range(chunks):
            if (c, k) != (chunks - 1, last_step):
                step(c, k)
    return call(functools.partial(final_kernel, chunks - 1), [inverse, coupling, face[-1], *x], [full], "last")[0]


def solution(mesh):
    return jax.shard_map(
        shards,
        mesh=mesh,
        in_specs=(
            P("ia", None, "ja", "ka"),
            P("ia", None, None, "ja", "ka"),
            P("ia", None, "ja", "ka"),
            P("ia", "ja", "ka"),
        ),
        out_specs=P("ia", None, "ja", "ka"),
        check_vma=False,
    )
```

```python
import functools

import jax
import jax.numpy as jnp
from jax import lax
from jax.experimental import pallas as pl
from jax.experimental.pallas import tpu as pltpu
from jax.sharding import PartitionSpec as P

advection = 0.012
viscosity = 0.006
damping = 0.003

CENTRE = -1.5 * advection - 6.0 * viscosity - 18.0 * damping
BEHIND_1 = 2.0 * advection + viscosity + 4.0 * damping
BEHIND_2 = -0.5 * advection - damping
NEAR = viscosity + 4.0 * damping
FAR = -damping

LANES = 128
TOP = 32767.0
VMEM = pltpu.VMEM
CHUNKS = 2
HALO_CHUNKS = 2


def scale_of(code):
    return jnp.exp2(code.astype(jnp.float32) * (1.0 / 256.0))


def put_coded(blocks, most, out_ref, rows):
    code = jnp.ceil(256.0 * jnp.log2(jnp.maximum(most, 1e-30))).astype(jnp.int32)
    factor = TOP / scale_of(code)
    for index, block in enumerate(blocks):
        coded = jnp.floor(block() * factor + 0.5)
        coded = jnp.minimum(jnp.maximum(coded, -TOP), TOP).astype(jnp.int32)
        out_ref[index * rows : (index + 1) * rows, :] = coded.astype(jnp.int16)
    count = len(blocks)
    out_ref[count * rows : (count + 1) * rows, :] = code.astype(jnp.int16)


def get_scale(coded_ref, count, rows):
    code = coded_ref[count * rows : (count + 1) * rows, :].astype(jnp.int32)
    return scale_of(code) * (1.0 / TOP)


def get_coded(coded_ref, index, rows, scale):
    return coded_ref[index * rows : (index + 1) * rows, :].astype(jnp.int32).astype(jnp.float32) * scale


def encode_kernel(start, width, state_ref, out_ref):
    planes, nv, rows, _ = state_ref.shape
    places = [
        (p, v, start + b * LANES) for p in range(planes) for v in range(nv) for b in range(width // LANES)
    ]
    most = None
    for p, v, at in places:
        size = jnp.abs(state_ref[p, v, :, at : at + LANES])
        most = size if most is None else jnp.maximum(most, size)
    blocks = [(lambda p=p, v=v, at=at: state_ref[p, v, :, at : at + LANES]) for p, v, at in places]
    put_coded(blocks, most, out_ref, rows)


def edges_kernel(both_k, state_ref, after_ref, j_first, j_second, *edges_k):
    planes, nv, rows, columns = state_ref.shape

    def rows_for(next_ref, previous_ref):
        for p in range(planes):
            for v in range(nv):
                end = rows - 1
                next_ref[p, v, 0:1, :] = NEAR * state_ref[p, v, end:rows, :] + FAR * state_ref[p, v, end - 1 : end, :]
                next_ref[p, v, 1:2, :] = FAR * state_ref[p, v, end:rows, :]
                previous_ref[p, v, 0:1, :] = FAR * state_ref[p, v, 0:1, :]
                previous_ref[p, v, 1:2, :] = NEAR * state_ref[p, v, 0:1, :] + FAR * state_ref[p, v, 1:2, :]

    even_j = lax.axis_index("ja") % 2 == 0
    pl.when(even_j)(lambda: rows_for(j_first, j_second))
    pl.when(jnp.logical_not(even_j))(lambda: rows_for(j_second, j_first))

    lane = lax.broadcasted_iota(jnp.int32, (rows, LANES), 1)

    def columns_for_next(out_ref):
        for p in range(planes):
            for v in range(nv):
                block = state_ref[p, v, :, columns - LANES :]
                one, two = pltpu.roll(block, 1, 1), pltpu.roll(block, 2, 1)
                out_ref[p, v] = jnp.where(lane < 1, NEAR * one, 0.0) + jnp.where(lane < 2, FAR * two, 0.0)

    def columns_for_previous(out_ref):
        for p in range(planes):
            for v in range(nv):
                block = state_ref[p, v, :, :LANES]
                one, two = pltpu.roll(block, LANES - 1, 1), pltpu.roll(block, LANES - 2, 1)
                out_ref[p, v] = jnp.where(lane > LANES - 2, NEAR * one, 0.0) + jnp.where(lane > LANES - 3, FAR * two, 0.0)

    even_k = lax.axis_index("ka") % 2 == 0

    @pl.when(even_k)
    def _():
        columns_for_next(edges_k[0])
        if both_k:
            columns_for_previous(edges_k[1])

    @pl.when(jnp.logical_not(even_k))
    def _():
        columns_for_previous(edges_k[0])
        if both_k:
            columns_for_next(edges_k[1])


def local_kernel(state_ref, wall_ref, *refs):
    x_outs, open_ref, rows_pad = refs[:-2], refs[-2], refs[-1]
    open_ref[...] = 1.0 - wall_ref[...].astype(jnp.float32)
    planes, nv, rows, columns = state_ref.shape
    width = columns // len(x_outs)
    nothing = jnp.zeros((rows, LANES), jnp.float32)
    rows_pad[0:8, :] = jnp.zeros((8, width), jnp.float32)
    rows_pad[8 + rows :, :] = jnp.zeros((8, width), jnp.float32)
    for chunk, x_out in enumerate(x_outs):
        start, stop = chunk * width, (chunk + 1) * width
        for v in range(nv):
            here = [state_ref[p, v, :, start:stop] for p in range(planes)]
            for p in range(planes):
                total = CENTRE * here[p]
                for shift, factor in ((-2, BEHIND_2), (-1, BEHIND_1), (1, NEAR), (2, FAR)):
                    if 0 <= p + shift < planes:
                        total += factor * here[p + shift]
                rows_pad[8 : 8 + rows, :] = here[p]
                total += NEAR * (rows_pad[7 : 7 + rows, :] + rows_pad[9 : 9 + rows, :])
                total += FAR * (rows_pad[6 : 6 + rows, :] + rows_pad[10 : 10 + rows, :])
                left = nothing if start == 0 else state_ref[p, v, :, start - LANES : start]
                right = nothing if stop == columns else state_ref[p, v, :, stop : stop + LANES]
                wide = jnp.concatenate([left, here[p], right], axis=1)
                span = wide.shape[1]
                one = pltpu.roll(wide, 1, 1) + pltpu.roll(wide, span - 1, 1)
                two = pltpu.roll(wide, 2, 1) + pltpu.roll(wide, span - 2, 1)
                total += (NEAR * one + FAR * two)[:, LANES : LANES + width]
                x_out[p, v] = total


def terms_ahead(planes, p):
    found = [(p + shift - planes, factor) for shift, factor in ((1, NEAR), (2, FAR))]
    return [(q, factor) for q, factor in found if q >= 0]


def terms_behind(planes, p):
    found = [(planes + p - shift, factor) for shift, factor in ((1, BEHIND_1), (2, BEHIND_2))]
    return [(q, factor) for q, factor in found if q < planes]


def halo_kernel(half, halves, counts, j_first, j_second, edges_k, neighbour, open_ref, x_ins, x_outs):
    planes, nv, rows, width = x_outs[0].shape
    per = width // LANES
    parts = len(x_outs)
    start = half * parts * width
    place_i, place_j, place_k = (lax.axis_index(name) for name in ("ia", "ja", "ka"))
    count_i, count_j, count_k = counts
    scale = get_scale(neighbour, planes * nv * per * parts, rows)
    even_i = place_i % 2 == 0

    def with_planes(terms_of):
        for p in range(planes):
            for v in range(nv):
                for block in range(per * parts):
                    own = slice(block % per * LANES, (block % per + 1) * LANES)
                    total = x_ins[block // per][p, v, :, own]
                    for q, factor in terms_of(planes, p):
                        total += factor * get_coded(neighbour, (q * nv + v) * per * parts + block, rows, scale)
                    x_outs[block // per][p, v, :, own] = total

    takes_ahead = jnp.logical_and(even_i, place_i + 1 < count_i)
    takes_behind = jnp.logical_not(even_i)
    pl.when(takes_ahead)(lambda: with_planes(terms_ahead))
    pl.when(takes_behind)(lambda: with_planes(terms_behind))
    if count_i % 2:
        pl.when(place_i == count_i - 1)(lambda: with_planes(lambda planes, p: []))

    even_j = place_j % 2 == 0
    odd_j = jnp.logical_not(even_j)
    from_next = place_j + 1 < count_j
    from_previous = place_j > 0

    def add_rows(ref, low):
        at = 0 if low else rows - 2
        for p in range(planes):
            for v in range(nv):
                for part, x_out in enumerate(x_outs):
                    first = start + part * width
                    x_out[p, v, at : at + 2, :] += ref[p, v, :, first : first + width]

    pl.when(jnp.logical_and(even_j, from_next))(lambda: add_rows(j_first, False))
    pl.when(jnp.logical_and(even_j, from_previous))(lambda: add_rows(j_second, True))
    pl.when(odd_j)(lambda: add_rows(j_first, True))
    pl.when(jnp.logical_and(odd_j, from_next))(lambda: add_rows(j_second, False))

    even_k = place_k % 2 == 0
    odd_k = jnp.logical_not(even_k)

    def add_columns(ref, low):
        at = 0 if low else width - LANES
        x_out = x_outs[0 if low else -1]
        for p in range(planes):
            for v in range(nv):
                x_out[p, v, :, at : at + LANES] += ref[p, v]

    if half == 0:
        pl.when(odd_k)(lambda: add_columns(edges_k[0], True))
        if len(edges_k) > 1:
            pl.when(jnp.logical_and(even_k, place_k > 0))(lambda: add_columns(edges_k[1], True))
    if half == halves - 1:
        pl.when(jnp.logical_and(even_k, place_k + 1 < count_k))(lambda: add_columns(edges_k[0], False))
        if len(edges_k) > 1:
            pl.when(jnp.logical_and(odd_k, place_k + 1 < count_k))(lambda: add_columns(edges_k[1], False))

    for p in range(planes):
        for part, x_out in enumerate(x_outs):
            first = start + part * width
            open_cells = open_ref[p, :, first : first + width]
            for v in range(nv):
                x_out[p, v] = open_cells * x_out[p, v]


def apply_block(inverse_ref, p, at, vector):
    result = []
    for a in range(len(vector)):
        total = None
        for b in range(len(vector)):
            term = inverse_ref[p, a, b, :, at : at + LANES].astype(jnp.float32) * vector[b]
            total = term if total is None else total + term
        result.append(total)
    return result


def forward_part(chunk, parts, hop, count, inverse_ref, coupling_ref, open_ref, neighbour, face, x_in, x_out, send):
    planes, nv, rows, width = x_out.shape
    per = width // LANES
    first = hop == 0
    terms_of = None
    if not first:
        face_scale = get_scale(face, nv * per, rows)
        if hop % 2 == 0:
            terms_of = terms_behind
        elif hop < count - 1:
            terms_of = terms_ahead
    if terms_of is not None:
        scale = get_scale(neighbour, planes * nv * per * parts, rows)
    skip = chunk % parts * per
    most = None
    for block in range(per):
        own = slice(block * LANES, (block + 1) * LANES)
        at = chunk * width + block * LANES
        running = None
        if not first:
            running = [get_coded(face, v * per + block, rows, face_scale) for v in range(nv)]
        for p in range(planes):
            factor = coupling_ref[p, 0, :, at : at + LANES]
            if terms_of is not None:
                open_cells = open_ref[p, :, at : at + LANES]
            right = []
            for v in range(nv):
                entry = x_in[p, v, :, own]
                if terms_of is not None:
                    extra = None
                    for q, weight in terms_of(planes, p):
                        term = weight * get_coded(neighbour, (q * nv + v) * per * parts + skip + block, rows, scale)
                        extra = term if extra is None else extra + term
                    if extra is not None:
                        entry += open_cells * extra
                if running is not None:
                    entry += factor * running[v]
                right.append(entry)
            running = apply_block(inverse_ref, p, at, right)
            for v in range(nv):
                x_out[p, v, :, own] = running[v]
        for v in range(nv):
            size = jnp.abs(running[v])
            most = size if most is None else jnp.maximum(most, size)
    if send is not None:
        put_face(planes - 1, most, x_out, send)


def put_face(plane, most, x_out, send):
    nv, rows, width = x_out.shape[1:]
    blocks = [
        (lambda v=v, at=b * LANES: x_out[plane, v, :, at : at + LANES])
        for v in range(nv)
        for b in range(width // LANES)
    ]
    put_coded(blocks, most, send, rows)


def backward_part(chunk, last, inverse_ref, coupling_ref, face, x_in, x_out, send):
    planes, nv, rows, width = x_out.shape
    per = width // LANES
    if not last:
        scale = get_scale(face, nv * per, rows)
    most = None
    for block in range(per):
        own = slice(block * LANES, (block + 1) * LANES)
        at = chunk * width + block * LANES
        running = None
        if not last:
            running = [get_coded(face, v * per + block, rows, scale) for v in range(nv)]
        for p in reversed(range(planes)):
            base = [x_in[p, v, :, own] for v in range(nv)]
            if running is None:
                running = base
            else:
                factor = coupling_ref[p, 1, :, at : at + LANES]
                change = apply_block(inverse_ref, p, at, [factor * running[v] for v in range(nv)])
                running = [base[v] + change[v] for v in range(nv)]
            for v in range(nv):
                x_out[p, v, :, own] = running[v]
        for v in range(nv):
            size = jnp.abs(running[v])
            most = size if most is None else jnp.maximum(most, size)
    if send is not None:
        put_face(0, most, x_out, send)


def forward_kernel(chunk, parts, hop, count, inverse_ref, coupling_ref, open_ref, neighbour, face, x_in, x_out, send):
    active = lax.axis_index("ia") == hop
    last = hop == count - 1

    @pl.when(active)
    def _():
        forward_part(
            chunk, parts, hop, count, inverse_ref, coupling_ref, open_ref, neighbour, face, x_in, x_out,
            None if last else send,
        )
        if last:
            backward_part(chunk, True, inverse_ref, coupling_ref, None, x_out, x_out, send)

    @pl.when(jnp.logical_not(active))
    def _():
        x_out[...] = x_in[...]


def backward_kernel(chunk, hop, inverse_ref, coupling_ref, face, x_in, x_out, send):
    active = lax.axis_index("ia") == hop

    @pl.when(active)
    def _():
        backward_part(chunk, False, inverse_ref, coupling_ref, face, x_in, x_out, send)

    @pl.when(jnp.logical_not(active))
    def _():
        x_out[...] = x_in[...]


def first_kernel(chunk, parts, count, inverse_ref, coupling_ref, *refs):
    forward_kernel(chunk, parts, 0, count, inverse_ref, coupling_ref, None, None, None, *refs)


def unsent_kernel(chunk, *refs):
    backward_kernel(chunk, 0, *refs, None)


def final_kernel(chunk, inverse_ref, coupling_ref, face, *refs):
    parts, out = refs[:-1], refs[-1]
    width = parts[0].shape[3]
    mine = out.at[:, :, :, chunk * width : (chunk + 1) * width]
    active = lax.axis_index("ia") == 0

    @pl.when(active)
    def _():
        backward_part(chunk, False, inverse_ref, coupling_ref, face, parts[chunk], mine, None)

    @pl.when(jnp.logical_not(active))
    def _():
        mine[...] = parts[chunk][...]

    for other, part in enumerate(parts):
        if other != chunk:
            out[:, :, :, other * width : (other + 1) * width] = part[...]


def whole():
    return pl.BlockSpec(memory_space=VMEM)


def call(kernel, operands, outs, name, alias=None, scratch=(), cost=None):
    return pl.pallas_call(
        kernel,
        in_specs=[whole()] * len(operands),
        out_specs=[whole()] * len(outs),
        out_shape=outs,
        scratch_shapes=list(scratch),
        input_output_aliases=alias or {},
        compiler_params=pltpu.CompilerParams(vmem_limit_bytes=12 * 2**20),
        cost_estimate=cost,
        name=name,
    )(*operands)


def swaps(count, first):
    if count % 2 == 0:
        return [(i, (i + 1 if i % 2 == first else i - 1) % count) for i in range(count)]
    partner = list(range(count))
    for i in range(first, count - 1, 2):
        partner[i], partner[i + 1] = i + 1, i
    return list(enumerate(partner))


def shards(state, inverse, coupling, wall):
    planes, nv, rows, columns = state.shape
    chunks, halves = CHUNKS, HALO_CHUNKS
    parts = chunks // halves
    width = columns // chunks
    per = width // LANES
    counts = count, count_j, count_k = [lax.axis_size(name) for name in ("ia", "ja", "ka")]
    sets_k = 1 if count_k == 2 else 2

    halo_code = jax.ShapeDtypeStruct(((planes * nv * per * parts + 1) * rows, LANES), jnp.int16)
    face_code = jax.ShapeDtypeStruct(((nv * per + 1) * rows, LANES), jnp.int16)
    full = jax.ShapeDtypeStruct(state.shape, jnp.float32)
    part = jax.ShapeDtypeStruct((planes, nv, rows, width), jnp.float32)
    edge_j = jax.ShapeDtypeStruct((planes, nv, 2, columns), jnp.float32)
    edge_k = jax.ShapeDtypeStruct((planes, nv, rows, LANES), jnp.float32)
    cells = jax.ShapeDtypeStruct((planes, rows, columns), jnp.float32)

    coded = []
    for h in range(halves):
        kernel = functools.partial(encode_kernel, h * parts * width, parts * width)
        coded += call(kernel, [state], [halo_code], "encode")
    near = [lax.ppermute(coded[h], "ia", swaps(count, 0)) for h in range(halves)]
    made = call(
        functools.partial(edges_kernel, sets_k == 2), [state, coded[-1]], [edge_j] * 2 + [edge_k] * sets_k, "edges"
    )
    edges_j, edges_k = made[:2], made[2:]
    edges_k = [lax.ppermute(edge, "ka", swaps(count_k, s)) for s, edge in enumerate(edges_k)]
    edges_j = [lax.ppermute(edge, "ja", swaps(count_j, s)) for s, edge in enumerate(edges_j)]
    size = state.size
    *local, open_cells = call(
        local_kernel,
        [state, wall],
        [part] * chunks + [cells],
        "local",
        None,
        [VMEM((rows + 16, width), jnp.float32)],
        pl.CostEstimate(flops=40 * size, bytes_accessed=10 * size, transcendentals=0),
    )

    def hop_pair(value, source, target):
        exchange = min(source, target) % 2 == 0 and count % 2 == 0
        return lax.ppermute(value, "ia", swaps(count, 0) if exchange else [(source, target)])

    def pass_on(h, *gate):
        passed = near[h] if count == 4 else coded[h]
        if gate:
            passed = lax.optimization_barrier((passed, *gate))[0]
        return lax.ppermute(passed, "ia", [(i, i ^ 2) for i in range(4)] if count == 4 else swaps(count, 1))

    last_step = 2 * count - 2
    x, sent, face, far = list(local), {}, [None] * chunks, [pass_on(0, open_cells)]

    def halo(h):
        def kernel(*refs):
            rest = refs[2 + sets_k : 4 + sets_k]
            xs = refs[4 + sets_k :]
            halo_kernel(h, halves, counts, *refs[:2], refs[2 : 2 + sets_k], *rest, xs[:parts], xs[parts:])

        own = slice(h * parts, (h + 1) * parts)
        operands = [*edges_j, *edges_k, near[h], open_cells, *x[own]]
        first = len(operands) - parts
        x[own] = call(kernel, operands, [part] * parts, "halo", {first + i: i for i in range(parts)})

    def step(c, k):
        hop = min(k, last_step - k)
        forward = k < count
        gate = sent.get((c - 1, 0)) if k == 0 else None
        entry = x[c] if gate is None else lax.optimization_barrier((x[c], gate))[0]
        if k == 0:
            kernel = functools.partial(first_kernel, c, parts, count)
            operands = [inverse, coupling, entry]
        elif forward:
            kernel = functools.partial(forward_kernel, c, parts, hop, count)
            operands = [inverse, coupling, open_cells, far[c // parts], face[c], entry]
        elif k < last_step:
            kernel = functools.partial(backward_kernel, c, hop)
            operands = [inverse, coupling, face[c], entry]
        else:
            kernel = functools.partial(unsent_kernel, c)
            operands = [inverse, coupling, face[c], entry]
        alias = {len(operands) - 1: 0}
        name = "forward" if forward else "backward"
        if k == last_step:
            (x[c],) = call(kernel, operands, [part], name, alias)
            return
        x[c], sent[c, k] = call(kernel, operands, [part, face_code], name, alias)
        face[c] = hop_pair(sent[c, k], hop, hop + 1 if k < count - 1 else hop - 1)

    halo(0)
    step(0, 0)
    for h in range(1, halves):
        far.append(pass_on(h, sent[0, 0]))
        halo(h)
    for k in range(last_step + 1):
        for c in range(chunks):
            if (c, k) not in ((0, 0), (chunks - 1, last_step)):
                step(c, k)
    return call(functools.partial(final_kernel, chunks - 1), [inverse, coupling, face[-1], *x], [full], "last")[0]


def solution(mesh):
    return jax.shard_map(
        shards,
        mesh=mesh,
        in_specs=(
            P("ia", None, "ja", "ka"),
            P("ia", None, None, "ja", "ka"),
            P("ia", None, "ja", "ka"),
            P("ia", "ja", "ka"),
        ),
        out_specs=P("ia", None, "ja", "ka"),
        check_vma=False,
    )
```

```python
import functools

import jax
import jax.numpy as jnp
from jax import lax
from jax.experimental import pallas as pl
from jax.experimental.pallas import tpu as pltpu
from jax.sharding import PartitionSpec as P

advection = 0.012
viscosity = 0.006
damping = 0.003

CENTRE = -1.5 * advection - 6.0 * viscosity - 18.0 * damping
BEHIND_1 = 2.0 * advection + viscosity + 4.0 * damping
BEHIND_2 = -0.5 * advection - damping
NEAR = viscosity + 4.0 * damping
FAR = -damping

LANES = 128
TOP = 32767.0
VMEM = pltpu.VMEM
CHUNKS = 2
HALO_CHUNKS = 2


def scale_of(code):
    return jnp.exp2(code.astype(jnp.float32) * (1.0 / 256.0))


def put_coded(blocks, most, out_ref, rows):
    code = jnp.ceil(256.0 * jnp.log2(jnp.maximum(most, 1e-30))).astype(jnp.int32)
    factor = TOP / scale_of(code)
    for index, block in enumerate(blocks):
        coded = jnp.floor(block() * factor + 0.5)
        coded = jnp.minimum(jnp.maximum(coded, -TOP), TOP).astype(jnp.int32)
        out_ref[index * rows : (index + 1) * rows, :] = coded.astype(jnp.int16)
    count = len(blocks)
    out_ref[count * rows : (count + 1) * rows, :] = code.astype(jnp.int16)


def get_scale(coded_ref, count, rows):
    code = coded_ref[count * rows : (count + 1) * rows, :].astype(jnp.int32)
    return scale_of(code) * (1.0 / TOP)


def get_coded(coded_ref, index, rows, scale):
    return coded_ref[index * rows : (index + 1) * rows, :].astype(jnp.int32).astype(jnp.float32) * scale


def encode_kernel(start, width, state_ref, out_ref):
    planes, nv, rows, _ = state_ref.shape
    places = [
        (p, v, start + b * LANES) for p in range(planes) for v in range(nv) for b in range(width // LANES)
    ]
    most = None
    for p, v, at in places:
        size = jnp.abs(state_ref[p, v, :, at : at + LANES])
        most = size if most is None else jnp.maximum(most, size)
    blocks = [(lambda p=p, v=v, at=at: state_ref[p, v, :, at : at + LANES]) for p, v, at in places]
    put_coded(blocks, most, out_ref, rows)


def edges_kernel(both_k, state_ref, after_ref, j_first, j_second, *edges_k):
    planes, nv, rows, columns = state_ref.shape

    def rows_for(next_ref, previous_ref):
        for p in range(planes):
            for v in range(nv):
                end = rows - 1
                next_ref[p, v, 0:1, :] = NEAR * state_ref[p, v, end:rows, :] + FAR * state_ref[p, v, end - 1 : end, :]
                next_ref[p, v, 1:2, :] = FAR * state_ref[p, v, end:rows, :]
                previous_ref[p, v, 0:1, :] = FAR * state_ref[p, v, 0:1, :]
                previous_ref[p, v, 1:2, :] = NEAR * state_ref[p, v, 0:1, :] + FAR * state_ref[p, v, 1:2, :]

    even_j = lax.axis_index("ja") % 2 == 0
    pl.when(even_j)(lambda: rows_for(j_first, j_second))
    pl.when(jnp.logical_not(even_j))(lambda: rows_for(j_second, j_first))

    lane = lax.broadcasted_iota(jnp.int32, (rows, LANES), 1)

    def columns_for_next(out_ref):
        for p in range(planes):
            for v in range(nv):
                block = state_ref[p, v, :, columns - LANES :]
                one, two = pltpu.roll(block, 1, 1), pltpu.roll(block, 2, 1)
                out_ref[p, v] = jnp.where(lane < 1, NEAR * one, 0.0) + jnp.where(lane < 2, FAR * two, 0.0)

    def columns_for_previous(out_ref):
        for p in range(planes):
            for v in range(nv):
                block = state_ref[p, v, :, :LANES]
                one, two = pltpu.roll(block, LANES - 1, 1), pltpu.roll(block, LANES - 2, 1)
                out_ref[p, v] = jnp.where(lane > LANES - 2, NEAR * one, 0.0) + jnp.where(lane > LANES - 3, FAR * two, 0.0)

    even_k = lax.axis_index("ka") % 2 == 0

    @pl.when(even_k)
    def _():
        columns_for_next(edges_k[0])
        if both_k:
            columns_for_previous(edges_k[1])

    @pl.when(jnp.logical_not(even_k))
    def _():
        columns_for_previous(edges_k[0])
        if both_k:
            columns_for_next(edges_k[1])


def local_kernel(state_ref, wall_ref, *refs):
    x_outs, open_ref, rows_pad = refs[:-2], refs[-2], refs[-1]
    open_ref[...] = 1.0 - wall_ref[...].astype(jnp.float32)
    planes, nv, rows, columns = state_ref.shape
    width = columns // len(x_outs)
    nothing = jnp.zeros((rows, LANES), jnp.float32)
    rows_pad[0:8, :] = jnp.zeros((8, width), jnp.float32)
    rows_pad[8 + rows :, :] = jnp.zeros((8, width), jnp.float32)
    for chunk, x_out in enumerate(x_outs):
        start, stop = chunk * width, (chunk + 1) * width
        for v in range(nv):
            here = [state_ref[p, v, :, start:stop] for p in range(planes)]
            for p in range(planes):
                total = CENTRE * here[p]
                for shift, factor in ((-2, BEHIND_2), (-1, BEHIND_1), (1, NEAR), (2, FAR)):
                    if 0 <= p + shift < planes:
                        total += factor * here[p + shift]
                rows_pad[8 : 8 + rows, :] = here[p]
                total += NEAR * (rows_pad[7 : 7 + rows, :] + rows_pad[9 : 9 + rows, :])
                total += FAR * (rows_pad[6 : 6 + rows, :] + rows_pad[10 : 10 + rows, :])
                left = nothing if start == 0 else state_ref[p, v, :, start - LANES : start]
                right = nothing if stop == columns else state_ref[p, v, :, stop : stop + LANES]
                wide = jnp.concatenate([left, here[p], right], axis=1)
                span = wide.shape[1]
                one = pltpu.roll(wide, 1, 1) + pltpu.roll(wide, span - 1, 1)
                two = pltpu.roll(wide, 2, 1) + pltpu.roll(wide, span - 2, 1)
                total += (NEAR * one + FAR * two)[:, LANES : LANES + width]
                x_out[p, v] = total


def terms_ahead(planes, p):
    found = [(p + shift - planes, factor) for shift, factor in ((1, NEAR), (2, FAR))]
    return [(q, factor) for q, factor in found if q >= 0]


def terms_behind(planes, p):
    found = [(planes + p - shift, factor) for shift, factor in ((1, BEHIND_1), (2, BEHIND_2))]
    return [(q, factor) for q, factor in found if q < planes]


def halo_kernel(half, halves, counts, j_first, j_second, edges_k, neighbour, open_ref, x_ins, x_outs):
    planes, nv, rows, width = x_outs[0].shape
    per = width // LANES
    parts = len(x_outs)
    start = half * parts * width
    place_i, place_j, place_k = (lax.axis_index(name) for name in ("ia", "ja", "ka"))
    count_i, count_j, count_k = counts
    scale = get_scale(neighbour, planes * nv * per * parts, rows)
    even_i = place_i % 2 == 0

    def with_planes(terms_of):
        for p in range(planes):
            for v in range(nv):
                for block in range(per * parts):
                    own = slice(block % per * LANES, (block % per + 1) * LANES)
                    total = x_ins[block // per][p, v, :, own]
                    for q, factor in terms_of(planes, p):
                        total += factor * get_coded(neighbour, (q * nv + v) * per * parts + block, rows, scale)
                    x_outs[block // per][p, v, :, own] = total

    takes_ahead = jnp.logical_and(even_i, place_i + 1 < count_i)
    takes_behind = jnp.logical_not(even_i)
    pl.when(takes_ahead)(lambda: with_planes(terms_ahead))
    pl.when(takes_behind)(lambda: with_planes(terms_behind))
    if count_i % 2:
        pl.when(place_i == count_i - 1)(lambda: with_planes(lambda planes, p: []))

    even_j = place_j % 2 == 0
    odd_j = jnp.logical_not(even_j)
    from_next = place_j + 1 < count_j
    from_previous = place_j > 0

    def add_rows(ref, low):
        at = 0 if low else rows - 2
        for p in range(planes):
            for v in range(nv):
                for part, x_out in enumerate(x_outs):
                    first = start + part * width
                    x_out[p, v, at : at + 2, :] += ref[p, v, :, first : first + width]

    pl.when(jnp.logical_and(even_j, from_next))(lambda: add_rows(j_first, False))
    pl.when(jnp.logical_and(even_j, from_previous))(lambda: add_rows(j_second, True))
    pl.when(odd_j)(lambda: add_rows(j_first, True))
    pl.when(jnp.logical_and(odd_j, from_next))(lambda: add_rows(j_second, False))

    even_k = place_k % 2 == 0
    odd_k = jnp.logical_not(even_k)

    def add_columns(ref, low):
        at = 0 if low else width - LANES
        x_out = x_outs[0 if low else -1]
        for p in range(planes):
            for v in range(nv):
                x_out[p, v, :, at : at + LANES] += ref[p, v]

    if half == 0:
        pl.when(odd_k)(lambda: add_columns(edges_k[0], True))
        if len(edges_k) > 1:
            pl.when(jnp.logical_and(even_k, place_k > 0))(lambda: add_columns(edges_k[1], True))
    if half == halves - 1:
        pl.when(jnp.logical_and(even_k, place_k + 1 < count_k))(lambda: add_columns(edges_k[0], False))
        if len(edges_k) > 1:
            pl.when(jnp.logical_and(odd_k, place_k + 1 < count_k))(lambda: add_columns(edges_k[1], False))

    for p in range(planes):
        for part, x_out in enumerate(x_outs):
            first = start + part * width
            open_cells = open_ref[p, :, first : first + width]
            for v in range(nv):
                x_out[p, v] = open_cells * x_out[p, v]


def apply_block(inverse_ref, p, at, vector):
    result = []
    for a in range(len(vector)):
        total = None
        for b in range(len(vector)):
            term = inverse_ref[p, a, b, :, at : at + LANES].astype(jnp.float32) * vector[b]
            total = term if total is None else total + term
        result.append(total)
    return result


def forward_part(chunk, parts, hop, count, inverse_ref, coupling_ref, open_ref, neighbour, face, x_in, x_out, send):
    planes, nv, rows, width = x_out.shape
    per = width // LANES
    first = hop == 0
    terms_of = None
    if not first:
        face_scale = get_scale(face, nv * per, rows)
        if hop % 2 == 0:
            terms_of = terms_behind
        elif hop < count - 1:
            terms_of = terms_ahead
    if terms_of is not None:
        scale = get_scale(neighbour, planes * nv * per * parts, rows)
    skip = chunk % parts * per
    most = None
    for block in range(per):
        own = slice(block * LANES, (block + 1) * LANES)
        at = chunk * width + block * LANES
        running = None
        if not first:
            running = [get_coded(face, v * per + block, rows, face_scale) for v in range(nv)]
        for p in range(planes):
            factor = coupling_ref[p, 0, :, at : at + LANES]
            if terms_of is not None:
                open_cells = open_ref[p, :, at : at + LANES]
            right = []
            for v in range(nv):
                entry = x_in[p, v, :, own]
                if terms_of is not None:
                    extra = None
                    for q, weight in terms_of(planes, p):
                        term = weight * get_coded(neighbour, (q * nv + v) * per * parts + skip + block, rows, scale)
                        extra = term if extra is None else extra + term
                    if extra is not None:
                        entry += open_cells * extra
                if running is not None:
                    entry += factor * running[v]
                right.append(entry)
            running = apply_block(inverse_ref, p, at, right)
            for v in range(nv):
                x_out[p, v, :, own] = running[v]
        for v in range(nv):
            size = jnp.abs(running[v])
            most = size if most is None else jnp.maximum(most, size)
    if send is not None:
        put_face(planes - 1, most, x_out, send)


def put_face(plane, most, x_out, send):
    nv, rows, width = x_out.shape[1:]
    blocks = [
        (lambda v=v, at=b * LANES: x_out[plane, v, :, at : at + LANES])
        for v in range(nv)
        for b in range(width // LANES)
    ]
    put_coded(blocks, most, send, rows)


def backward_part(chunk, last, inverse_ref, coupling_ref, face, x_in, x_out, send):
    planes, nv, rows, width = x_out.shape
    per = width // LANES
    if not last:
        scale = get_scale(face, nv * per, rows)
    most = None
    for block in range(per):
        own = slice(block * LANES, (block + 1) * LANES)
        at = chunk * width + block * LANES
        running = None
        if not last:
            running = [get_coded(face, v * per + block, rows, scale) for v in range(nv)]
        for p in reversed(range(planes)):
            base = [x_in[p, v, :, own] for v in range(nv)]
            if running is None:
                running = base
            else:
                factor = coupling_ref[p, 1, :, at : at + LANES]
                change = apply_block(inverse_ref, p, at, [factor * running[v] for v in range(nv)])
                running = [base[v] + change[v] for v in range(nv)]
            for v in range(nv):
                x_out[p, v, :, own] = running[v]
        for v in range(nv):
            size = jnp.abs(running[v])
            most = size if most is None else jnp.maximum(most, size)
    if send is not None:
        put_face(0, most, x_out, send)


def forward_kernel(chunk, parts, hop, count, inverse_ref, coupling_ref, open_ref, neighbour, face, x_in, x_out, send):
    active = lax.axis_index("ia") == hop
    last = hop == count - 1

    @pl.when(active)
    def _():
        forward_part(
            chunk, parts, hop, count, inverse_ref, coupling_ref, open_ref, neighbour, face, x_in, x_out,
            None if last else send,
        )
        if last:
            backward_part(chunk, True, inverse_ref, coupling_ref, None, x_out, x_out, send)

    @pl.when(jnp.logical_not(active))
    def _():
        x_out[...] = x_in[...]


def backward_kernel(chunk, hop, inverse_ref, coupling_ref, face, x_in, x_out, send):
    active = lax.axis_index("ia") == hop

    @pl.when(active)
    def _():
        backward_part(chunk, False, inverse_ref, coupling_ref, face, x_in, x_out, send)

    @pl.when(jnp.logical_not(active))
    def _():
        x_out[...] = x_in[...]


def first_kernel(chunk, parts, count, inverse_ref, coupling_ref, *refs):
    forward_kernel(chunk, parts, 0, count, inverse_ref, coupling_ref, None, None, None, *refs)


def unsent_kernel(chunk, *refs):
    backward_kernel(chunk, 0, *refs, None)


def final_kernel(chunk, inverse_ref, coupling_ref, face, *refs):
    parts, out = refs[:-1], refs[-1]
    width = parts[0].shape[3]
    mine = out.at[:, :, :, chunk * width : (chunk + 1) * width]
    active = lax.axis_index("ia") == 0

    @pl.when(active)
    def _():
        backward_part(chunk, False, inverse_ref, coupling_ref, face, parts[chunk], mine, None)

    @pl.when(jnp.logical_not(active))
    def _():
        mine[...] = parts[chunk][...]

    for other, part in enumerate(parts):
        if other != chunk:
            out[:, :, :, other * width : (other + 1) * width] = part[...]


def whole():
    return pl.BlockSpec(memory_space=VMEM)


def call(kernel, operands, outs, name, alias=None, scratch=(), cost=None):
    return pl.pallas_call(
        kernel,
        in_specs=[whole()] * len(operands),
        out_specs=[whole()] * len(outs),
        out_shape=outs,
        scratch_shapes=list(scratch),
        input_output_aliases=alias or {},
        compiler_params=pltpu.CompilerParams(vmem_limit_bytes=12 * 2**20),
        cost_estimate=cost,
        name=name,
    )(*operands)


def swaps(count, first):
    if count % 2 == 0:
        return [(i, (i + 1 if i % 2 == first else i - 1) % count) for i in range(count)]
    partner = list(range(count))
    for i in range(first, count - 1, 2):
        partner[i], partner[i + 1] = i + 1, i
    return list(enumerate(partner))


def shards(state, inverse, coupling, wall):
    planes, nv, rows, columns = state.shape
    chunks, halves = CHUNKS, HALO_CHUNKS
    parts = chunks // halves
    width = columns // chunks
    per = width // LANES
    counts = count, count_j, count_k = [lax.axis_size(name) for name in ("ia", "ja", "ka")]
    sets_k = 1 if count_k == 2 else 2

    halo_code = jax.ShapeDtypeStruct(((planes * nv * per * parts + 1) * rows, LANES), jnp.int16)
    face_code = jax.ShapeDtypeStruct(((nv * per + 1) * rows, LANES), jnp.int16)
    full = jax.ShapeDtypeStruct(state.shape, jnp.float32)
    part = jax.ShapeDtypeStruct((planes, nv, rows, width), jnp.float32)
    edge_j = jax.ShapeDtypeStruct((planes, nv, 2, columns), jnp.float32)
    edge_k = jax.ShapeDtypeStruct((planes, nv, rows, LANES), jnp.float32)
    cells = jax.ShapeDtypeStruct((planes, rows, columns), jnp.float32)

    coded = []
    for h in range(halves):
        kernel = functools.partial(encode_kernel, h * parts * width, parts * width)
        coded += call(kernel, [state], [halo_code], "encode")
    near = [lax.ppermute(coded[h], "ia", swaps(count, 0)) for h in range(halves)]
    made = call(
        functools.partial(edges_kernel, sets_k == 2), [state, coded[-1]], [edge_j] * 2 + [edge_k] * sets_k, "edges"
    )
    edges_j, edges_k = made[:2], made[2:]
    edges_k = [lax.ppermute(edge, "ka", swaps(count_k, s)) for s, edge in enumerate(edges_k)]
    edges_j = [lax.ppermute(edge, "ja", swaps(count_j, s)) for s, edge in enumerate(edges_j)]
    size = state.size
    *local, open_cells = call(
        local_kernel,
        [state, wall],
        [part] * chunks + [cells],
        "local",
        None,
        [VMEM((rows + 16, width), jnp.float32)],
        pl.CostEstimate(flops=40 * size, bytes_accessed=10 * size, transcendentals=0),
    )

    def hop_pair(value, source, target):
        first = min(source, target) % 2
        exchange = count % 2 == 0 and (first == 0 or source < target)
        return lax.ppermute(value, "ia", swaps(count, first) if exchange else [(source, target)])

    def pass_on(h, *gate):
        passed = near[h] if count == 4 else coded[h]
        if gate:
            passed = lax.optimization_barrier((passed, *gate))[0]
        return lax.ppermute(passed, "ia", [(i, i ^ 2) for i in range(4)] if count == 4 else swaps(count, 1))

    last_step = 2 * count - 2
    x, sent, face, far = list(local), {}, [None] * chunks, [pass_on(0, open_cells)]

    def halo(h):
        def kernel(*refs):
            rest = refs[2 + sets_k : 4 + sets_k]
            xs = refs[4 + sets_k :]
            halo_kernel(h, halves, counts, *refs[:2], refs[2 : 2 + sets_k], *rest, xs[:parts], xs[parts:])

        own = slice(h * parts, (h + 1) * parts)
        operands = [*edges_j, *edges_k, near[h], open_cells, *x[own]]
        first = len(operands) - parts
        x[own] = call(kernel, operands, [part] * parts, "halo", {first + i: i for i in range(parts)})

    def step(c, k):
        hop = min(k, last_step - k)
        forward = k < count
        gate = sent.get((c - 1, 0)) if k == 0 else None
        entry = x[c] if gate is None else lax.optimization_barrier((x[c], gate))[0]
        if k == 0:
            kernel = functools.partial(first_kernel, c, parts, count)
            operands = [inverse, coupling, entry]
        elif forward:
            kernel = functools.partial(forward_kernel, c, parts, hop, count)
            operands = [inverse, coupling, open_cells, far[c // parts], face[c], entry]
        elif k < last_step:
            kernel = functools.partial(backward_kernel, c, hop)
            operands = [inverse, coupling, face[c], entry]
        else:
            kernel = functools.partial(unsent_kernel, c)
            operands = [inverse, coupling, face[c], entry]
        alias = {len(operands) - 1: 0}
        name = "forward" if forward else "backward"
        if k == last_step:
            (x[c],) = call(kernel, operands, [part], name, alias)
            return
        x[c], sent[c, k] = call(kernel, operands, [part, face_code], name, alias)
        face[c] = hop_pair(sent[c, k], hop, hop + 1 if k < count - 1 else hop - 1)

    halo(0)
    step(0, 0)
    for h in range(1, halves):
        far.append(pass_on(h, sent[0, 0]))
        halo(h)
    for k in range(last_step + 1):
        for c in range(chunks):
            if (c, k) not in ((0, 0), (chunks - 1, last_step)):
                step(c, k)
    return call(functools.partial(final_kernel, chunks - 1), [inverse, coupling, face[-1], *x], [full], "last")[0]


def solution(mesh):
    return jax.shard_map(
        shards,
        mesh=mesh,
        in_specs=(
            P("ia", None, "ja", "ka"),
            P("ia", None, None, "ja", "ka"),
            P("ia", None, "ja", "ka"),
            P("ia", "ja", "ka"),
        ),
        out_specs=P("ia", None, "ja", "ka"),
        check_vma=False,
    )
```

```python
import functools

import jax
import jax.numpy as jnp
from jax import lax
from jax.experimental import pallas as pl
from jax.experimental.pallas import tpu as pltpu
from jax.sharding import PartitionSpec as P

advection = 0.012
viscosity = 0.006
damping = 0.003

CENTRE = -1.5 * advection - 6.0 * viscosity - 18.0 * damping
BEHIND_1 = 2.0 * advection + viscosity + 4.0 * damping
BEHIND_2 = -0.5 * advection - damping
NEAR = viscosity + 4.0 * damping
FAR = -damping

LANES = 128
TOP = 32767.0
VMEM = pltpu.VMEM
CHUNKS = 2
HALO_CHUNKS = 2


def scale_of(code):
    return jnp.exp2(code.astype(jnp.float32) * (1.0 / 256.0))


def put_coded(blocks, most, out_ref, rows):
    code = jnp.ceil(256.0 * jnp.log2(jnp.maximum(most, 1e-30))).astype(jnp.int32)
    factor = TOP / scale_of(code)
    for index, block in enumerate(blocks):
        coded = jnp.floor(block() * factor + 0.5)
        coded = jnp.minimum(jnp.maximum(coded, -TOP), TOP).astype(jnp.int32)
        out_ref[index * rows : (index + 1) * rows, :] = coded.astype(jnp.int16)
    count = len(blocks)
    out_ref[count * rows : (count + 1) * rows, :] = code.astype(jnp.int16)


def get_scale(coded_ref, count, rows):
    code = coded_ref[count * rows : (count + 1) * rows, :].astype(jnp.int32)
    return scale_of(code) * (1.0 / TOP)


def get_coded(coded_ref, index, rows, scale):
    return coded_ref[index * rows : (index + 1) * rows, :].astype(jnp.int32).astype(jnp.float32) * scale


def encode_kernel(start, width, state_ref, out_ref):
    planes, nv, rows, _ = state_ref.shape
    places = [
        (p, v, start + b * LANES) for p in range(planes) for v in range(nv) for b in range(width // LANES)
    ]
    most = None
    for p, v, at in places:
        size = jnp.abs(state_ref[p, v, :, at : at + LANES])
        most = size if most is None else jnp.maximum(most, size)
    blocks = [(lambda p=p, v=v, at=at: state_ref[p, v, :, at : at + LANES]) for p, v, at in places]
    put_coded(blocks, most, out_ref, rows)


def edges_kernel(both_k, state_ref, after_ref, j_first, j_second, *edges_k):
    planes, nv, rows, columns = state_ref.shape

    def rows_for(next_ref, previous_ref):
        for p in range(planes):
            for v in range(nv):
                end = rows - 1
                next_ref[p, v, 0:1, :] = NEAR * state_ref[p, v, end:rows, :] + FAR * state_ref[p, v, end - 1 : end, :]
                next_ref[p, v, 1:2, :] = FAR * state_ref[p, v, end:rows, :]
                previous_ref[p, v, 0:1, :] = FAR * state_ref[p, v, 0:1, :]
                previous_ref[p, v, 1:2, :] = NEAR * state_ref[p, v, 0:1, :] + FAR * state_ref[p, v, 1:2, :]

    even_j = lax.axis_index("ja") % 2 == 0
    pl.when(even_j)(lambda: rows_for(j_first, j_second))
    pl.when(jnp.logical_not(even_j))(lambda: rows_for(j_second, j_first))

    lane = lax.broadcasted_iota(jnp.int32, (rows, LANES), 1)

    def columns_for_next(out_ref):
        for p in range(planes):
            for v in range(nv):
                block = state_ref[p, v, :, columns - LANES :]
                one, two = pltpu.roll(block, 1, 1), pltpu.roll(block, 2, 1)
                out_ref[p, v] = jnp.where(lane < 1, NEAR * one, 0.0) + jnp.where(lane < 2, FAR * two, 0.0)

    def columns_for_previous(out_ref):
        for p in range(planes):
            for v in range(nv):
                block = state_ref[p, v, :, :LANES]
                one, two = pltpu.roll(block, LANES - 1, 1), pltpu.roll(block, LANES - 2, 1)
                out_ref[p, v] = jnp.where(lane > LANES - 2, NEAR * one, 0.0) + jnp.where(lane > LANES - 3, FAR * two, 0.0)

    even_k = lax.axis_index("ka") % 2 == 0

    @pl.when(even_k)
    def _():
        columns_for_next(edges_k[0])
        if both_k:
            columns_for_previous(edges_k[1])

    @pl.when(jnp.logical_not(even_k))
    def _():
        columns_for_previous(edges_k[0])
        if both_k:
            columns_for_next(edges_k[1])


def local_kernel(state_ref, wall_ref, *refs):
    x_outs, open_ref, rows_pad = refs[:-2], refs[-2], refs[-1]
    open_ref[...] = 1.0 - wall_ref[...].astype(jnp.float32)
    planes, nv, rows, columns = state_ref.shape
    width = columns // len(x_outs)
    nothing = jnp.zeros((rows, LANES), jnp.float32)
    rows_pad[0:8, :] = jnp.zeros((8, width), jnp.float32)
    rows_pad[8 + rows :, :] = jnp.zeros((8, width), jnp.float32)
    for chunk, x_out in enumerate(x_outs):
        start, stop = chunk * width, (chunk + 1) * width
        for v in range(nv):
            here = [state_ref[p, v, :, start:stop] for p in range(planes)]
            for p in range(planes):
                total = CENTRE * here[p]
                for shift, factor in ((-2, BEHIND_2), (-1, BEHIND_1), (1, NEAR), (2, FAR)):
                    if 0 <= p + shift < planes:
                        total += factor * here[p + shift]
                rows_pad[8 : 8 + rows, :] = here[p]
                total += NEAR * (rows_pad[7 : 7 + rows, :] + rows_pad[9 : 9 + rows, :])
                total += FAR * (rows_pad[6 : 6 + rows, :] + rows_pad[10 : 10 + rows, :])
                left = nothing if start == 0 else state_ref[p, v, :, start - LANES : start]
                right = nothing if stop == columns else state_ref[p, v, :, stop : stop + LANES]
                wide = jnp.concatenate([left, here[p], right], axis=1)
                span = wide.shape[1]
                one = pltpu.roll(wide, 1, 1) + pltpu.roll(wide, span - 1, 1)
                two = pltpu.roll(wide, 2, 1) + pltpu.roll(wide, span - 2, 1)
                total += (NEAR * one + FAR * two)[:, LANES : LANES + width]
                x_out[p, v] = total


def terms_ahead(planes, p):
    found = [(p + shift - planes, factor) for shift, factor in ((1, NEAR), (2, FAR))]
    return [(q, factor) for q, factor in found if q >= 0]


def terms_behind(planes, p):
    found = [(planes + p - shift, factor) for shift, factor in ((1, BEHIND_1), (2, BEHIND_2))]
    return [(q, factor) for q, factor in found if q < planes]


def halo_kernel(half, halves, counts, j_first, j_second, edges_k, neighbour, open_ref, x_ins, x_outs):
    planes, nv, rows, width = x_outs[0].shape
    per = width // LANES
    parts = len(x_outs)
    start = half * parts * width
    place_i, place_j, place_k = (lax.axis_index(name) for name in ("ia", "ja", "ka"))
    count_i, count_j, count_k = counts
    scale = get_scale(neighbour, planes * nv * per * parts, rows)
    even_i = place_i % 2 == 0

    def with_planes(terms_of):
        for p in range(planes):
            for v in range(nv):
                for block in range(per * parts):
                    own = slice(block % per * LANES, (block % per + 1) * LANES)
                    total = x_ins[block // per][p, v, :, own]
                    for q, factor in terms_of(planes, p):
                        total += factor * get_coded(neighbour, (q * nv + v) * per * parts + block, rows, scale)
                    x_outs[block // per][p, v, :, own] = total

    takes_ahead = jnp.logical_and(even_i, place_i + 1 < count_i)
    takes_behind = jnp.logical_not(even_i)
    pl.when(takes_ahead)(lambda: with_planes(terms_ahead))
    pl.when(takes_behind)(lambda: with_planes(terms_behind))
    if count_i % 2:
        pl.when(place_i == count_i - 1)(lambda: with_planes(lambda planes, p: []))

    even_j = place_j % 2 == 0
    odd_j = jnp.logical_not(even_j)
    from_next = place_j + 1 < count_j
    from_previous = place_j > 0

    def add_rows(ref, low):
        at = 0 if low else rows - 2
        for p in range(planes):
            for v in range(nv):
                for part, x_out in enumerate(x_outs):
                    first = start + part * width
                    x_out[p, v, at : at + 2, :] += ref[p, v, :, first : first + width]

    pl.when(jnp.logical_and(even_j, from_next))(lambda: add_rows(j_first, False))
    pl.when(jnp.logical_and(even_j, from_previous))(lambda: add_rows(j_second, True))
    pl.when(odd_j)(lambda: add_rows(j_first, True))
    pl.when(jnp.logical_and(odd_j, from_next))(lambda: add_rows(j_second, False))

    even_k = place_k % 2 == 0
    odd_k = jnp.logical_not(even_k)

    def add_columns(ref, low):
        at = 0 if low else width - LANES
        x_out = x_outs[0 if low else -1]
        for p in range(planes):
            for v in range(nv):
                x_out[p, v, :, at : at + LANES] += ref[p, v]

    if half == 0:
        pl.when(odd_k)(lambda: add_columns(edges_k[0], True))
        if len(edges_k) > 1:
            pl.when(jnp.logical_and(even_k, place_k > 0))(lambda: add_columns(edges_k[1], True))
    if half == halves - 1:
        pl.when(jnp.logical_and(even_k, place_k + 1 < count_k))(lambda: add_columns(edges_k[0], False))
        if len(edges_k) > 1:
            pl.when(jnp.logical_and(odd_k, place_k + 1 < count_k))(lambda: add_columns(edges_k[1], False))

    for p in range(planes):
        for part, x_out in enumerate(x_outs):
            first = start + part * width
            open_cells = open_ref[p, :, first : first + width]
            for v in range(nv):
                x_out[p, v] = open_cells * x_out[p, v]


def apply_block(inverse_ref, p, at, vector):
    result = []
    for a in range(len(vector)):
        total = None
        for b in range(len(vector)):
            term = inverse_ref[p, a, b, :, at : at + LANES].astype(jnp.float32) * vector[b]
            total = term if total is None else total + term
        result.append(total)
    return result


def forward_part(chunk, parts, hop, count, inverse_ref, coupling_ref, open_ref, neighbour, face, x_in, x_out, send):
    planes, nv, rows, width = x_out.shape
    per = width // LANES
    first = hop == 0
    terms_of = None
    if not first:
        face_scale = get_scale(face, nv * per, rows)
        if hop % 2 == 0:
            terms_of = terms_behind
        elif hop < count - 1:
            terms_of = terms_ahead
    if terms_of is not None:
        scale = get_scale(neighbour, planes * nv * per * parts, rows)
    skip = chunk % parts * per
    most = None
    for block in range(per):
        own = slice(block * LANES, (block + 1) * LANES)
        at = chunk * width + block * LANES
        running = None
        if not first:
            running = [get_coded(face, v * per + block, rows, face_scale) for v in range(nv)]
        for p in range(planes):
            factor = coupling_ref[p, 0, :, at : at + LANES]
            if terms_of is not None:
                open_cells = open_ref[p, :, at : at + LANES]
            right = []
            for v in range(nv):
                entry = x_in[p, v, :, own]
                if terms_of is not None:
                    extra = None
                    for q, weight in terms_of(planes, p):
                        term = weight * get_coded(neighbour, (q * nv + v) * per * parts + skip + block, rows, scale)
                        extra = term if extra is None else extra + term
                    if extra is not None:
                        entry += open_cells * extra
                if running is not None:
                    entry += factor * running[v]
                right.append(entry)
            running = apply_block(inverse_ref, p, at, right)
            for v in range(nv):
                x_out[p, v, :, own] = running[v]
        for v in range(nv):
            size = jnp.abs(running[v])
            most = size if most is None else jnp.maximum(most, size)
    if send is not None:
        put_face(planes - 1, most, x_out, send)


def put_face(plane, most, x_out, send):
    nv, rows, width = x_out.shape[1:]
    blocks = [
        (lambda v=v, at=b * LANES: x_out[plane, v, :, at : at + LANES])
        for v in range(nv)
        for b in range(width // LANES)
    ]
    put_coded(blocks, most, send, rows)


def backward_part(chunk, last, inverse_ref, coupling_ref, face, x_in, x_out, send):
    planes, nv, rows, width = x_out.shape
    per = width // LANES
    if not last:
        scale = get_scale(face, nv * per, rows)
    most = None
    for block in range(per):
        own = slice(block * LANES, (block + 1) * LANES)
        at = chunk * width + block * LANES
        running = None
        if not last:
            running = [get_coded(face, v * per + block, rows, scale) for v in range(nv)]
        for p in reversed(range(planes)):
            base = [x_in[p, v, :, own] for v in range(nv)]
            if running is None:
                running = base
            else:
                factor = coupling_ref[p, 1, :, at : at + LANES]
                change = apply_block(inverse_ref, p, at, [factor * running[v] for v in range(nv)])
                running = [base[v] + change[v] for v in range(nv)]
            for v in range(nv):
                x_out[p, v, :, own] = running[v]
        for v in range(nv):
            size = jnp.abs(running[v])
            most = size if most is None else jnp.maximum(most, size)
    if send is not None:
        put_face(0, most, x_out, send)


def forward_kernel(chunk, parts, hop, count, inverse_ref, coupling_ref, open_ref, neighbour, face, x_in, x_out, send):
    active = lax.axis_index("ia") == hop
    last = hop == count - 1

    @pl.when(active)
    def _():
        forward_part(
            chunk, parts, hop, count, inverse_ref, coupling_ref, open_ref, neighbour, face, x_in, x_out,
            None if last else send,
        )
        if last:
            backward_part(chunk, True, inverse_ref, coupling_ref, None, x_out, x_out, send)

    @pl.when(jnp.logical_not(active))
    def _():
        x_out[...] = x_in[...]


def backward_kernel(chunk, hop, inverse_ref, coupling_ref, face, x_in, x_out, send):
    active = lax.axis_index("ia") == hop

    @pl.when(active)
    def _():
        backward_part(chunk, False, inverse_ref, coupling_ref, face, x_in, x_out, send)

    @pl.when(jnp.logical_not(active))
    def _():
        x_out[...] = x_in[...]


def final_kernel(chunk, inverse_ref, coupling_ref, face, *refs):
    parts, out = refs[:-1], refs[-1]
    width = parts[0].shape[3]
    mine = out.at[:, :, :, chunk * width : (chunk + 1) * width]
    active = lax.axis_index("ia") == 0

    @pl.when(active)
    def _():
        backward_part(chunk, False, inverse_ref, coupling_ref, face, parts[chunk], mine, None)

    @pl.when(jnp.logical_not(active))
    def _():
        mine[...] = parts[chunk][...]

    for other, part in enumerate(parts):
        if other != chunk:
            out[:, :, :, other * width : (other + 1) * width] = part[...]


def whole():
    return pl.BlockSpec(memory_space=VMEM)


def call(kernel, operands, outs, name, alias=None, scratch=(), cost=None):
    return pl.pallas_call(
        kernel,
        in_specs=[whole()] * len(operands),
        out_specs=[whole()] * len(outs),
        out_shape=outs,
        scratch_shapes=list(scratch),
        input_output_aliases=alias or {},
        compiler_params=pltpu.CompilerParams(vmem_limit_bytes=12 * 2**20),
        cost_estimate=cost,
        name=name,
    )(*operands)


def swaps(count, first):
    if count % 2 == 0:
        return [(i, (i + 1 if i % 2 == first else i - 1) % count) for i in range(count)]
    partner = list(range(count))
    for i in range(first, count - 1, 2):
        partner[i], partner[i + 1] = i + 1, i
    return list(enumerate(partner))


def shards(state, inverse, coupling, wall):
    planes, nv, rows, columns = state.shape
    chunks, halves = CHUNKS, HALO_CHUNKS
    parts = chunks // halves
    width = columns // chunks
    per = width // LANES
    counts = count, count_j, count_k = [lax.axis_size(name) for name in ("ia", "ja", "ka")]
    sets_k = 1 if count_k == 2 else 2

    halo_code = jax.ShapeDtypeStruct(((planes * nv * per * parts + 1) * rows, LANES), jnp.int16)
    face_code = jax.ShapeDtypeStruct(((nv * per + 1) * rows, LANES), jnp.int16)
    full = jax.ShapeDtypeStruct(state.shape, jnp.float32)
    part = jax.ShapeDtypeStruct((planes, nv, rows, width), jnp.float32)
    edge_j = jax.ShapeDtypeStruct((planes, nv, 2, columns), jnp.float32)
    edge_k = jax.ShapeDtypeStruct((planes, nv, rows, LANES), jnp.float32)
    cells = jax.ShapeDtypeStruct((planes, rows, columns), jnp.float32)

    coded = []
    for h in range(halves):
        kernel = functools.partial(encode_kernel, h * parts * width, parts * width)
        coded += call(kernel, [state], [halo_code], "encode")
    near = [lax.ppermute(coded[h], "ia", swaps(count, 0)) for h in range(halves)]
    made = call(
        functools.partial(edges_kernel, sets_k == 2), [state, coded[-1]], [edge_j] * 2 + [edge_k] * sets_k, "edges"
    )
    edges_j, edges_k = made[:2], made[2:]
    edges_k = [lax.ppermute(edge, "ka", swaps(count_k, s)) for s, edge in enumerate(edges_k)]
    edges_j = [lax.ppermute(edge, "ja", swaps(count_j, s)) for s, edge in enumerate(edges_j)]
    size = state.size
    *local, open_cells = call(
        local_kernel,
        [state, wall],
        [part] * chunks + [cells],
        "local",
        None,
        [VMEM((rows + 16, width), jnp.float32)],
        pl.CostEstimate(flops=40 * size, bytes_accessed=10 * size, transcendentals=0),
    )

    def hop_pair(value, source, target):
        first = min(source, target) % 2
        exchange = count % 2 == 0 and (first == 0 or source < target)
        return lax.ppermute(value, "ia", swaps(count, first) if exchange else [(source, target)])

    def pass_on(h, *gate):
        passed = near[h] if count == 4 else coded[h]
        if gate:
            passed = lax.optimization_barrier((passed, *gate))[0]
        return lax.ppermute(passed, "ia", [(i, i ^ 2) for i in range(4)] if count == 4 else swaps(count, 1))

    x, far, face = [], [pass_on(0)], [None] * chunks
    for h in range(halves):
        def kernel(*refs, h=h):
            rest = refs[2 + sets_k : 4 + sets_k]
            xs = refs[4 + sets_k :]
            halo_kernel(h, halves, counts, *refs[:2], refs[2 : 2 + sets_k], *rest, xs[:parts], xs[parts:])

        operands = [*edges_j, *edges_k, near[h], open_cells, *local[h * parts : (h + 1) * parts]]
        first = len(operands) - parts
        x += call(kernel, operands, [part] * parts, "halo", {first + i: i for i in range(parts)})
        for c in range(h * parts, (h + 1) * parts):
            def kernel(inverse_ref, coupling_ref, *refs, c=c):
                forward_kernel(c, parts, 0, count, inverse_ref, coupling_ref, None, None, None, *refs)

            x[c], send = call(kernel, [inverse, coupling, x[c]], [part, face_code], "forward", {2: 0})
            face[c] = hop_pair(send, 0, 1)
        if h:
            far.append(pass_on(h, send))

    for hop in range(1, count):
        for c in range(chunks):
            kernel = functools.partial(forward_kernel, c, parts, hop, count)
            operands = [inverse, coupling, open_cells, far[c // parts], face[c], x[c]]
            x[c], send = call(kernel, operands, [part, face_code], "forward", {5: 0})
            face[c] = hop_pair(send, hop, hop + 1) if hop < count - 1 else hop_pair(send, hop, hop - 1)
    for hop in reversed(range(1, count - 1)):
        for c in range(chunks):
            kernel = functools.partial(backward_kernel, c, hop)
            x[c], send = call(kernel, [inverse, coupling, face[c], x[c]], [part, face_code], "backward", {3: 0})
            face[c] = hop_pair(send, hop, hop - 1)
    for c in range(chunks - 1):
        def kernel(*refs, c=c):
            backward_kernel(c, 0, *refs, None)

        (x[c],) = call(kernel, [inverse, coupling, face[c], x[c]], [part], "backward", {3: 0})
    return call(functools.partial(final_kernel, chunks - 1), [inverse, coupling, face[-1], *x], [full], "last")[0]


def solution(mesh):
    return jax.shard_map(
        shards,
        mesh=mesh,
        in_specs=(
            P("ia", None, "ja", "ka"),
            P("ia", None, None, "ja", "ka"),
            P("ia", None, "ja", "ka"),
            P("ia", "ja", "ka"),
        ),
        out_specs=P("ia", None, "ja", "ka"),
        check_vma=False,
    )
```
